32 devices in a mesh: dp: 8 (over z, y), tensor: 4 (over x, core).
Axes of the slice: x: 2, y: 2, z: 4, core: 2. Of those that a mesh axis runs over, the one named last changes fastest.
Arguments:
- table_cells: bfloat16 [8, 32, 89, 512], P('dp'), may hold values from -6 to 6
- splits: int32 [8], P('dp'), may hold values from 2 to 30, as said below
- feat_qkv: bfloat16 [512, 3, 512], P(None, None, 'tensor'), may hold values from -0.25 to 0.25
- feat_out: bfloat16 [512, 512], P('tensor'), may hold values from -1 to 1
- feat_out_bias: bfloat16 [512], replicated, may hold values from -1.5 to 1.5
- row_qkv: bfloat16 [512, 3, 512], P(None, None, 'tensor'), may hold values from -0.25 to 0.25
- row_out: bfloat16 [512, 512], P('tensor'), may hold values from -1 to 1
- row_out_bias: bfloat16 [512], replicated, may hold values from -1.5 to 1.5
- up_weight: bfloat16 [512, 2048], P(None, 'tensor'), may hold values from -0.25 to 0.25
- up_bias: bfloat16 [2048], P('tensor'), may hold values from -2.5 to 2.5
- down_weight: bfloat16 [2048, 512], P('tensor'), may hold values from -0.125 to 0.125
- down_bias: bfloat16 [512], replicated, may hold values from -1.5 to 1.5
- norm_gains: bfloat16 [3, 512], replicated, may hold values from 0.5 to 1.5
- norm_biases: bfloat16 [3, 512], replicated, may hold values from -1.5 to 1.5
- cotangent: bfloat16 [8, 32, 89, 512], P('dp'), may hold values from -6 to 6
Outputs:
- output: bfloat16 [8, 32, 89, 512], P('dp')
- input_grad: bfloat16 [8, 32, 89, 512], P('dp')
- feat_qkv_grad: float32 [512, 3, 512], P(None, None, 'tensor')
- feat_out_grad: float32 [512, 512], P('tensor')
- feat_out_bias_grad: float32 [512], replicated
- row_qkv_grad: float32 [512, 3, 512], P(None, None, 'tensor')
- row_out_grad: float32 [512, 512], P('tensor')
- row_out_bias_grad: float32 [512], replicated
- up_weight_grad: float32 [512, 2048], P(None, 'tensor')
- up_bias_grad: float32 [2048], P('tensor')
- down_weight_grad: float32 [2048, 512], P('tensor')
- down_bias_grad: float32 [512], replicated
- norm_gains_grad: float32 [3, 512], replicated
- norm_biases_grad: float32 [3, 512], replicated
The draws below stay inside these ranges and needn't reach their ends.
Inputs may be any that keep to these rules, and one draw needn't show every extreme that they name: `splits`: a table's context rows are rows 0 to split - 1; every draw holds a table with the fewest and a table with the most.
All inputs are finite; a program needn't handle non-finite values.
Results may differ from the reference program's by a relative error of at most 0.028.
Values may be sent and summed in bfloat16 or wider, within the bound.
No kernel may reach another device: no remote copies, remote signals or barrier semaphores. Data moves between devices by JAX's collectives and lax.ppermute only.
A program may use at most 192 MiB of HBM per device.

```python
import jax
import jax.numpy as jnp
from jax import lax

D = 512
H = 4
HD = 128
FF = 2048
R = 32
F = 89
TABLES = 8
N_TENSOR = 4


def draw_splits(key, part):
    key = jax.random.fold_in(key, 7)
    lowest = (R + 19) // 20
    highest = R - lowest
    drawn = jax.random.randint(key, (TABLES,), lowest, highest + 1)
    picks = jax.random.permutation(jax.random.fold_in(key, 1), TABLES)
    drawn = drawn.at[picks[0]].set(lowest)
    drawn = drawn.at[picks[1]].set(highest)
    return drawn.astype(jnp.int32)


def block_levels(key, dims, cuts, smallest, largest):
    def one(position, shards_of):
        steps = jax.random.uniform(jax.random.fold_in(jax.random.fold_in(key, 6), position), (shards_of,), jnp.float32, smallest / len(cuts), largest / len(cuts))
        return jnp.repeat(jnp.exp(steps), dims[position] // shards_of).reshape((-1,) + (1,) * (len(dims) - position - 1))

    factor_of = one(*cuts[0])
    for cut in cuts[1:]:
        factor_of = factor_of * one(*cut)
    return factor_of


def gaussian(rng, shape, width, reach, shards=(), held_as=jnp.bfloat16):
    values = jax.random.normal(rng, shape, jnp.float32) * width
    if len(shards) > 0:
        values = block_levels(rng, shape, shards, -0.22, 0.18) * values
    return jnp.clip(values, min=-reach, max=reach).astype(held_as)


def setup_inputs(seed: int = 0) -> dict:
    seeds = jax.random.split(jax.random.key(seed), 16)
    table_cells = gaussian(seeds[0], (TABLES, R, F, D), 1.0, 6.0, ((0, 8),))
    splits = draw_splits(jax.random.fold_in(seeds[15], 71), 0)
    feat_qkv = gaussian(seeds[2], (D, 3, H * HD), D ** -0.5, 0.25, ((2, 4),))
    feat_out = gaussian(seeds[3], (H * HD, D), (D // 16) ** -0.5, 1.0, ((0, 4),))
    feat_out_bias = gaussian(seeds[4], (D,), 0.3, 1.5)
    row_qkv = gaussian(seeds[5], (D, 3, H * HD), D ** -0.5, 0.25, ((2, 4),))
    row_out = gaussian(seeds[6], (H * HD, D), (D // 16) ** -0.5, 1.0, ((0, 4),))
    row_out_bias = gaussian(seeds[7], (D,), 0.3, 1.5)
    up_weight = gaussian(seeds[8], (D, FF), D ** -0.5, 0.25, ((1, 4),))
    up_bias = gaussian(seeds[9], (FF,), 0.5, 2.5, ((0, 4),))
    down_weight = gaussian(seeds[10], (FF, D), FF ** -0.5, 0.125, ((0, 4),))
    down_bias = gaussian(seeds[11], (D,), 0.3, 1.5)
    norm_gains = jnp.clip(1.0 + 0.1 * jax.random.normal(seeds[12], (3, D), jnp.float32), 0.5, 1.5).astype(jnp.bfloat16)
    norm_biases = gaussian(seeds[13], (3, D), 0.3, 1.5)
    cotangent = gaussian(seeds[14], (TABLES, R, F, D), 1.0, 6.0, ((0, 8),))
    return {"table_cells": table_cells, "splits": splits, "feat_qkv": feat_qkv, "feat_out": feat_out, "feat_out_bias": feat_out_bias, "row_qkv": row_qkv, "row_out": row_out, "row_out_bias": row_out_bias, "up_weight": up_weight, "up_bias": up_bias, "down_weight": down_weight, "down_bias": down_bias, "norm_gains": norm_gains, "norm_biases": norm_biases, "cotangent": cotangent}


@jax.custom_vjp
def low(v):
    return lax.optimization_barrier(v.astype(jnp.bfloat16)).astype(jnp.float32)

@jax.custom_vjp
def low_back(v):
    return v

def low_keep(v):
    return (low(v), None)

def low_pass(kept, grad):
    return (grad,)

def back_keep(v):
    return (v, None)

def back_low(kept, grad):
    return (low(grad),)
low.defvjp(low_keep, low_pass)
low_back.defvjp(back_keep, back_low)
EPSILON = 1e-05
NEGATIVE = -1e+30
HIGHEST = lax.Precision.HIGHEST

def layer_norm(values, gain, shift):
    centered = values - lax.optimization_barrier(jnp.mean(values, axis=-1, keepdims=True))
    inverse = lax.rsqrt(lax.optimization_barrier(jnp.mean(centered * centered, axis=-1, keepdims=True)) + EPSILON)
    return centered * inverse * gain + shift

def group_sum(heads, weight):
    lead = heads.shape[:-1]
    grouped = heads.reshape(lead + (N_TENSOR, heads.shape[-1] // N_TENSOR))
    blocks = weight.reshape((N_TENSOR, weight.shape[0] // N_TENSOR, weight.shape[1]))
    partial_out = jnp.einsum('rfgk,gkd->rfgd', grouped, blocks, precision=HIGHEST)
    return lax.optimization_barrier(jnp.sum(low(low_back(partial_out)), axis=2))

def attention(normed, qkv_weight, out_weight, out_bias, score_spec, apply_spec, allowed):
    row_count, feature_count = (normed.shape[0], normed.shape[1])
    packed = low(low_back(jnp.einsum('rfd,dck->rfck', normed, qkv_weight, precision=HIGHEST)))
    packed = packed.reshape(row_count, feature_count, 3, H, HD)
    queries = packed[:, :, 0]
    key_heads = packed[:, :, 1]
    values = packed[:, :, 2]
    scores = jnp.einsum(score_spec, queries, key_heads, precision=HIGHEST) * HD ** (-0.5)
    if allowed is not None:
        scores = jnp.where(allowed, scores, NEGATIVE)
    probabilities = jax.nn.softmax(low_back(scores), axis=-1)
    mixed_heads = low(low_back(jnp.einsum(apply_spec, low(probabilities), values, precision=HIGHEST)))
    return group_sum(mixed_heads.reshape(row_count, feature_count, H * HD), out_weight) + out_bias

def forward(cells, split_row, params):
    feat_qkv, feat_out, feat_out_bias, row_qkv, row_out, row_out_bias, up_weight, up_bias, down_weight, down_bias, norm_gains, norm_biases = params
    first = cells + attention(low(layer_norm(cells, norm_gains[0], norm_biases[0])), feat_qkv, feat_out, feat_out_bias, 'rfhe,rghe->rhfg', 'rhfg,rghe->rfhe', None)
    allowed = (jnp.arange(R) < split_row).reshape(1, 1, 1, R)
    second = first + attention(low(layer_norm(first, norm_gains[1], norm_biases[1])), row_qkv, row_out, row_out_bias, 'rfhe,tfhe->fhrt', 'fhrt,tfhe->rfhe', allowed)
    normed = low(layer_norm(second, norm_gains[2], norm_biases[2]))
    hidden_pre = low_back(jnp.einsum('rfd,dk->rfk', normed, up_weight, precision=HIGHEST) + up_bias)
    hidden = low(jax.nn.gelu(hidden_pre, approximate=False))
    return second + group_sum(hidden, down_weight) + down_bias

def reference(table_cells, splits, feat_qkv, feat_out, feat_out_bias, row_qkv, row_out, row_out_bias, up_weight, up_bias, down_weight, down_bias, norm_gains, norm_biases, cotangent):
    params = tuple((weight.astype(jnp.float32) for weight in (feat_qkv, feat_out, feat_out_bias, row_qkv, row_out, row_out_bias, up_weight, up_bias, down_weight, down_bias, norm_gains, norm_biases)))

    def table_step(totals, table_item):
        cells, upstream, split_row = table_item

        def inner(cells_in, params_in):
            return forward(cells_in, split_row, params_in)
        result, pullback = jax.vjp(inner, cells, params)
        cell_grad, param_grads = pullback(upstream)
        totals = jax.tree.map(jnp.add, totals, param_grads)
        return (totals, (result.astype(jnp.bfloat16), cell_grad.astype(jnp.bfloat16)))
    zero_grads = jax.tree.map(jnp.zeros_like, params)
    totals, outputs = lax.scan(table_step, zero_grads, (table_cells.astype(jnp.float32), cotangent.astype(jnp.float32), splits))
    return (outputs[0], outputs[1], totals[0], totals[1], totals[2], totals[3], totals[4], totals[5], totals[6], totals[7], totals[8], totals[9], totals[10], totals[11])
```

```python
from functools import partial

import jax
import jax.numpy as jnp
from jax import lax
from jax.experimental import pallas as pl
from jax.experimental.pallas import tpu as pltpu
from jax.sharding import PartitionSpec as P

HD = 128
EPSILON = 1e-05
NEGATIVE = -1e30
SCALE = HD**-0.5
BF = jnp.bfloat16
F32 = jnp.float32
SUB = 8
MIB = 1 << 20


def mm(a, b):
    return jnp.dot(a, b, preferred_element_type=F32)


def mm_nt(a, b):
    return lax.dot_general(a, b, (((1,), (1,)), ((), ())), preferred_element_type=F32)


def mm_tn(a, b):
    return lax.dot_general(a, b, (((0,), (0,)), ((), ())), preferred_element_type=F32)


def standardize(values):
    centered = values - jnp.mean(values, axis=-1, keepdims=True)
    inverse = lax.rsqrt(jnp.mean(centered * centered, axis=-1, keepdims=True) + EPSILON)
    return centered * inverse, inverse


def norm_backward(upstream, normed, inverse, gain):
    scaled = upstream * gain
    return inverse * (
        scaled
        - jnp.mean(scaled, axis=-1, keepdims=True)
        - normed * jnp.mean(scaled * normed, axis=-1, keepdims=True)
    )


def column_sum(values):
    return jnp.sum(values, axis=0, keepdims=True)


def softmax_rows(scores):
    top = jnp.max(scores, axis=-1, keepdims=True)
    grown = jnp.exp(scores - top)
    return grown * (1.0 / jnp.sum(grown, axis=-1, keepdims=True))


def gelu_parts(z):
    t = 1.0 / (1.0 + (0.3275911 * 0.7071067811865476) * jnp.abs(z))
    e = jnp.exp(-0.5 * z * z)
    poly = t * (
        0.127414796 + t * (-0.142248368 + t * (0.7107068705 + t * (-0.7265760135 + t * 0.5307027145)))
    )
    tail = poly * e
    cdf = jnp.where(z >= 0, 1.0 - tail, tail)
    return z * cdf, cdf + z * (e * 0.3989422804014327)


def feature_probabilities(q, k, feature_count):
    scores = mm_nt(q, k) * SCALE
    column = lax.broadcasted_iota(jnp.int32, scores.shape, 1)
    return softmax_rows(jnp.where(column < feature_count, scores, NEGATIVE))


def feature_forward_kernel(
    t_ref, cells_ref, gains_ref, shifts_ref, w_ref, o0, o1, o2, o3, cell_scr, mix_scr
):
    rows, feature_count, width = cells_ref.shape
    padded = cell_scr.shape[1]

    @pl.when(pl.program_id(0) == 0)
    def _():
        cell_scr[...] = jnp.zeros_like(cell_scr)

    cell_scr[:, 0:feature_count, :] = cells_ref[...].astype(F32)
    normed, _ = standardize(cell_scr[...].reshape(rows * padded, width))
    low = (normed * gains_ref[...].astype(F32)[0:1] + shifts_ref[...].astype(F32)[0:1]).astype(BF)
    qkv = mm(low, w_ref[...]).astype(BF)
    for r in range(rows):
        part = qkv[r * padded : (r + 1) * padded]
        p = feature_probabilities(part[:, :HD], part[:, HD : 2 * HD], feature_count)
        mixed = mm(p.astype(BF), part[:, 2 * HD :])
        mix_scr[r] = mixed.reshape(padded // SUB, SUB, HD)
    groups = o0.shape[0]
    for k, out in enumerate((o0, o1, o2, o3)):
        dest = lax.bitwise_xor(t_ref[0], k)
        piece = mix_scr[:, pl.ds(dest * groups, groups)]
        piece = jnp.transpose(piece, (1, 0, 2, 3))
        out[...] = piece.reshape(groups, rows * SUB, HD).astype(BF)


def feature_forward(t, cells, gains, shifts, weight, start, count, step):
    _, feature_count, width = cells.shape
    groups = -(-feature_count // (4 * SUB))
    padded = 4 * groups * SUB
    first = start // step
    out = jax.ShapeDtypeStruct((groups, count * SUB, HD), BF)
    whole = lambda i: (0, 0)
    return pl.pallas_call(
        feature_forward_kernel,
        grid=(count // step,),
        out_shape=[out] * 4,
        in_specs=[
            pl.BlockSpec(memory_space=pltpu.SMEM),
            pl.BlockSpec((step, feature_count, width), lambda i: (i + first, 0, 0)),
            pl.BlockSpec(gains.shape, whole),
            pl.BlockSpec(shifts.shape, whole),
            pl.BlockSpec(weight.shape, whole),
        ],
        out_specs=[pl.BlockSpec((groups, step * SUB, HD), lambda i: (0, i, 0))] * 4,
        scratch_shapes=[
            pltpu.VMEM((step, padded, width), F32),
            pltpu.VMEM((step, padded // SUB, SUB, HD), F32),
        ],
        compiler_params=pltpu.CompilerParams(vmem_limit_bytes=40 * MIB),
        cost_estimate=pl.CostEstimate(
            flops=2 * count * padded * (width * 3 * HD + 2 * padded * HD),
            bytes_accessed=4 * MIB,
            transcendentals=0,
        ),
        name="feature_forward",
    )(t, cells, gains, shifts, weight)


def columns_kernel(t_ref, cells_ref, grad_ref, cells_out, grad_out, scr):
    rows, feature_count, width = cells_ref.shape
    groups = cells_out.shape[0]

    @pl.when(pl.program_id(0) == 0)
    def _():
        scr[...] = jnp.zeros_like(scr)

    for source, out in ((cells_ref, cells_out), (grad_ref, grad_out)):
        scr[:, 0:feature_count, :] = source[...].astype(F32)
        for g in range(groups):
            at = pl.multiple_of((t_ref[0] * groups + g) * SUB, SUB)
            piece = scr[:, pl.ds(at, SUB), :]
            out[g] = piece.reshape(rows * SUB, width).astype(BF)


def feature_columns(t, cells, grads, step):
    row_count, feature_count, width = cells.shape
    groups = -(-feature_count // (4 * SUB))
    out = jax.ShapeDtypeStruct((groups, row_count * SUB, width), BF)
    block = pl.BlockSpec((step, feature_count, width), lambda i: (i, 0, 0))
    return pl.pallas_call(
        columns_kernel,
        grid=(row_count // step,),
        out_shape=[out] * 2,
        in_specs=[pl.BlockSpec(memory_space=pltpu.SMEM), block, block],
        out_specs=[pl.BlockSpec((groups, step * SUB, width), lambda i: (0, i, 0))] * 2,
        scratch_shapes=[pltpu.VMEM((step, 4 * groups * SUB, width), F32)],
        compiler_params=pltpu.CompilerParams(vmem_limit_bytes=24 * MIB),
        cost_estimate=pl.CostEstimate(flops=MIB, bytes_accessed=8 * MIB, transcendentals=0),
        name="feature_columns",
    )(t, cells, grads)


def row_forward_kernel(
    split_ref, m0, m1, m2, m3, cells_ref, wo_ref, wo_bias, gains_ref, shifts_ref, wq0, wq1, wq2, wq3,
    wr_ref, wr_bias, first_ref, n2_ref, qkv_ref, p_ref, o2_ref, second_ref, n3_ref, bias_scr,
):
    cells = cells_ref.shape[1]

    @pl.when(pl.program_id(0) == 0)
    def _():
        query = lax.broadcasted_iota(jnp.int32, (cells, cells), 0)
        key = lax.broadcasted_iota(jnp.int32, (cells, cells), 1)
        same = lax.bitwise_and(query, SUB - 1) == lax.bitwise_and(key, SUB - 1)
        live = jnp.logical_and(same, key < split_ref[0] * SUB)
        bias_scr[...] = jnp.where(live, 0.0, NEGATIVE)

    gains = gains_ref[...].astype(F32)
    shifts = shifts_ref[...].astype(F32)
    mixed = jnp.concatenate([m[0] for m in (m0, m1, m2, m3)], axis=-1)
    first = cells_ref[0].astype(F32) + mm(mixed, wo_ref[...]) + wo_bias[...].astype(F32)
    first_ref[0] = first
    normed, _ = standardize(first)
    low = (normed * gains[1:2] + shifts[1:2]).astype(BF)
    n2_ref[0] = low
    outs = []
    for h, wq in enumerate((wq0, wq1, wq2, wq3)):
        qkv = mm(low, wq[...]).astype(BF)
        qkv_ref[0, :, 3 * HD * h : 3 * HD * (h + 1)] = qkv
        scores = mm_nt(qkv[:, :HD], qkv[:, HD : 2 * HD]) * SCALE + bias_scr[...]
        p = softmax_rows(scores).astype(BF)
        p_ref[0, h] = p
        outs.append(mm(p, qkv[:, 2 * HD :]).astype(BF))
    mixed = jnp.concatenate(outs, axis=-1)
    o2_ref[0] = mixed
    second = first + mm(mixed, wr_ref[...]) + wr_bias[...].astype(F32)
    second_ref[0] = second
    normed, _ = standardize(second)
    n3_ref[0] = (normed * gains[2:3] + shifts[2:3]).astype(BF)


def row_forward(split, mixed, cells, wo, wo_bias, gains, shifts, wqs, wr, wr_bias):
    groups, n, width = cells.shape
    per_group = lambda i: (i, 0, 0)
    block = lambda w: pl.BlockSpec((1, n, w), per_group)
    full = lambda a: pl.BlockSpec(a.shape, lambda i: (0,) * a.ndim)
    shape = lambda w, dt: jax.ShapeDtypeStruct((groups, n, w), dt)
    wide = 12 * HD
    return pl.pallas_call(
        row_forward_kernel,
        grid=(groups,),
        out_shape=[
            shape(width, F32), shape(width, BF), shape(wide, BF),
            jax.ShapeDtypeStruct((groups, 4, n, n), BF), shape(4 * HD, BF), shape(width, F32), shape(width, BF),
        ],
        in_specs=[pl.BlockSpec(memory_space=pltpu.SMEM)]
        + [block(HD)] * 4
        + [block(width), full(wo), full(wo_bias), full(gains), full(shifts)]
        + [full(w) for w in wqs]
        + [full(wr), full(wr_bias)],
        out_specs=[
            block(width), block(width), block(wide),
            pl.BlockSpec((1, 4, n, n), lambda i: (i, 0, 0, 0)), block(4 * HD), block(width), block(width),
        ],
        scratch_shapes=[pltpu.VMEM((n, n), F32)],
        compiler_params=pltpu.CompilerParams(vmem_limit_bytes=48 * MIB),
        cost_estimate=pl.CostEstimate(
            flops=2 * groups * n * (width * wide + 2 * width * 4 * HD + 8 * n * HD),
            bytes_accessed=16 * MIB, transcendentals=0,
        ),
        name="row_forward",
    )(split, *mixed, cells, wo, wo_bias, gains, shifts, *wqs, wr, wr_bias)


def hidden_part(n3, n3_t, gl, gl_t, up, bias, down, i, last, up_acc, down_acc, bias_acc, grad_ref):
    z = mm(n3, up) + bias
    act, slope = gelu_parts(z)
    m = act.astype(BF)
    out = mm(m, down)
    dz = (mm_nt(gl, down) * slope).astype(BF)
    dn3 = mm_nt(dz, up)
    width = up.shape[1]

    up_grad = mm(n3_t, dz)
    down_grad = mm(gl_t, m)
    bias_grad = column_sum(dz.astype(F32))

    @pl.when(i == 0)
    def _():
        up_acc[...] = up_grad
        down_acc[...] = down_grad
        bias_acc[...] = bias_grad

    @pl.when(i > 0)
    def _():
        up_acc[...] += up_grad
        down_acc[...] += down_grad
        bias_acc[...] += bias_grad

    @pl.when(i == last)
    def _():
        grad_ref[:, :width] = up_acc[...].astype(BF)
        grad_ref[:, width:] = down_acc[...].astype(BF)

    return out, dn3


def hidden_first_kernel(
    n3_ref, gl_ref, up0, up1, bias0, bias1, down0, down1, out_ref, dn3_ref, grad0, grad1, bg0, bg1,
    ua0, ua1, da0, da1,
):
    i, last = pl.program_id(0), pl.num_programs(0) - 1
    n3, gl = n3_ref[0], gl_ref[0]
    n3_t, gl_t = n3.T, gl.T
    a, da = hidden_part(
        n3, n3_t, gl, gl_t, up0[...], bias0[...].astype(F32), down0[...], i, last, ua0, da0, bg0, grad0)
    b, db = hidden_part(
        n3, n3_t, gl, gl_t, up1[...], bias1[...].astype(F32), down1[...], i, last, ua1, da1, bg1, grad1)
    out_ref[0] = a + b
    dn3_ref[0] = da + db


def hidden_second_kernel(
    n3_ref, gl_ref, up0, up1, bias0, bias1, down0, down1, out_in, dn3_in, second_ref, down_bias, gains_ref,
    out_ref, g2_ref, gl2_ref, grad0, grad1, bg0, bg1, stats_ref, ua0, ua1, da0, da1,
):
    i, last = pl.program_id(0), pl.num_programs(0) - 1
    n3, gl = n3_ref[0], gl_ref[0]
    n3_t, gl_t = n3.T, gl.T
    a, da = hidden_part(
        n3, n3_t, gl, gl_t, up0[...], bias0[...].astype(F32), down0[...], i, last, ua0, da0, bg0, grad0)
    b, db = hidden_part(
        n3, n3_t, gl, gl_t, up1[...], bias1[...].astype(F32), down1[...], i, last, ua1, da1, bg1, grad1)
    second = second_ref[0]
    out_ref[0] = (second + out_in[0] + a + b + down_bias[...].astype(F32)).astype(BF)
    dn3 = dn3_in[0] + da + db
    normed, inverse = standardize(second)
    g3 = gl.astype(F32)
    g2 = g3 + norm_backward(dn3, normed, inverse, gains_ref[...].astype(F32)[2:3])
    g2_ref[0] = g2
    gl2_ref[0] = g2.astype(BF)
    stats = jnp.concatenate(
        [column_sum(g3), column_sum(g2), column_sum(dn3 * normed), column_sum(dn3),
         jnp.zeros((4, g3.shape[1]), F32)], axis=0)

    @pl.when(i == 0)
    def _():
        stats_ref[...] = stats

    @pl.when(i > 0)
    def _():
        stats_ref[...] += stats


def hidden_call(n3, gl, ups, biases, downs, extra=None):
    groups, n, width = n3.shape
    hidden = ups[0].shape[1]
    block = lambda w: pl.BlockSpec((1, n, w), lambda i: (i, 0, 0))
    full = lambda a: pl.BlockSpec(a.shape, lambda i: (0,) * len(a.shape))
    cells = lambda dt: jax.ShapeDtypeStruct((groups, n, width), dt)
    grad = jax.ShapeDtypeStruct((width, hidden + width), BF)
    bias_grad = jax.ShapeDtypeStruct((1, hidden), F32)
    args = [n3, gl, *ups, *biases, *downs]
    specs = [block(width), block(width)] + [full(a) for a in args[2:]]
    if extra is None:
        kernel = hidden_first_kernel
        outs = [cells(F32), cells(F32), grad, grad, bias_grad, bias_grad]
        out_specs = [block(width)] * 2 + [full(o) for o in outs[2:]]
    else:
        kernel = hidden_second_kernel
        args += extra
        specs += [block(width)] * 3 + [full(a) for a in extra[3:]]
        outs = [cells(BF), cells(F32), cells(BF), grad, grad, bias_grad, bias_grad,
                jax.ShapeDtypeStruct((8, width), F32)]
        out_specs = [block(width)] * 3 + [full(o) for o in outs[3:]]
    return pl.pallas_call(
        kernel,
        grid=(groups,),
        out_shape=outs,
        in_specs=specs,
        out_specs=out_specs,
        scratch_shapes=[pltpu.VMEM((width, hidden), F32)] * 2 + [pltpu.VMEM((width, width), F32)] * 2,
        compiler_params=pltpu.CompilerParams(vmem_limit_bytes=48 * MIB),
        cost_estimate=pl.CostEstimate(
            flops=2 * groups * n * width * hidden * 12, bytes_accessed=16 * MIB, transcendentals=0),
        name="hidden_first" if extra is None else "hidden_second",
    )(*args)


def attention_backward(q, k, v, p, do):
    dp = mm_nt(do, v)
    pf = p.astype(F32)
    ds = (pf * (dp - jnp.sum(dp * pf, axis=-1, keepdims=True))).astype(BF)
    dq = mm(ds, k) * SCALE
    dk = mm_tn(ds, q) * SCALE
    dv = mm_tn(p, do)
    return jnp.concatenate([dq, dk, dv], axis=-1).astype(BF)


def row_backward_kernel(
    t_ref, g2_ref, first_ref, qkv_ref, p_ref, gains_ref, wq0, wq1, wq2, wq3, wr_ref,
    dqkv_ref, gl1_ref, s0, s1, s2, s3, stats_ref, g1_scr,
):
    i = pl.program_id(0)
    g2 = g2_ref[0]
    do = mm_nt(g2.astype(BF), wr_ref[...]).astype(BF)
    dn2 = None
    for h, wq in enumerate((wq0, wq1, wq2, wq3)):
        at = 3 * HD * h
        grads = attention_backward(
            qkv_ref[0, :, at : at + HD], qkv_ref[0, :, at + HD : at + 2 * HD],
            qkv_ref[0, :, at + 2 * HD : at + 3 * HD], p_ref[0, h], do[:, HD * h : HD * (h + 1)])
        dqkv_ref[0, :, at : at + 3 * HD] = grads
        term = mm_nt(grads, wq[...])
        dn2 = term if dn2 is None else dn2 + term
    normed, inverse = standardize(first_ref[0])
    g1 = g2 + norm_backward(dn2, normed, inverse, gains_ref[...].astype(F32)[1:2])
    g1_scr[...] = g1
    gl1_ref[0] = g1.astype(BF)
    rows = s0.shape[1]
    for k, out in enumerate((s0, s1, s2, s3)):
        at = pl.multiple_of(lax.bitwise_xor(t_ref[0], k) * rows, rows)
        out[0] = g1_scr[pl.ds(at, rows), :].astype(BF)
    stats = jnp.concatenate(
        [column_sum(g1), column_sum(dn2 * normed), column_sum(dn2), jnp.zeros((5, g1.shape[1]), F32)], axis=0)

    @pl.when(i == 0)
    def _():
        stats_ref[...] = stats

    @pl.when(i > 0)
    def _():
        stats_ref[...] += stats


def row_backward(t, g2, first, qkv, p, gains, wqs, wr):
    groups, n, width = g2.shape
    block = lambda w, m=n: pl.BlockSpec((1, m, w), lambda i: (i, 0, 0))
    full = lambda a: pl.BlockSpec(a.shape, lambda i: (0,) * len(a.shape))
    wide = qkv.shape[2]
    send = jax.ShapeDtypeStruct((groups, n // 4, width), BF)
    return pl.pallas_call(
        row_backward_kernel,
        grid=(groups,),
        out_shape=[
            jax.ShapeDtypeStruct((groups, n, wide), BF), jax.ShapeDtypeStruct((groups, n, width), BF),
            send, send, send, send, jax.ShapeDtypeStruct((8, width), F32),
        ],
        in_specs=[pl.BlockSpec(memory_space=pltpu.SMEM), block(width), block(width), block(wide),
                  pl.BlockSpec((1, 4, n, n), lambda i: (i, 0, 0, 0)), full(gains)]
        + [full(w) for w in wqs] + [full(wr)],
        out_specs=[block(wide), block(width)] + [block(width, n // 4)] * 4
        + [pl.BlockSpec((8, width), lambda i: (0, 0))],
        scratch_shapes=[pltpu.VMEM((n, width), F32)],
        compiler_params=pltpu.CompilerParams(vmem_limit_bytes=48 * MIB),
        cost_estimate=pl.CostEstimate(
            flops=2 * groups * n * (width * wide + width * 4 * HD + 16 * n * HD),
            bytes_accessed=16 * MIB, transcendentals=0),
        name="row_backward",
    )(t, g2, first, qkv, p, gains, *wqs, wr)


def row_weights_kernel(n2_ref, dqkv_ref, gl2_ref, o2_ref, gl1_ref, m0, m1, m2, m3, keep_ref, send_ref):
    groups, n, width = n2_ref.shape
    cells = groups * n
    n2_t = n2_ref[...].reshape(cells, width).T
    gl2_t = gl2_ref[...].reshape(cells, width).T
    gl1_t = gl1_ref[...].reshape(cells, width).T
    for h, m in enumerate((m0, m1, m2, m3)):
        out = (keep_ref, send_ref)[h % 2]
        at = 3 * HD * h
        out[h // 2, :, 0 : 3 * HD] = mm(
            n2_t, dqkv_ref[:, :, at : at + 3 * HD].reshape(cells, 3 * HD)).astype(BF)
        out[h // 2, :, 3 * HD : 4 * HD] = mm(
            gl2_t, o2_ref[:, :, HD * h : HD * (h + 1)].reshape(cells, HD)).astype(BF)
        out[h // 2, :, 4 * HD : 5 * HD] = mm(gl1_t, m[...].reshape(cells, HD)).astype(BF)


def row_weights(n2, dqkv, gl2, o2, gl1, mixed):
    groups, n, width = n2.shape
    out = jax.ShapeDtypeStruct((2, width, 5 * HD), BF)
    vmem = pl.BlockSpec(memory_space=pltpu.VMEM)
    return pl.pallas_call(
        row_weights_kernel,
        out_shape=[out] * 2,
        in_specs=[vmem] * 9,
        out_specs=[vmem] * 2,
        compiler_params=pltpu.CompilerParams(vmem_limit_bytes=48 * MIB),
        cost_estimate=pl.CostEstimate(
            flops=2 * groups * n * width * 20 * HD, bytes_accessed=10 * MIB, transcendentals=0),
        name="row_weights",
    )(n2, dqkv, gl2, o2, gl1, *mixed)


def feature_again_kernel(
    t_ref, cells_ref, gains_ref, shifts_ref, wq0, wq1, wq2, wq3, n1_ref, qkv_ref, p_ref, cell_scr
):
    rows, feature_count, width = cells_ref.shape
    padded = cell_scr.shape[1]

    @pl.when(pl.program_id(0) == 0)
    def _():
        cell_scr[...] = jnp.zeros_like(cell_scr)

    cell_scr[:, 0:feature_count, :] = cells_ref[...].astype(F32)
    normed, _ = standardize(cell_scr[...].reshape(rows * padded, width))
    low = (normed * gains_ref[...].astype(F32)[0:1] + shifts_ref[...].astype(F32)[0:1]).astype(BF)
    n1_ref[...] = low
    for h, wq in enumerate((wq0, wq1, wq2, wq3)):
        qkv = mm(low, wq[...]).astype(BF)
        qkv_ref[:, 3 * HD * h : 3 * HD * (h + 1)] = qkv
        for r in range(rows):
            part = qkv[r * padded : (r + 1) * padded]
            p = feature_probabilities(part[:, :HD], part[:, HD : 2 * HD], feature_count)
            p_ref[r, h] = p.astype(BF)


def feature_again(t, cells, gains, shifts, wqs, own, step):
    _, feature_count, width = cells.shape
    groups = -(-feature_count // (4 * SUB))
    padded = 4 * groups * SUB
    steps = own // step
    grid_spec = pltpu.PrefetchScalarGridSpec(
        num_scalar_prefetch=1,
        grid=(steps,),
        in_specs=[
            pl.BlockSpec((step, feature_count, width), lambda i, t: (t[0] * steps + i, 0, 0)),
            pl.BlockSpec(gains.shape, lambda i, t: (0, 0)),
            pl.BlockSpec(shifts.shape, lambda i, t: (0, 0)),
        ]
        + [pl.BlockSpec(w.shape, lambda i, t: (0, 0)) for w in wqs],
        out_specs=[
            pl.BlockSpec((step * padded, width), lambda i, t: (i, 0)),
            pl.BlockSpec((step * padded, 12 * HD), lambda i, t: (i, 0)),
            pl.BlockSpec((step, 4, padded, padded), lambda i, t: (i, 0, 0, 0)),
        ],
        scratch_shapes=[pltpu.VMEM((step, padded, width), F32)],
    )
    return pl.pallas_call(
        feature_again_kernel,
        grid_spec=grid_spec,
        out_shape=[
            jax.ShapeDtypeStruct((own * padded, width), BF),
            jax.ShapeDtypeStruct((own * padded, 12 * HD), BF),
            jax.ShapeDtypeStruct((own, 4, padded, padded), BF),
        ],
        compiler_params=pltpu.CompilerParams(vmem_limit_bytes=40 * MIB),
        cost_estimate=pl.CostEstimate(
            flops=2 * own * padded * (width * 12 * HD + 4 * padded * HD), bytes_accessed=8 * MIB, transcendentals=0),
        name="feature_again",
    )(t, cells, gains, shifts, *wqs)


def feature_backward_kernel(t_ref, r0, r1, r2, r3, wo_ref, qkv_ref, p_ref, dqkv_ref, g1_ref):
    rows, padded, width = g1_ref.shape
    groups = r0.shape[0]
    for k, piece in enumerate((r0, r1, r2, r3)):
        for g in range(groups):
            at = pl.multiple_of((lax.bitwise_xor(t_ref[0], k) * groups + g) * SUB, SUB)
            g1_ref[:, pl.ds(at, SUB), :] = piece[g].astype(F32).reshape(rows, SUB, width)
    gl = g1_ref[...].reshape(rows * padded, width).astype(BF)
    do = mm_nt(gl, wo_ref[...]).astype(BF)
    for r in range(rows):
        span = slice(r * padded, (r + 1) * padded)
        for h in range(4):
            at = 3 * HD * h
            dqkv_ref[span, at : at + 3 * HD] = attention_backward(
                qkv_ref[span, at : at + HD], qkv_ref[span, at + HD : at + 2 * HD],
                qkv_ref[span, at + 2 * HD : at + 3 * HD], p_ref[r, h], do[span, HD * h : HD * (h + 1)])


def feature_backward(t, pieces, wo, qkv, p, step):
    own, _, padded, _ = p.shape
    groups, _, width = pieces[0].shape
    wide = qkv.shape[1]
    return pl.pallas_call(
        feature_backward_kernel,
        grid=(own // step,),
        out_shape=[
            jax.ShapeDtypeStruct((own * padded, wide), BF),
            jax.ShapeDtypeStruct((own, padded, width), F32),
        ],
        in_specs=[pl.BlockSpec(memory_space=pltpu.SMEM)]
        + [pl.BlockSpec((groups, step * SUB, width), lambda i: (0, i, 0))] * 4
        + [
            pl.BlockSpec(wo.shape, lambda i: (0, 0)),
            pl.BlockSpec((step * padded, wide), lambda i: (i, 0)),
            pl.BlockSpec((step, 4, padded, padded), lambda i: (i, 0, 0, 0)),
        ],
        out_specs=[
            pl.BlockSpec((step * padded, wide), lambda i: (i, 0)),
            pl.BlockSpec((step, padded, width), lambda i: (i, 0, 0)),
        ],
        compiler_params=pltpu.CompilerParams(vmem_limit_bytes=40 * MIB),
        cost_estimate=pl.CostEstimate(
            flops=2 * own * padded * (width * 4 * HD + 20 * padded * HD), bytes_accessed=9 * MIB, transcendentals=0),
        name="feature_backward",
    )(t, *pieces, wo, qkv, p)


def feature_weights_kernel(n1_ref, dqkv_ref, keep_ref, send_ref):
    n1_t = n1_ref[...].T
    for h in range(4):
        out = (keep_ref, send_ref)[h % 2]
        out[h // 2] = mm(n1_t, dqkv_ref[:, 3 * HD * h : 3 * HD * (h + 1)]).astype(BF)


def feature_weights(n1, dqkv):
    cells, width = n1.shape
    out = jax.ShapeDtypeStruct((2, width, 3 * HD), BF)
    vmem = pl.BlockSpec(memory_space=pltpu.VMEM)
    return pl.pallas_call(
        feature_weights_kernel,
        out_shape=[out] * 2,
        in_specs=[vmem] * 2,
        out_specs=[vmem] * 2,
        compiler_params=pltpu.CompilerParams(vmem_limit_bytes=40 * MIB),
        cost_estimate=pl.CostEstimate(
            flops=2 * cells * width * 12 * HD, bytes_accessed=5 * MIB, transcendentals=0),
        name="feature_weights",
    )(n1, dqkv)


def feature_input_kernel(t_ref, cells_ref, g1_ref, dqkv_ref, gains_ref, wq0, wq1, wq2, wq3, out_ref, stats_ref, scr):
    i = pl.program_id(0)
    rows, feature_count, width = cells_ref.shape
    padded = scr.shape[1]

    @pl.when(i == 0)
    def _():
        scr[...] = jnp.zeros_like(scr)

    scr[:, 0:feature_count, :] = cells_ref[...].astype(F32)
    normed, inverse = standardize(scr[...].reshape(rows * padded, width))
    dn1 = None
    for h, wq in enumerate((wq0, wq1, wq2, wq3)):
        term = mm_nt(dqkv_ref[:, 3 * HD * h : 3 * HD * (h + 1)], wq[...])
        dn1 = term if dn1 is None else dn1 + term
    g1 = g1_ref[...].reshape(rows * padded, width)
    g0 = g1 + norm_backward(dn1, normed, inverse, gains_ref[...].astype(F32)[0:1])
    g0 = g0.reshape(rows, padded, width)
    out_ref[...] = g0[:, 0:feature_count, :].astype(BF)
    stats = jnp.concatenate(
        [column_sum(dn1 * normed), column_sum(dn1), jnp.zeros((6, width), F32)], axis=0)

    @pl.when(i == 0)
    def _():
        stats_ref[...] = stats

    @pl.when(i > 0)
    def _():
        stats_ref[...] += stats


def feature_input(t, cells, g1, dqkv, gains, wqs, step):
    own, padded, width = g1.shape
    feature_count = cells.shape[1]
    steps = own // step
    grid_spec = pltpu.PrefetchScalarGridSpec(
        num_scalar_prefetch=1,
        grid=(steps,),
        in_specs=[
            pl.BlockSpec((step, feature_count, width), lambda i, t: (t[0] * steps + i, 0, 0)),
            pl.BlockSpec((step, padded, width), lambda i, t: (i, 0, 0)),
            pl.BlockSpec((step * padded, dqkv.shape[1]), lambda i, t: (i, 0)),
            pl.BlockSpec(gains.shape, lambda i, t: (0, 0)),
        ]
        + [pl.BlockSpec(w.shape, lambda i, t: (0, 0)) for w in wqs],
        out_specs=[
            pl.BlockSpec((step, feature_count, width), lambda i, t: (i, 0, 0)),
            pl.BlockSpec((8, width), lambda i, t: (0, 0)),
        ],
        scratch_shapes=[pltpu.VMEM((step, padded, width), F32)],
    )
    return pl.pallas_call(
        feature_input_kernel,
        grid_spec=grid_spec,
        out_shape=[
            jax.ShapeDtypeStruct((own, feature_count, width), BF),
            jax.ShapeDtypeStruct((8, width), F32),
        ],
        compiler_params=pltpu.CompilerParams(vmem_limit_bytes=40 * MIB),
        cost_estimate=pl.CostEstimate(
            flops=2 * own * padded * width * 12 * HD, bytes_accessed=8 * MIB, transcendentals=0),
        name="feature_input",
    )(t, cells, g1, dqkv, gains, *wqs)


def rows_kernel(t_ref, p0, p1, p2, p3, out_ref, scr):
    rows, feature_count, width = out_ref.shape
    groups = p0.shape[0]
    for k, piece in enumerate((p0, p1, p2, p3)):
        for g in range(groups):
            at = pl.multiple_of((lax.bitwise_xor(t_ref[0], k) * groups + g) * SUB, SUB)
            scr[:, pl.ds(at, SUB), :] = piece[g].astype(F32).reshape(rows, SUB, width)
    out_ref[...] = scr[:, 0:feature_count, :].astype(BF)


def from_columns(t, pieces, row_count, feature_count, step):
    groups, _, width = pieces[0].shape
    return pl.pallas_call(
        rows_kernel,
        grid=(row_count // step,),
        out_shape=jax.ShapeDtypeStruct((row_count, feature_count, width), BF),
        in_specs=[pl.BlockSpec(memory_space=pltpu.SMEM)]
        + [pl.BlockSpec((groups, step * SUB, width), lambda i: (0, i, 0))] * 4,
        out_specs=pl.BlockSpec((step, feature_count, width), lambda i: (i, 0, 0)),
        scratch_shapes=[pltpu.VMEM((step, 4 * groups * SUB, width), F32)],
        compiler_params=pltpu.CompilerParams(vmem_limit_bytes=24 * MIB),
        cost_estimate=pl.CostEstimate(flops=MIB, bytes_accessed=6 * MIB, transcendentals=0),
        name="from_columns",
    )(t, *pieces)


def swap(values, axis, mask):
    count = lax.axis_size(axis)
    return lax.ppermute(values, axis, [(i, i ^ mask) for i in range(count)])


def gather_groups(own):
    far = swap(own, "tensor", 2)
    return own, swap(own, "tensor", 1), far, swap(far, "tensor", 1)


def dp_radices(count):
    radices = [2]
    rest = count // 2
    while rest > 1:
        step = 4 if rest % 4 == 0 else 2
        radices.append(step)
        rest //= step
    return radices


def digit_of(shift, radix):
    return lax.rem(lax.div(lax.axis_index("dp"), shift), radix)


def scatter_digit(values, shift, radix):
    rows = values.shape[-2] // radix
    mine = digit_of(shift, radix)
    cut = lambda j: lax.dynamic_slice_in_dim(values, lax.bitwise_xor(mine, j) * rows, rows, values.ndim - 2)
    total = cut(0).astype(F32)
    arrived = [swap(cut(j), "dp", j * shift) for j in range(1, radix)]
    for piece in arrived:
        total = total + piece.astype(F32)
    return total.astype(BF)


def gather_digit(values, shift, radix):
    rows = values.shape[-2]
    mine = digit_of(shift, radix)
    out = jnp.zeros(values.shape[:-2] + (rows * radix, values.shape[-1]), values.dtype)
    pieces = [values] + [swap(values, "dp", j * shift) for j in range(1, radix)]
    for j, piece in enumerate(pieces):
        out = lax.dynamic_update_slice_in_dim(out, piece, lax.bitwise_xor(mine, j) * rows, out.ndim - 2)
    return out


def reduce_groups(keep, send, order):
    values = (keep.astype(F32) + swap(send, "tensor", 1).astype(F32)).astype(BF)
    radices = dp_radices(lax.axis_size("dp"))
    shifts = [1]
    for radix in radices[:-1]:
        shifts.append(shifts[-1] * radix)
    done = []
    for stage in order(len(radices)):
        if stage == "x":
            values = (values[0].astype(F32) + swap(values[1], "tensor", 2).astype(F32)).astype(BF)
        else:
            values = scatter_digit(values, shifts[stage], radices[stage])
            done.append(stage)
    for stage in reversed(done):
        values = gather_digit(values, shifts[stage], radices[stage])
    return values.astype(F32)


def y_first(digits):
    return [0, "x"] + list(range(1, digits))


def z_first(digits):
    return list(range(1, digits)) + ["x", 0]


def x_first(digits):
    return ["x"] + list(range(digits))


def sum_everywhere(values):
    for mask in (1, 2):
        values = values + swap(values, "tensor", mask)
    shift = 1
    while shift < lax.axis_size("dp"):
        values = values + swap(values, "dp", shift)
        shift *= 2
    return values


def shards(
    table_cells, splits, feat_qkv, feat_out, feat_out_bias, row_qkv, row_out, row_out_bias,
    up_weight, up_bias, down_weight, down_bias, norm_gains, norm_biases, cotangent,
):
    shape = table_cells.shape
    _, row_count, feature_count, width = shape
    own_rows = row_count // 4
    hidden = up_weight.shape[1]
    t = lax.axis_index("tensor").astype(jnp.int32).reshape(1)
    cells = table_cells.reshape(shape[1:])
    grads = cotangent.reshape(shape[1:])
    fob, rob, dnb = (b.reshape(1, width) for b in (feat_out_bias, row_out_bias, down_bias))
    fq = feat_qkv.reshape(width, 3 * HD)
    rq = row_qkv.reshape(width, 3 * HD)

    outs_own = jnp.concatenate(
        [feat_out, row_out, jnp.broadcast_to(up_bias.reshape(1, hidden), (16, hidden))], axis=0)
    outs = gather_groups(outs_own)
    rqs = gather_groups(rq)
    ups = gather_groups(up_weight)
    downs = gather_groups(down_weight)
    fqs = gather_groups(fq)
    fo = jnp.concatenate([w[:HD] for w in outs], axis=0)
    ro = jnp.concatenate([w[HD : 2 * HD] for w in outs], axis=0)
    ubs = [w[2 * HD : 2 * HD + 1] for w in outs]

    mixed = feature_forward(t, cells, norm_gains, norm_biases, fq, 0, row_count, 8)
    mixed = [mixed[0]] + [swap(mixed[k], "tensor", k) for k in (1, 2, 3)]
    cells_f, grads_f = feature_columns(t, cells, grads, 8)

    first, n2, row_packed, row_p, o2, second, n3 = row_forward(
        splits, mixed, cells_f, fo, fob, norm_gains, norm_biases, rqs, ro, rob)
    out_a, dn3_a, hg0, hg1, bg0, bg1 = hidden_call(n3, grads_f, ups[:2], ubs[:2], downs[:2])
    out_f, g2, gl2, hg2, hg3, bg2, bg3, stats_a = hidden_call(
        n3, grads_f, ups[2:], ubs[2:], downs[2:], [out_a, dn3_a, second, dnb, norm_gains])
    dqkv_r, gl1, s0, s1, s2, s3, stats_b = row_backward(t, g2, first, row_packed, row_p, norm_gains, rqs, ro)
    pieces = [s0] + [swap(s, "tensor", k) for k, s in ((1, s1), (2, s2), (3, s3))]

    n1, feat_packed, feat_p = feature_again(t, cells, norm_gains, norm_biases, fqs, own_rows, 4)
    row_keep, row_send = row_weights(n2, dqkv_r, gl2, o2, gl1, mixed)
    out_pieces = gather_groups(out_f)
    output = from_columns(t, out_pieces, row_count, feature_count, 8).reshape(shape)

    dqkv_f, g1 = feature_backward(t, pieces, fo, feat_packed, feat_p, 4)
    feat_keep, feat_send = feature_weights(n1, dqkv_f)
    g0, stats_c = feature_input(t, cells, g1, dqkv_f, norm_gains, fqs, 4)

    hidden_keep, hidden_send = jnp.stack([hg0, hg2]), jnp.stack([hg1, hg3])
    up_grad = reduce_groups(hidden_keep[:, :, :hidden], hidden_send[:, :, :hidden], y_first)
    down_grad = reduce_groups(hidden_keep[:, :, hidden:], hidden_send[:, :, hidden:], z_first)
    row_grad = reduce_groups(row_keep, row_send, y_first)
    feat_grad = reduce_groups(feat_keep, feat_send, x_first)

    far = bg0 + swap(bg1, "tensor", 1), bg2 + swap(bg3, "tensor", 1)
    up_bias_part = far[0] + swap(far[1], "tensor", 2)
    shift = 1
    while shift < lax.axis_size("dp"):
        up_bias_part = up_bias_part + swap(up_bias_part, "dp", shift)
        shift *= 2

    small = sum_everywhere(jnp.concatenate([stats_a[:4], stats_b[:3], stats_c[:2]], axis=0))

    g0s = gather_groups(g0)
    input_grad = jnp.zeros((row_count, feature_count, width), BF)
    for k, piece in enumerate(g0s):
        input_grad = lax.dynamic_update_slice_in_dim(
            input_grad, piece, lax.bitwise_xor(t[0], k) * own_rows, 0)

    return (
        output,
        input_grad.reshape(shape),
        feat_grad.reshape(width, 3, HD),
        row_grad[:, 4 * HD :].T,
        small[4],
        row_grad[:, : 3 * HD].reshape(width, 3, HD),
        row_grad[:, 3 * HD : 4 * HD].T,
        small[1],
        up_grad,
        up_bias_part.reshape(hidden),
        down_grad.T,
        small[0],
        jnp.stack([small[7], small[5], small[2]]),
        jnp.stack([small[8], small[6], small[3]]),
    )


def solution(mesh):
    return jax.shard_map(
        shards,
        mesh=mesh,
        in_specs=(
            P("dp", None, None, None), P("dp"), P(None, None, "tensor"), P("tensor", None), P(),
            P(None, None, "tensor"), P("tensor", None), P(), P(None, "tensor"), P("tensor"),
            P("tensor", None), P(), P(), P(), P("dp", None, None, None),
        ),
        out_specs=(
            P("dp", None, None, None), P("dp", None, None, None), P(None, None, "tensor"),
            P("tensor", None), P(), P(None, None, "tensor"), P("tensor", None), P(),
            P(None, "tensor"), P("tensor"), P("tensor", None), P(), P(), P(),
        ),
        check_vma=False,
    )
```

```python
from functools import partial

import jax
import jax.numpy as jnp
from jax import lax
from jax.experimental import pallas as pl
from jax.experimental.pallas import tpu as pltpu
from jax.sharding import PartitionSpec as P

HD = 128
EPSILON = 1e-05
NEGATIVE = -1e30
SCALE = HD**-0.5
BF = jnp.bfloat16
F32 = jnp.float32
MIB = 1 << 20
FB = 8
RB = 16


def mm(a, b):
    return jnp.dot(a, b, preferred_element_type=F32)


def mm_nt(a, b):
    return lax.dot_general(a, b, (((1,), (1,)), ((), ())), preferred_element_type=F32)


def mm_tn(a, b):
    return lax.dot_general(a, b, (((0,), (0,)), ((), ())), preferred_element_type=F32)


def standardize(values):
    centered = values - jnp.mean(values, axis=-1, keepdims=True)
    inverse = lax.rsqrt(jnp.mean(centered * centered, axis=-1, keepdims=True) + EPSILON)
    return centered * inverse, inverse


def norm_backward(upstream, normed, inverse, gain):
    scaled = upstream * gain
    return inverse * (
        scaled
        - jnp.mean(scaled, axis=-1, keepdims=True)
        - normed * jnp.mean(scaled * normed, axis=-1, keepdims=True)
    )


def column_sum(values):
    return jnp.sum(values, axis=0, keepdims=True)


def softmax_keys(scores):
    grown = jnp.exp(scores - jnp.max(scores, axis=0, keepdims=True))
    return grown * (1.0 / jnp.sum(grown, axis=0, keepdims=True))


def gelu_parts(z):
    t = 1.0 / (1.0 + (0.3275911 * 0.7071067811865476) * jnp.abs(z))
    e = jnp.exp(-0.5 * z * z)
    poly = t * (
        0.127414796 + t * (-0.142248368 + t * (0.7107068705 + t * (-0.7265760135 + t * 0.5307027145)))
    )
    tail = poly * e
    cdf = jnp.where(z >= 0, 1.0 - tail, tail)
    return z * cdf, cdf + z * (e * 0.3989422804014327)


def feature_probabilities(q, k, feature_count):
    scores = mm_nt(k, q) * SCALE
    key = lax.broadcasted_iota(jnp.int32, scores.shape, 0)
    return softmax_keys(jnp.where(key < feature_count, scores, NEGATIVE)).astype(BF)


def three(w):
    return jnp.concatenate([w[0], w[1], w[2]], axis=-1)


def stacked(w):
    n = w.shape[0] // 3
    return jnp.concatenate([w[c * n : (c + 1) * n] for c in range(3)], axis=-1)


def wide(pieces):
    n = pieces[0].shape[0] // 4
    return jnp.concatenate(
        [jnp.concatenate([p[j * n : (j + 1) * n] for j in range(4)], axis=-1) for p in pieces], axis=0)


def live_columns(block, first, feature_count):
    values = block.astype(F32)
    index = first + lax.broadcasted_iota(jnp.int32, values.shape, 0)
    return jnp.where(index < feature_count, values, 0.0)


ANY = pl.BlockSpec(memory_space=pl.ANY)
VMEM = pl.BlockSpec(memory_space=pltpu.VMEM)


def full(a):
    zeros = (0,) * len(a.shape)
    return pl.BlockSpec(a.shape, lambda *_: zeros)


def shaped(shape, dtype=BF):
    return jax.ShapeDtypeStruct(shape, dtype)


def call(kernel, name, grid, t, ins, outs, scratch=(), vmem=32):
    spec = pltpu.PrefetchScalarGridSpec(
        num_scalar_prefetch=2,
        grid=grid,
        in_specs=[s for _, s in ins],
        out_specs=[s for _, s in outs],
        scratch_shapes=list(scratch),
    )
    return pl.pallas_call(
        kernel,
        grid_spec=spec,
        out_shape=[a for a, _ in outs],
        compiler_params=pltpu.CompilerParams(vmem_limit_bytes=vmem * MIB),
        cost_estimate=pl.CostEstimate(flops=1, bytes_accessed=1, transcendentals=0),
        name=name,
    )(*t, *[a for a, _ in ins])


def pack_kernel(t_ref, d_ref, rq_ref, fo_ref, ro_ref, ub_ref, out_ref):
    width = rq_ref.shape[1]
    for c in range(3):
        out_ref[c * width : (c + 1) * width] = rq_ref[c]
    at = 3 * width
    for source in (fo_ref, ro_ref):
        for j in range(4):
            out_ref[at : at + HD] = source[:, j * HD : (j + 1) * HD]
            at += HD
    bias = jnp.concatenate([ub_ref[...].astype(F32)[:, j * HD : (j + 1) * HD] for j in range(4)], axis=0)
    out_ref[at : at + 16] = jnp.concatenate([bias, jnp.zeros((12, HD), F32)], axis=0).astype(BF)


def pack(t, rq, fo, ro, ub):
    out = shaped((3 * rq.shape[1] + 8 * HD + 16, HD))
    return call(pack_kernel, "pack", (), t, [(a, VMEM) for a in (rq, fo, ro, ub)], [(out, VMEM)], vmem=8)[0]


def pack_part(pack, what):
    rows = pack.shape[0] - 8 * HD - 16
    size, at = {"qkv": (rows, 0), "feat_out": (4 * HD, rows), "row_out": (4 * HD, rows + 4 * HD),
                "bias": (16, rows + 8 * HD)}[what]
    return pl.BlockSpec((size, HD), lambda *_: (at // size, 0))


def pack_parts(packs, what):
    return [(p, pack_part(p, what)) for p in packs]


def feature_forward_kernel(
    t_ref, d_ref, cells_ref, gains_ref, shifts_ref, w_ref, o0, o1, o2, o3, qkv_scr, mix_scr
):
    feature_count, rows, width = cells_ref.shape
    padded = qkv_scr.shape[1] // rows

    @pl.when(pl.program_id(0) == 0)
    def _():
        qkv_scr[...] = jnp.zeros_like(qkv_scr)

    cells = cells_ref[...].astype(F32).reshape(feature_count * rows, width)
    normed, _ = standardize(cells)
    low = (normed * gains_ref[...].astype(F32)[0:1] + shifts_ref[...].astype(F32)[0:1]).astype(BF)
    qkv = mm(low, three(w_ref))
    for c in range(3):
        qkv_scr[c, 0 : feature_count * rows, :] = qkv[:, c * HD : (c + 1) * HD]
    for r in range(rows):
        every = pl.ds(r, padded, stride=rows)
        q, k, v = (qkv_scr[c, every, :].astype(BF) for c in range(3))
        mix_scr[every, :] = mm_tn(feature_probabilities(q, k, feature_count), v)
    count = o0.shape[1]
    for k, out in enumerate((o0, o1, o2, o3)):
        at = pl.multiple_of(lax.bitwise_xor(t_ref[0], k) * count, count)
        out[0] = mix_scr[pl.ds(at, count), :].astype(BF)


def feature_forward(t, cells, gains, shifts, weight, columns):
    feature_count, row_count, width = cells.shape
    padded = 4 * columns
    steps = row_count // RB
    out = (shaped((steps, columns * RB, HD)), pl.BlockSpec((1, columns * RB, HD), lambda i, t, d: (i, 0, 0)))
    return call(
        feature_forward_kernel, "feature_forward", (steps,), t,
        [(cells, pl.BlockSpec((feature_count, RB, width), lambda i, t, d: (0, i, 0)))]
        + [(a, full(a)) for a in (gains, shifts, weight)],
        [out] * 4,
        [pltpu.VMEM((3, padded * RB, HD), F32), pltpu.VMEM((padded * RB, HD), F32)], vmem=28,
    )


def column_block(array, columns):
    _, rows, width = array.shape
    return pl.BlockSpec((columns, rows, width), lambda i, t, d: (t[0], 0, 0))


def in_order(m, columns):
    steps = m.shape[0]
    halves = [m[i].reshape(columns, RB, HD) for i in range(steps)]
    return jnp.concatenate(halves, axis=1).reshape(columns * RB * steps, HD)


def row_forward_kernel(
    t_ref, d_ref, split_ref, m0, m1, m2, m3, cells_ref, f0, f1, f2, f3, r0, r1, r2, r3, w0, w1, w2, w3,
    wo_bias, wr_bias, gains_ref, shifts_ref,
    first_ref, n2_ref, qkv_ref, p_ref, o2_ref, second_ref, n3_ref, *, feature_count,
):
    columns, rows, width = cells_ref.shape
    cells = columns * rows
    side = p_ref.shape[2]
    key = lax.broadcasted_iota(jnp.int32, (side, side), 0)
    query = lax.broadcasted_iota(jnp.int32, (side, side), 1)
    same = lax.div(query, rows) == lax.div(key, rows)
    bias = jnp.where(jnp.logical_and(same, lax.rem(key, rows) < split_ref[0]), 0.0, NEGATIVE)

    gains = gains_ref[...].astype(F32)
    shifts = shifts_ref[...].astype(F32)
    stream = live_columns(cells_ref[...], t_ref[0] * columns, feature_count).reshape(cells, width)
    mixed = jnp.concatenate([in_order(m, columns) for m in (m0, m1, m2, m3)], axis=-1)
    first = stream + mm(mixed, wide((f0, f1, f2, f3))) + wo_bias[...].astype(F32)
    first_ref[...] = first
    normed, _ = standardize(first)
    low = (normed * gains[1:2] + shifts[1:2]).astype(BF)
    n2_ref[...] = low
    for h, w in enumerate((w0, w1, w2, w3)):
        base = 3 * HD * h
        qkv_ref[:, base : base + 3 * HD] = mm(low, stacked(w)).astype(BF)
        for b in range(0, cells, side):
            span = slice(b, b + side)
            q, k, v = (qkv_ref[span, base + c * HD : base + (c + 1) * HD] for c in range(3))
            p = softmax_keys(mm_nt(k, q) * SCALE + bias).astype(BF)
            p_ref[h, b // side] = p
            o2_ref[span, h * HD : (h + 1) * HD] = mm_tn(p, v).astype(BF)
    second = first + mm(o2_ref[...], wide((r0, r1, r2, r3))) + wr_bias[...].astype(F32)
    second_ref[...] = second
    normed, _ = standardize(second)
    n3_ref[...] = (normed * gains[2:3] + shifts[2:3]).astype(BF)


def whole(shape, dtype=BF):
    return shaped(shape, dtype), full(shaped(shape, dtype))


def row_forward(t, split, mixed, cells, packs, wo_bias, wr_bias, gains, shifts, columns):
    feature_count, rows, width = cells.shape
    n = columns * rows
    side = 4 * rows
    ins = [(split, pl.BlockSpec(memory_space=pltpu.SMEM))] + [(m, full(m)) for m in mixed]
    ins += [(cells, column_block(cells, columns))]
    ins += pack_parts(packs, "feat_out") + pack_parts(packs, "row_out") + pack_parts(packs, "qkv")
    ins += [(a, full(a)) for a in (wo_bias, wr_bias, gains, shifts)]
    return call(
        partial(row_forward_kernel, feature_count=feature_count), "row_forward", (1,), t, ins,
        [whole((n, width), F32), whole((n, width)), whole((n, 12 * HD)), whole((4, n // side, side, side)),
         whole((n, 4 * HD)), whole((n, width), F32), whole((n, width))],
    )


def hidden_pair(t_ref, n3_ref, grad_ref, ups, packs, downs, grads, bias_grads, feature_count):
    columns, rows, width = grad_ref.shape
    g3 = live_columns(grad_ref[...], t_ref[0] * columns, feature_count).reshape(columns * rows, width)
    n3, gl = n3_ref[...], g3.astype(BF)
    n3_t, gl_t = n3.T, gl.T
    ms, dzs = [], []
    for up, pack, down, grad_ref, bias_grad in zip(ups, packs, downs, grads, bias_grads):
        bias = jnp.concatenate([pack[...].astype(F32)[j : j + 1] for j in range(4)], axis=-1)
        act, slope = gelu_parts(mm(n3, up[...]) + bias)
        m = act.astype(BF)
        dz = (mm_nt(gl, down[...]) * slope).astype(BF)
        grad_ref[:width] = mm(n3_t, dz).astype(BF)
        grad_ref[width:] = mm(gl_t, m).astype(BF)
        bias_grad[...] = column_sum(dz.astype(F32))
        ms.append(m)
        dzs.append(dz)
    out = mm(jnp.concatenate(ms, axis=-1), jnp.concatenate([d[...] for d in downs], axis=0))
    dn3 = mm_nt(jnp.concatenate(dzs, axis=-1), jnp.concatenate([u[...] for u in ups], axis=-1))
    return g3, out, dn3


def hidden_first_kernel(
    t_ref, d_ref, n3_ref, grad_ref, up0, up1, b0, b1, down0, down1, out_ref, dn3_ref, wg0, wg1, bg0, bg1,
    *, feature_count,
):
    _, out, dn3 = hidden_pair(
        t_ref, n3_ref, grad_ref, (up0, up1), (b0, b1), (down0, down1), (wg0, wg1), (bg0, bg1), feature_count)
    out_ref[...] = out
    dn3_ref[...] = dn3


def hidden_second_kernel(
    t_ref, d_ref, n3_ref, grad_ref, up0, up1, b0, b1, down0, down1, out_in, dn3_in, second_ref, down_bias, gains_ref,
    out_ref, g2_ref, gl2_ref, stats_ref, wg0, wg1, bg0, bg1, *, feature_count,
):
    g3, out, dn3 = hidden_pair(
        t_ref, n3_ref, grad_ref, (up0, up1), (b0, b1), (down0, down1), (wg0, wg1), (bg0, bg1), feature_count)
    second = second_ref[...]
    out_ref[...] = (second + out_in[...] + out + down_bias[...].astype(F32)).astype(BF)
    dn3 = dn3_in[...] + dn3
    normed, inverse = standardize(second)
    g2 = g3 + norm_backward(dn3, normed, inverse, gains_ref[...].astype(F32)[2:3])
    g2_ref[...] = g2
    gl2_ref[...] = g2.astype(BF)
    stats_ref[...] = rows_of([g3, g2, dn3 * normed, dn3])


def rows_of(arrays):
    return jnp.concatenate(
        [column_sum(a) for a in arrays] + [jnp.zeros((8 - len(arrays), arrays[0].shape[1]), F32)], axis=0)


def hidden_call(t, n3, grads, ups, packs, downs, columns, extra=None):
    n, width = n3.shape
    hidden = ups[0].shape[1]
    tail = [whole((2 * width, hidden))] * 2 + [whole((1, hidden), F32)] * 2
    ins = [(n3, full(n3)), (grads, column_block(grads, columns))]
    ins += [(a, full(a)) for a in ups] + pack_parts(packs, "bias") + [(a, full(a)) for a in downs]
    if extra is None:
        kernel, name = hidden_first_kernel, "hidden_first"
        results = [whole((n, width), F32)] * 2 + tail
    else:
        kernel, name = hidden_second_kernel, "hidden_second"
        ins += [(a, full(a)) for a in extra]
        results = [whole((n, width)), whole((n, width), F32), whole((n, width)), whole((8, width), F32)] + tail
    return call(partial(kernel, feature_count=grads.shape[0]), name, (1,), t, ins, results)


def attention_backward(q, k, v, p, do):
    dp = mm_nt(v, do)
    pf = p.astype(F32)
    ds = (pf * (dp - jnp.sum(dp * pf, axis=0, keepdims=True))).astype(BF)
    return mm_tn(ds, k) * SCALE, mm(ds, q) * SCALE, mm(p, do)


def row_backward_kernel(
    t_ref, d_ref, g2_ref, first_ref, qkv_ref, p_ref, gains_ref, w0, w1, w2, w3, r0, r1, r2, r3,
    dqkv_ref, gl1_ref, s0, s1, s2, s3, stats_ref, g1_scr,
):
    g2 = g2_ref[...]
    cells, width = g2.shape
    side = p_ref.shape[2]
    do = mm_nt(g2.astype(BF), wide((r0, r1, r2, r3))).astype(BF)
    for h in range(4):
        at = 3 * HD * h
        for b in range(0, cells, side):
            span = slice(b, b + side)
            q, k, v = (qkv_ref[span, at + c * HD : at + (c + 1) * HD] for c in range(3))
            parts = attention_backward(q, k, v, p_ref[h, b // side], do[span, HD * h : HD * (h + 1)])
            for c, part in enumerate(parts):
                dqkv_ref[span, at + c * HD : at + (c + 1) * HD] = part.astype(BF)
    dn2 = mm_nt(dqkv_ref[...], jnp.concatenate([stacked(w) for w in (w0, w1, w2, w3)], axis=-1))
    normed, inverse = standardize(first_ref[...])
    g1 = g2 + norm_backward(dn2, normed, inverse, gains_ref[...].astype(F32)[1:2])
    columns, rows, _ = g1_scr.shape
    g1_scr[...] = g1.reshape(columns, rows, width)
    gl1_ref[...] = g1.astype(BF)
    share = rows // 4
    for k, out in enumerate((s0, s1, s2, s3)):
        at = pl.multiple_of(lax.bitwise_xor(t_ref[0], k) * share, share)
        out[...] = g1_scr[:, pl.ds(at, share), :].reshape(columns * share, width).astype(BF)
    stats_ref[...] = rows_of([g1, dn2 * normed, dn2])


def row_backward(t, g2, first, qkv, p, gains, packs, rows):
    n, width = g2.shape
    ins = [(a, full(a)) for a in (g2, first, qkv, p, gains)]
    ins += pack_parts(packs, "qkv") + pack_parts(packs, "row_out")
    return call(
        row_backward_kernel, "row_backward", (1,), t, ins,
        [whole(qkv.shape), whole((n, width))] + [whole((n // 4, width))] * 4 + [whole((8, width), F32)],
        [pltpu.VMEM((n // rows, rows, width), F32)],
    )


def row_weights_kernel(t_ref, d_ref, n2_ref, dqkv_ref, gl2_ref, o2_ref, gl1_ref, m0, m1, m2, m3, keep_ref, send_ref):
    width = n2_ref.shape[1]
    columns = m0.shape[1] // RB
    grad = mm(n2_ref[...].T, dqkv_ref[...])
    out_grad = mm(gl2_ref[...].T, o2_ref[...])
    feat_grad = mm(gl1_ref[...].T, jnp.concatenate([in_order(m, columns) for m in (m0, m1, m2, m3)], axis=-1))
    for h in range(4):
        out = (keep_ref, send_ref)[h % 2]
        for c in range(3):
            out[h // 2, c * width : (c + 1) * width, :] = grad[:, (3 * h + c) * HD : (3 * h + c + 1) * HD].astype(BF)
        out[h // 2, 3 * width : 4 * width, :] = out_grad[:, HD * h : HD * (h + 1)].astype(BF)
        out[h // 2, 4 * width : 5 * width, :] = feat_grad[:, HD * h : HD * (h + 1)].astype(BF)


def row_weights(t, n2, dqkv, gl2, o2, gl1, mixed):
    width = n2.shape[1]
    return call(
        row_weights_kernel, "row_weights", (1,), t,
        [(a, full(a)) for a in (n2, dqkv, gl2, o2, gl1, *mixed)], [whole((2, 5 * width, HD))] * 2, vmem=24,
    )


def own_rows(t_ref, cells_ref, cell_scr, share):
    feature_count, block_rows, width = cells_ref.shape
    cell_scr[0:feature_count] = cells_ref[...].astype(F32)
    cell_scr[feature_count:] = jnp.zeros_like(cell_scr[feature_count:])
    at = pl.multiple_of(lax.rem(t_ref[0], block_rows // share) * share, share)
    return cell_scr[:, pl.ds(at, share), :].reshape(cell_scr.shape[0] * share, width)


def row_block(cells, share):
    feature_count, _, width = cells.shape
    per = RB // share
    return pl.BlockSpec((feature_count, RB, width), lambda i, t, d: (0, lax.div(t[0], per), 0))


def feature_again_kernel(
    t_ref, d_ref, cells_ref, gains_ref, shifts_ref, w0, w1, w2, w3, n1_ref, qkv_ref, p_ref, cell_scr, qkv_scr
):
    feature_count = cells_ref.shape[0]
    share, padded, _ = qkv_ref.shape
    normed, _ = standardize(own_rows(t_ref, cells_ref, cell_scr, share))
    low = (normed * gains_ref[...].astype(F32)[0:1] + shifts_ref[...].astype(F32)[0:1]).astype(BF)
    n1_ref[...] = low
    for h, w in enumerate((w0, w1, w2, w3)):
        packed = mm(low, three(w))
        for c in range(3):
            qkv_scr[c] = packed[:, c * HD : (c + 1) * HD]
        for r in range(share):
            q, k, v = (qkv_scr[c, pl.ds(r, padded, stride=share), :].astype(BF) for c in range(3))
            for c, part in enumerate((q, k, v)):
                qkv_ref[r, :, (3 * h + c) * HD : (3 * h + c + 1) * HD] = part
            p_ref[r, h] = feature_probabilities(q, k, feature_count)


def feature_again(t, cells, gains, shifts, weights, columns, share):
    width = cells.shape[2]
    padded = 4 * columns
    return call(
        feature_again_kernel, "feature_again", (1,), t,
        [(cells, row_block(cells, share))] + [(a, full(a)) for a in (gains, shifts, *weights)],
        [whole((padded * share, width)), whole((share, padded, 12 * HD)), whole((share, 4, padded, padded))],
        [pltpu.VMEM((padded, RB, width), F32), pltpu.VMEM((3, padded * share, HD), F32)], vmem=28,
    )


def feature_backward_kernel(
    t_ref, d_ref, r0, r1, r2, r3, f0, f1, f2, f3, qkv_ref, p_ref, n1_ref,
    g1_ref, dqkv_ref, keep_ref, send_ref, low_scr, do_scr, dqkv_scr,
):
    width = g1_ref.shape[1]
    share, padded, _ = qkv_ref.shape
    for k, piece in enumerate((r0, r1, r2, r3)):
        count = piece.shape[0]
        at = pl.multiple_of(lax.bitwise_xor(t_ref[0], k) * count, count)
        low_scr[pl.ds(at, count), :] = piece[...]
        g1_ref[pl.ds(at, count), :] = piece[...].astype(F32)
    do = mm_nt(low_scr[...], wide((f0, f1, f2, f3)))
    for h in range(4):
        do_scr[h] = do[:, h * HD : (h + 1) * HD]
    n1_t = n1_ref[...].T
    for h in range(4):
        for r in range(share):
            every = pl.ds(r, padded, stride=share)
            q, k, v = (qkv_ref[r, :, (3 * h + c) * HD : (3 * h + c + 1) * HD] for c in range(3))
            parts = attention_backward(q, k, v, p_ref[r, h], do_scr[h, every, :].astype(BF))
            for c, part in enumerate(parts):
                dqkv_scr[3 * h + c, every, :] = part
        out = (keep_ref, send_ref)[h % 2]
        for c in range(3):
            dqkv_ref[:, (3 * h + c) * HD : (3 * h + c + 1) * HD] = dqkv_scr[3 * h + c].astype(BF)
        grad = mm(n1_t, dqkv_ref[:, 3 * HD * h : 3 * HD * (h + 1)]).astype(BF)
        for c in range(3):
            out[h // 2, c * width : (c + 1) * width, :] = grad[:, c * HD : (c + 1) * HD]


def feature_backward(t, pieces, packs, qkv, p, n1):
    share, _, padded, _ = p.shape
    width = pieces[0].shape[1]
    cells = share * padded
    return call(
        feature_backward_kernel, "feature_backward", (1,), t,
        [(a, full(a)) for a in pieces] + pack_parts(packs, "feat_out") + [(a, full(a)) for a in (qkv, p, n1)],
        [whole((cells, width), F32), whole((cells, 12 * HD))] + [whole((2, 3 * width, HD))] * 2,
        [pltpu.VMEM((cells, width), BF), pltpu.VMEM((4, cells, HD), F32), pltpu.VMEM((12, cells, HD), F32)],
    )


def feature_input_kernel(
    t_ref, d_ref, cells_ref, g1_ref, dqkv_ref, gains_ref, w0, w1, w2, w3, stats_a, stats_b, b0, b1, b2, b3,
    out_ref, stats_ref, cell_scr,
):
    cells, width = g1_ref.shape
    share = cells // cell_scr.shape[0]
    normed, inverse = standardize(own_rows(t_ref, cells_ref, cell_scr, share))
    dn1 = mm_nt(dqkv_ref[...], jnp.concatenate([three(w) for w in (w0, w1, w2, w3)], axis=-1))
    g0 = g1_ref[...] + norm_backward(dn1, normed, inverse, gains_ref[...].astype(F32)[0:1])
    out_ref[...] = g0[: out_ref.shape[0]].astype(BF)
    stats_ref[0:8] = stats_a[...]
    stats_ref[8:16] = stats_b[...]
    stats_ref[4:5] = column_sum(dn1 * normed)
    stats_ref[5:6] = column_sum(dn1)
    stats_ref[16:24] = jnp.zeros((8, width), F32)
    for k, row in enumerate((b0, b1, b2, b3)):
        stats_ref[pl.ds(16 + lax.bitwise_xor(t_ref[0], k), 1), :] = row[...]


def feature_input(t, cells, g1, dqkv, gains, weights, sums, share):
    count, width = g1.shape
    kept = (cells.shape[0] + 1) // 2 * 2 * share
    return call(
        feature_input_kernel, "feature_input", (1,), t,
        [(cells, row_block(cells, share))] + [(a, full(a)) for a in (g1, dqkv, gains, *weights, *sums)],
        [whole((kept, width)), whole((24, width), F32)],
        [pltpu.VMEM((count // share, RB, width), F32)], vmem=28,
    )


def columns_home_kernel(t_ref, d_ref, p0, p1, p2, p3, out_ref):
    for k, piece in enumerate((p0, p1, p2, p3)):

        @pl.when(pl.program_id(0) == lax.bitwise_xor(t_ref[0], k))
        def _():
            out_ref[...] = piece[...]


def columns_home(t, pieces, feature_count):
    columns, rows, width = pieces[0].shape
    return call(
        columns_home_kernel, "columns_home", (4,), t, [(p, full(p)) for p in pieces],
        [(shaped((feature_count, rows, width)), pl.BlockSpec((columns, rows, width), lambda i, t, d: (i, 0, 0)))], vmem=16,
    )[0]


def rows_home_kernel(t_ref, d_ref, p0, p1, p2, p3, out_ref, scr):
    columns, rows, width = scr.shape
    share = rows // 4
    for k, piece in enumerate((p0, p1, p2, p3)):
        at = pl.multiple_of(lax.bitwise_xor(t_ref[0], k) * share, share)
        scr[:, pl.ds(at, share), :] = piece[...].astype(F32).reshape(columns, share, width)
    out_ref[...] = scr[...].astype(BF)


def rows_home(t, pieces, feature_count, rows):
    count, width = pieces[0].shape
    share = rows // 4
    columns = count // share // 5
    return call(
        rows_home_kernel, "rows_home", (5,), t,
        [(p, pl.BlockSpec((columns * share, width), lambda i, t, d: (i, 0))) for p in pieces],
        [(shaped((feature_count, rows, width)), pl.BlockSpec((columns, rows, width), lambda i, t, d: (i, 0, 0)))],
        [pltpu.VMEM((columns, rows, width), F32)], vmem=12,
    )[0]


def swap(values, axis, mask):
    count = lax.axis_size(axis)
    return lax.ppermute(values, axis, [(i, i ^ mask) for i in range(count)])


def gather_groups(own):
    far = swap(own, "tensor", 2)
    return own, swap(own, "tensor", 1), far, swap(far, "tensor", 1)


def held(values, *others):
    if isinstance(values, tuple):
        return lax.optimization_barrier((values[0], *others))[0], *values[1:]
    return lax.optimization_barrier((values, *others))[0]


def dp_masks():
    masks, mask = [], 1
    while mask < lax.axis_size("dp"):
        masks.append(mask)
        mask *= 2
    return masks


def digit(d_ref, mask):
    return lax.rem(lax.div(d_ref[0], mask), 2)


def merge_kernel(t_ref, d_ref, *refs, jobs):
    at = 0
    ins = []
    for job in jobs:
        ins.append((refs[at : at + len(job["own"])], refs[at + len(job["own"]) : at + 2 * len(job["own"])]))
        at += 2 * len(job["own"])
    for job, (own, other) in zip(jobs, ins):
        outs = refs[at : at + job["outs"]]
        at += job["outs"]
        kind, mask = job["next"]
        if job["join"] is None:
            start, rows = job["rows"]

            def total(j, first, count):
                part = (Ellipsis, pl.ds(start + first, count), slice(None))
                return own[j][part].astype(F32) + other[j][part].astype(F32)

            if kind == "half":
                half = rows // 2
                for out, side in zip(outs, (digit(d_ref, mask), 1 - digit(d_ref, mask))):
                    first = pl.multiple_of(side * half, half)
                    for j in range(len(own)):
                        sums = total(j, first, half).astype(out.dtype)
                        if len(own) > 1:
                            out[j] = sums
                        else:
                            out[...] = sums
            elif kind == "group":
                sums = total(0, 0, rows)
                outs[0][...] = sums[0].astype(outs[0].dtype)
                outs[1][...] = sums[1].astype(outs[1].dtype)
            else:
                outs[0][...] = total(0, 0, rows).astype(outs[0].dtype)
        else:
            rows = own[0].shape[-2]
            side = digit(d_ref, job["join"])
            for source, place in ((own[0], side), (other[0], 1 - side)):
                first = pl.multiple_of(place * rows, rows)
                outs[0][..., pl.ds(first, rows), :] = source[...].astype(outs[0].dtype)


class Chain:
    def __init__(self, own, other, order, rows=None, low=BF):
        self.own, self.other, self.low = tuple(own), tuple(other), low
        dp = [m for m in order if m != "x"]
        halved = dp[:-1] if low == BF else []
        self.plan = []
        for m in order:
            if m == "x":
                self.plan.append(("group" if low == BF else "whole", "x", None))
            else:
                self.plan.append(("half" if m in halved else "whole", m, None))
        for m in reversed(halved):
            self.plan.append(("whole", m, m))
        self.join = None
        self.rows = rows
        self.result = None

    def job(self):
        n, w = self.own[0].shape[-2:]
        start, rows = self.rows or (0, n)
        lead = self.own[0].shape[:-2]
        if len(self.own) > 1:
            lead = (len(self.own),)
        kind, mask, _ = self.plan[0] if self.plan else ("final", None, None)
        if self.join is not None:
            shape = lead + (2 * n, w)
        elif kind == "half":
            shape = lead + (rows // 2, w)
        elif kind == "group":
            shape = (rows, w)
        else:
            shape = lead + (rows, w)
        out = shaped(shape, F32 if kind == "final" else self.low)
        count = 2 if kind in ("half", "group") else 1
        spec = {"own": self.own, "other": self.other, "next": (kind, mask), "join": self.join,
                "rows": (start, rows), "outs": count}
        return spec, [out] * count

    def take(self, outs):
        if not self.plan:
            self.result = outs[0]
            return
        kind, mask, join = self.plan.pop(0)
        sent = outs[-1]
        self.own = (outs[0],)
        self.other = (swap(sent, "tensor", 2) if mask == "x" else swap(sent, "dp", mask),)
        self.sent = sent
        self.join, self.rows = join, None


def merge(t, chains):
    jobs, outs, ins = [], [], []
    for chain in chains:
        spec, shapes = chain.job()
        ins += [*spec["own"], *spec["other"]]
        jobs.append({k: (v if k != "own" else [0] * len(v)) for k, v in spec.items() if k != "other"})
        outs.append(shapes)
    flat = [o for shapes in outs for o in shapes]
    results = call(partial(merge_kernel, jobs=jobs), "merge", (), t, [(a, VMEM) for a in ins], [(o, VMEM) for o in flat], vmem=20)
    at = 0
    for chain, shapes in zip(chains, outs):
        chain.take(results[at : at + len(shapes)])
        at += len(shapes)
    return results


def shards(
    table_cells, splits, feat_qkv, feat_out, feat_out_bias, row_qkv, row_out, row_out_bias,
    up_weight, up_bias, down_weight, down_bias, norm_gains, norm_biases, cotangent,
):
    shape = table_cells.shape
    _, row_count, feature_count, width = shape
    share = row_count // 4
    columns = -(-feature_count // (4 * FB)) * FB
    t = tuple(lax.axis_index(a).astype(jnp.int32).reshape(1) for a in ("tensor", "dp"))
    masks = dp_masks()
    cells = jnp.transpose(table_cells[0], (1, 0, 2))
    grads = jnp.transpose(cotangent[0], (1, 0, 2))
    fob, rob, dnb, upb = (b.reshape(1, width) for b in (feat_out_bias, row_out_bias, down_bias, up_bias))
    fq = jnp.transpose(feat_qkv, (1, 0, 2))
    rq = jnp.transpose(row_qkv, (1, 0, 2))

    packs = gather_groups(pack(t, rq, feat_out, row_out, upb))
    mixed = feature_forward(t, cells, norm_gains, norm_biases, fq, columns)
    mixed = [mixed[0]] + [swap(mixed[k], "tensor", k) for k in (1, 2, 3)]
    ups = gather_groups(held(up_weight, mixed[2], mixed[3]))
    downs = gather_groups(held(down_weight, mixed[2], mixed[3]))
    fqs = gather_groups(held(fq, downs[2]))

    first, n2, row_packed, row_p, o2, second, n3 = row_forward(
        t, splits, mixed, cells, packs, fob, rob, norm_gains, norm_biases, columns)
    out_a, dn3_a, hg0, hg1, bg0, bg1 = hidden_call(t, n3, grads, ups[:2], packs[:2], downs[:2], columns)
    out_f, g2, gl2, stats_a, hg2, hg3, bg2, bg3 = hidden_call(
        t, n3, grads, ups[2:], packs[2:], downs[2:], columns, [out_a, dn3_a, second, dnb, norm_gains])

    r1, r3 = swap(hg1, "tensor", 1), swap(hg3, "tensor", 1)
    up_chain = Chain((hg0, hg2), (r1, r3), [masks[0], "x"] + masks[1:], rows=(0, width))
    down_chain = Chain((hg0, hg2), (r1, r3), masks[1:] + ["x", masks[0]], rows=(width, width))
    sent = merge(t, [up_chain, down_chain])

    dqkv_r, gl1, s0, s1, s2, s3, stats_b = row_backward(
        held(t, *sent), g2, first, row_packed, row_p, norm_gains, packs, row_count)
    pieces = [s0] + [swap(s, "tensor", k) for k, s in ((1, s1), (2, s2), (3, s3))]

    row_keep, row_send = row_weights(t, n2, dqkv_r, gl2, o2, gl1, mixed)
    row_chain = Chain((row_keep,), (swap(row_send, "tensor", 1),), [masks[0], "x"] + masks[1:])
    sent = merge(held(t, row_send), [up_chain, down_chain])
    sent = merge(held(t, *sent), [row_chain])
    n1, feat_packed, feat_p = feature_again(
        held(t, *sent), cells, norm_gains, norm_biases, fqs, columns, share)
    out_pieces = gather_groups(held(out_f.reshape(columns, row_count, width), pieces[2], pieces[3]))

    g1, dqkv_f, feat_keep, feat_send = feature_backward(t, pieces, packs, feat_packed, feat_p, n1)
    sent = merge(held(t, dqkv_f), [up_chain, down_chain])
    feat_chain = Chain((feat_keep,), (swap(feat_send, "tensor", 1),), ["x"] + masks)
    g0, sums = feature_input(
        held(t, *sent), cells, g1, dqkv_f, norm_gains, fqs, (stats_a, stats_b, bg0, bg1, bg2, bg3), share)
    small_chain = Chain((sums,), (swap(sums, "tensor", 1),), ["x"] + masks, low=F32)

    chains = [feat_chain, small_chain, row_chain, up_chain, down_chain]
    sent = merge(held(t, sums), chains)
    g0s = gather_groups(held(g0, feat_chain.other[0]))
    output = columns_home(held(t, *sent), out_pieces, feature_count)
    sent = merge(held(t, output), [feat_chain, small_chain, up_chain, down_chain])
    while True:
        chains = [c for c in chains if c.result is None]
        if not chains:
            break
        sent = merge(held(t, *sent), chains)
    input_grad = rows_home(t, g0s, feature_count, row_count)

    up_grad, down_grad = up_chain.result, down_chain.result.T
    row_grad, feat_grad, small = row_chain.result, feat_chain.result, small_chain.result

    def qkv_shape(grad):
        return jnp.transpose(grad.reshape(3, width, HD), (1, 0, 2))

    home = lambda a: jnp.transpose(a, (1, 0, 2)).reshape(shape)
    return (
        home(output),
        home(input_grad),
        qkv_shape(feat_grad),
        row_grad[4 * width :].T,
        small[8],
        qkv_shape(row_grad[: 3 * width]),
        row_grad[3 * width : 4 * width].T,
        small[1],
        up_grad,
        lax.dynamic_index_in_dim(small, 16 + t[0][0], 0, keepdims=False),
        down_grad,
        small[0],
        jnp.stack([small[4], small[9], small[2]]),
        jnp.stack([small[5], small[10], small[3]]),
    )


def solution(mesh):
    return jax.shard_map(
        shards,
        mesh=mesh,
        in_specs=(
            P("dp", None, None, None), P("dp"), P(None, None, "tensor"), P("tensor", None), P(),
            P(None, None, "tensor"), P("tensor", None), P(), P(None, "tensor"), P("tensor"),
            P("tensor", None), P(), P(), P(), P("dp", None, None, None),
        ),
        out_specs=(
            P("dp", None, None, None), P("dp", None, None, None), P(None, None, "tensor"),
            P("tensor", None), P(), P(None, None, "tensor"), P("tensor", None), P(),
            P(None, "tensor"), P("tensor"), P("tensor", None), P(), P(), P(),
        ),
        check_vma=False,
    )
```

```python
from functools import partial

import jax
import jax.numpy as jnp
from jax import lax
from jax.experimental import pallas as pl
from jax.experimental.pallas import tpu as pltpu
from jax.sharding import PartitionSpec as P

HD = 128
EPSILON = 1e-05
NEGATIVE = -1e30
SCALE = HD**-0.5
BF = jnp.bfloat16
F32 = jnp.float32
MIB = 1 << 20
FB = 8
RB = 16


def mm(a, b):
    return jnp.dot(a, b, preferred_element_type=F32)


def mm_nt(a, b):
    return lax.dot_general(a, b, (((1,), (1,)), ((), ())), preferred_element_type=F32)


def mm_tn(a, b):
    return lax.dot_general(a, b, (((0,), (0,)), ((), ())), preferred_element_type=F32)


def standardize(values):
    centered = values - jnp.mean(values, axis=-1, keepdims=True)
    inverse = lax.rsqrt(jnp.mean(centered * centered, axis=-1, keepdims=True) + EPSILON)
    return centered * inverse, inverse


def norm_backward(upstream, normed, inverse, gain):
    scaled = upstream * gain
    return inverse * (
        scaled
        - jnp.mean(scaled, axis=-1, keepdims=True)
        - normed * jnp.mean(scaled * normed, axis=-1, keepdims=True)
    )


def column_sum(values):
    return jnp.sum(values, axis=0, keepdims=True)


def softmax_keys(scores):
    grown = jnp.exp(scores - jnp.max(scores, axis=0, keepdims=True))
    return grown * (1.0 / jnp.sum(grown, axis=0, keepdims=True))


def gelu_parts(z):
    t = 1.0 / (1.0 + (0.3275911 * 0.7071067811865476) * jnp.abs(z))
    e = jnp.exp(-0.5 * z * z)
    poly = t * (
        0.127414796 + t * (-0.142248368 + t * (0.7107068705 + t * (-0.7265760135 + t * 0.5307027145)))
    )
    tail = poly * e
    cdf = jnp.where(z >= 0, 1.0 - tail, tail)
    return z * cdf, cdf + z * (e * 0.3989422804014327)


def feature_probabilities(q, k, feature_count):
    scores = mm_nt(k, q) * SCALE
    key = lax.broadcasted_iota(jnp.int32, scores.shape, 0)
    return softmax_keys(jnp.where(key < feature_count, scores, NEGATIVE)).astype(BF)


def three(w):
    return jnp.concatenate([w[0], w[1], w[2]], axis=-1)


def stacked(w):
    n = w.shape[0] // 3
    return jnp.concatenate([w[c * n : (c + 1) * n] for c in range(3)], axis=-1)


def wide(pieces):
    n = pieces[0].shape[0] // 4
    return jnp.concatenate(
        [jnp.concatenate([p[j * n : (j + 1) * n] for j in range(4)], axis=-1) for p in pieces], axis=0)


def live_columns(block, first, feature_count):
    values = block.astype(F32)
    index = first + lax.broadcasted_iota(jnp.int32, values.shape, 0)
    return jnp.where(index < feature_count, values, 0.0)


ANY = pl.BlockSpec(memory_space=pl.ANY)
VMEM = pl.BlockSpec(memory_space=pltpu.VMEM)


def full(a):
    zeros = (0,) * len(a.shape)
    return pl.BlockSpec(a.shape, lambda *_: zeros)


def shaped(shape, dtype=BF):
    return jax.ShapeDtypeStruct(shape, dtype)


def call(kernel, name, grid, t, ins, outs, scratch=(), vmem=32, us=1):
    spec = pltpu.PrefetchScalarGridSpec(
        num_scalar_prefetch=2,
        grid=grid,
        in_specs=[s for _, s in ins],
        out_specs=[s for _, s in outs],
        scratch_shapes=list(scratch),
    )
    return pl.pallas_call(
        kernel,
        grid_spec=spec,
        out_shape=[a for a, _ in outs],
        compiler_params=pltpu.CompilerParams(vmem_limit_bytes=vmem * MIB),
        cost_estimate=pl.CostEstimate(flops=1, bytes_accessed=1, transcendentals=0),
        name=name,
    )(*t, *[a for a, _ in ins])


def pack_kernel(t_ref, d_ref, rq_ref, fo_ref, ro_ref, ub_ref, out_ref):
    width = rq_ref.shape[1]
    for c in range(3):
        out_ref[c * width : (c + 1) * width] = rq_ref[c]
    at = 3 * width
    for source in (fo_ref, ro_ref):
        for j in range(4):
            out_ref[at : at + HD] = source[:, j * HD : (j + 1) * HD]
            at += HD
    bias = jnp.concatenate([ub_ref[...].astype(F32)[:, j * HD : (j + 1) * HD] for j in range(4)], axis=0)
    out_ref[at : at + 16] = jnp.concatenate([bias, jnp.zeros((12, HD), F32)], axis=0).astype(BF)


def pack(t, rq, fo, ro, ub):
    out = shaped((3 * rq.shape[1] + 8 * HD + 16, HD))
    return call(pack_kernel, "pack", (), t, [(a, VMEM) for a in (rq, fo, ro, ub)], [(out, VMEM)], vmem=60)[0]


def pack_part(pack, what):
    rows = pack.shape[0] - 8 * HD - 16
    size, at = {"qkv": (rows, 0), "feat_out": (4 * HD, rows), "row_out": (4 * HD, rows + 4 * HD),
                "bias": (16, rows + 8 * HD)}[what]
    return pl.BlockSpec((size, HD), lambda *_: (at // size, 0))


def pack_parts(packs, what):
    return [(p, pack_part(p, what)) for p in packs]


def feature_forward_kernel(
    t_ref, d_ref, cells_ref, gains_ref, shifts_ref, w_ref, o0, o1, o2, o3, qkv_scr, mix_scr
):
    feature_count, rows, width = cells_ref.shape
    padded = qkv_scr.shape[1] // rows

    @pl.when(pl.program_id(0) == 0)
    def _():
        qkv_scr[...] = jnp.zeros_like(qkv_scr)

    cells = cells_ref[...].astype(F32).reshape(feature_count * rows, width)
    normed, _ = standardize(cells)
    low = (normed * gains_ref[...].astype(F32)[0:1] + shifts_ref[...].astype(F32)[0:1]).astype(BF)
    qkv = mm(low, three(w_ref))
    for c in range(3):
        qkv_scr[c, 0 : feature_count * rows, :] = qkv[:, c * HD : (c + 1) * HD]
    for r in range(rows):
        every = pl.ds(r, padded, stride=rows)
        q, k, v = (qkv_scr[c, every, :].astype(BF) for c in range(3))
        mix_scr[every, :] = mm_tn(feature_probabilities(q, k, feature_count), v)
    count = o0.shape[1]
    for k, out in enumerate((o0, o1, o2, o3)):
        at = pl.multiple_of(lax.bitwise_xor(t_ref[0], k) * count, count)
        out[0] = mix_scr[pl.ds(at, count), :].astype(BF)


def feature_forward(t, cells, gains, shifts, weight, columns):
    feature_count, row_count, width = cells.shape
    padded = 4 * columns
    steps = row_count // RB
    out = (shaped((steps, columns * RB, HD)), pl.BlockSpec((1, columns * RB, HD), lambda i, t, d: (i, 0, 0)))
    return call(
        feature_forward_kernel, "feature_forward", (steps,), t,
        [(cells, pl.BlockSpec((feature_count, RB, width), lambda i, t, d: (0, i, 0)))]
        + [(a, full(a)) for a in (gains, shifts, weight)],
        [out] * 4,
        [pltpu.VMEM((3, padded * RB, HD), F32), pltpu.VMEM((padded * RB, HD), F32)], vmem=28, us=11
    )


def column_block(array, columns):
    _, rows, width = array.shape
    return pl.BlockSpec((columns, rows, width), lambda i, t, d: (t[0], 0, 0))


def in_order(m, columns):
    steps = m.shape[0]
    halves = [m[i].reshape(columns, RB, HD) for i in range(steps)]
    return jnp.concatenate(halves, axis=1).reshape(columns * RB * steps, HD)


def row_forward_kernel(
    t_ref, d_ref, split_ref, m0, m1, m2, m3, cells_ref, f0, f1, f2, f3, r0, r1, r2, r3, w0, w1, w2, w3,
    wo_bias, wr_bias, gains_ref, shifts_ref,
    first_ref, n2_ref, qkv_ref, p_ref, o2_ref, second_ref, n3_ref, *, feature_count,
):
    columns, rows, width = cells_ref.shape
    cells = columns * rows
    side = p_ref.shape[2]
    key = lax.broadcasted_iota(jnp.int32, (side, side), 0)
    query = lax.broadcasted_iota(jnp.int32, (side, side), 1)
    same = lax.div(query, rows) == lax.div(key, rows)
    bias = jnp.where(jnp.logical_and(same, lax.rem(key, rows) < split_ref[0]), 0.0, NEGATIVE)

    gains = gains_ref[...].astype(F32)
    shifts = shifts_ref[...].astype(F32)
    stream = live_columns(cells_ref[...], t_ref[0] * columns, feature_count).reshape(cells, width)
    mixed = jnp.concatenate([in_order(m, columns) for m in (m0, m1, m2, m3)], axis=-1)
    first = stream + mm(mixed, wide((f0, f1, f2, f3))) + wo_bias[...].astype(F32)
    first_ref[...] = first
    normed, _ = standardize(first)
    low = (normed * gains[1:2] + shifts[1:2]).astype(BF)
    n2_ref[...] = low
    for h, w in enumerate((w0, w1, w2, w3)):
        base = 3 * HD * h
        qkv_ref[:, base : base + 3 * HD] = mm(low, stacked(w)).astype(BF)
        for b in range(0, cells, side):
            span = slice(b, b + side)
            q, k, v = (qkv_ref[span, base + c * HD : base + (c + 1) * HD] for c in range(3))
            p = softmax_keys(mm_nt(k, q) * SCALE + bias).astype(BF)
            p_ref[h, b // side] = p
            o2_ref[span, h * HD : (h + 1) * HD] = mm_tn(p, v).astype(BF)
    second = first + mm(o2_ref[...], wide((r0, r1, r2, r3))) + wr_bias[...].astype(F32)
    second_ref[...] = second
    normed, _ = standardize(second)
    n3_ref[...] = (normed * gains[2:3] + shifts[2:3]).astype(BF)


def whole(shape, dtype=BF):
    return shaped(shape, dtype), full(shaped(shape, dtype))


def row_forward(t, split, mixed, cells, packs, wo_bias, wr_bias, gains, shifts, columns):
    feature_count, rows, width = cells.shape
    n = columns * rows
    side = 4 * rows
    ins = [(split, pl.BlockSpec(memory_space=pltpu.SMEM))] + [(m, full(m)) for m in mixed]
    ins += [(cells, column_block(cells, columns))]
    ins += pack_parts(packs, "feat_out") + pack_parts(packs, "row_out") + pack_parts(packs, "qkv")
    ins += [(a, full(a)) for a in (wo_bias, wr_bias, gains, shifts)]
    return call(
        partial(row_forward_kernel, feature_count=feature_count), "row_forward", (1,), t, ins,
        [whole((n, width), F32), whole((n, width)), whole((n, 12 * HD)), whole((4, n // side, side, side)),
         whole((n, 4 * HD)), whole((n, width), F32), whole((n, width))], us=9
    )


def hidden_pair(t_ref, n3_ref, grad_ref, ups, packs, downs, grads, bias_grads, feature_count):
    columns, rows, width = grad_ref.shape
    g3 = live_columns(grad_ref[...], t_ref[0] * columns, feature_count).reshape(columns * rows, width)
    n3, gl = n3_ref[...], g3.astype(BF)
    n3_t, gl_t = n3.T, gl.T
    ms, dzs = [], []
    for up, pack, down, grad_ref, bias_grad in zip(ups, packs, downs, grads, bias_grads):
        bias = jnp.concatenate([pack[...].astype(F32)[j : j + 1] for j in range(4)], axis=-1)
        act, slope = gelu_parts(mm(n3, up[...]) + bias)
        m = act.astype(BF)
        dz = (mm_nt(gl, down[...]) * slope).astype(BF)
        grad_ref[:width] = mm(n3_t, dz).astype(BF)
        grad_ref[width:] = mm(gl_t, m).astype(BF)
        bias_grad[...] = column_sum(dz.astype(F32))
        ms.append(m)
        dzs.append(dz)
    out = mm(jnp.concatenate(ms, axis=-1), jnp.concatenate([d[...] for d in downs], axis=0))
    dn3 = mm_nt(jnp.concatenate(dzs, axis=-1), jnp.concatenate([u[...] for u in ups], axis=-1))
    return g3, out, dn3


def hidden_first_kernel(
    t_ref, d_ref, n3_ref, grad_ref, up0, up1, b0, b1, down0, down1, out_ref, dn3_ref, wg0, wg1, bg0, bg1,
    *, feature_count,
):
    _, out, dn3 = hidden_pair(
        t_ref, n3_ref, grad_ref, (up0, up1), (b0, b1), (down0, down1), (wg0, wg1), (bg0, bg1), feature_count)
    out_ref[...] = out
    dn3_ref[...] = dn3


def hidden_second_kernel(
    t_ref, d_ref, n3_ref, grad_ref, up0, up1, b0, b1, down0, down1, out_in, dn3_in, second_ref, down_bias, gains_ref,
    out_ref, g2_ref, gl2_ref, stats_ref, wg0, wg1, bg0, bg1, *, feature_count,
):
    g3, out, dn3 = hidden_pair(
        t_ref, n3_ref, grad_ref, (up0, up1), (b0, b1), (down0, down1), (wg0, wg1), (bg0, bg1), feature_count)
    second = second_ref[...]
    out_ref[...] = (second + out_in[...] + out + down_bias[...].astype(F32)).astype(BF)
    dn3 = dn3_in[...] + dn3
    normed, inverse = standardize(second)
    g2 = g3 + norm_backward(dn3, normed, inverse, gains_ref[...].astype(F32)[2:3])
    g2_ref[...] = g2
    gl2_ref[...] = g2.astype(BF)
    stats_ref[...] = rows_of([g3, g2, dn3 * normed, dn3])


def rows_of(arrays):
    return jnp.concatenate(
        [column_sum(a) for a in arrays] + [jnp.zeros((8 - len(arrays), arrays[0].shape[1]), F32)], axis=0)


def hidden_call(t, n3, grads, ups, packs, downs, columns, extra=None):
    n, width = n3.shape
    hidden = ups[0].shape[1]
    tail = [whole((2 * width, hidden))] * 2 + [whole((1, hidden), F32)] * 2
    ins = [(n3, full(n3)), (grads, column_block(grads, columns))]
    ins += [(a, full(a)) for a in ups] + pack_parts(packs, "bias") + [(a, full(a)) for a in downs]
    if extra is None:
        kernel, name = hidden_first_kernel, "hidden_first"
        results = [whole((n, width), F32)] * 2 + tail
    else:
        kernel, name = hidden_second_kernel, "hidden_second"
        ins += [(a, full(a)) for a in extra]
        results = [whole((n, width)), whole((n, width), F32), whole((n, width)), whole((8, width), F32)] + tail
    return call(partial(kernel, feature_count=grads.shape[0]), name, (1,), t, ins, results, us=7)


def attention_backward(q, k, v, p, do):
    dp = mm_nt(v, do)
    pf = p.astype(F32)
    ds = (pf * (dp - jnp.sum(dp * pf, axis=0, keepdims=True))).astype(BF)
    return mm_tn(ds, k) * SCALE, mm(ds, q) * SCALE, mm(p, do)


def row_backward_kernel(
    t_ref, d_ref, g2_ref, first_ref, qkv_ref, p_ref, gains_ref, w0, w1, w2, w3, r0, r1, r2, r3,
    dqkv_ref, gl1_ref, s0, s1, s2, s3, stats_ref, g1_scr,
):
    g2 = g2_ref[...]
    cells, width = g2.shape
    side = p_ref.shape[2]
    do = mm_nt(g2.astype(BF), wide((r0, r1, r2, r3))).astype(BF)
    for h in range(4):
        at = 3 * HD * h
        for b in range(0, cells, side):
            span = slice(b, b + side)
            q, k, v = (qkv_ref[span, at + c * HD : at + (c + 1) * HD] for c in range(3))
            parts = attention_backward(q, k, v, p_ref[h, b // side], do[span, HD * h : HD * (h + 1)])
            for c, part in enumerate(parts):
                dqkv_ref[span, at + c * HD : at + (c + 1) * HD] = part.astype(BF)
    dn2 = mm_nt(dqkv_ref[...], jnp.concatenate([stacked(w) for w in (w0, w1, w2, w3)], axis=-1))
    normed, inverse = standardize(first_ref[...])
    g1 = g2 + norm_backward(dn2, normed, inverse, gains_ref[...].astype(F32)[1:2])
    columns, rows, _ = g1_scr.shape
    g1_scr[...] = g1.reshape(columns, rows, width)
    gl1_ref[...] = g1.astype(BF)
    share = rows // 4
    for k, out in enumerate((s0, s1, s2, s3)):
        at = pl.multiple_of(lax.bitwise_xor(t_ref[0], k) * share, share)
        out[...] = g1_scr[:, pl.ds(at, share), :].reshape(columns * share, width).astype(BF)
    stats_ref[...] = rows_of([g1, dn2 * normed, dn2])


def row_backward(t, g2, first, qkv, p, gains, packs, rows):
    n, width = g2.shape
    ins = [(a, full(a)) for a in (g2, first, qkv, p, gains)]
    ins += pack_parts(packs, "qkv") + pack_parts(packs, "row_out")
    return call(
        row_backward_kernel, "row_backward", (1,), t, ins,
        [whole(qkv.shape), whole((n, width))] + [whole((n // 4, width))] * 4 + [whole((8, width), F32)],
        [pltpu.VMEM((n // rows, rows, width), F32)], us=9
    )


def row_weights_kernel(t_ref, d_ref, n2_ref, dqkv_ref, gl2_ref, o2_ref, gl1_ref, m0, m1, m2, m3, keep_ref, send_ref):
    width = n2_ref.shape[1]
    columns = m0.shape[1] // RB
    grad = mm(n2_ref[...].T, dqkv_ref[...]).astype(BF)
    out_grad = mm(gl2_ref[...].T, o2_ref[...]).astype(BF)
    feat_grad = mm(gl1_ref[...].T, jnp.concatenate([in_order(m, columns) for m in (m0, m1, m2, m3)], axis=-1)).astype(BF)
    for h in range(4):
        out = (keep_ref, send_ref)[h % 2].at[h // 2]
        blocks = [grad[:, (3 * h + c) * HD : (3 * h + c + 1) * HD] for c in range(3)]
        blocks += [out_grad[:, HD * h : HD * (h + 1)], feat_grad[:, HD * h : HD * (h + 1)]]
        for at, first, count, lane in row_places(width):
            out[at : at + count, lane * HD : (lane + 1) * HD] = blocks[first // width][first % width : first % width + count]


def row_places(width):
    tall = 5 * width // 4
    first = 0
    while first < 5 * width:
        count = min(width - first % width, tall - first % tall)
        yield first % tall, first, count, first // tall
        first += count


def row_weights(t, n2, dqkv, gl2, o2, gl1, mixed):
    width = n2.shape[1]
    return call(
        row_weights_kernel, "row_weights", (1,), t,
        [(a, full(a)) for a in (n2, dqkv, gl2, o2, gl1, *mixed)], [whole((2, 5 * width // 4, 4 * HD))] * 2, vmem=24,
    )


def own_rows(t_ref, cells_ref, cell_scr, share):
    feature_count, block_rows, width = cells_ref.shape
    cell_scr[0:feature_count] = cells_ref[...].astype(F32)
    cell_scr[feature_count:] = jnp.zeros_like(cell_scr[feature_count:])
    at = pl.multiple_of(lax.rem(t_ref[0], block_rows // share) * share, share)
    return cell_scr[:, pl.ds(at, share), :].reshape(cell_scr.shape[0] * share, width)


def row_block(cells, share):
    feature_count, _, width = cells.shape
    per = RB // share
    return pl.BlockSpec((feature_count, RB, width), lambda i, t, d: (0, lax.div(t[0], per), 0))


def feature_again_kernel(
    t_ref, d_ref, cells_ref, gains_ref, shifts_ref, w0, w1, w2, w3, n1_ref, qkv_ref, p_ref, cell_scr, qkv_scr
):
    feature_count = cells_ref.shape[0]
    share, padded, _ = qkv_ref.shape
    normed, _ = standardize(own_rows(t_ref, cells_ref, cell_scr, share))
    low = (normed * gains_ref[...].astype(F32)[0:1] + shifts_ref[...].astype(F32)[0:1]).astype(BF)
    n1_ref[...] = low
    for h, w in enumerate((w0, w1, w2, w3)):
        packed = mm(low, three(w))
        for c in range(3):
            qkv_scr[c] = packed[:, c * HD : (c + 1) * HD]
        for r in range(share):
            q, k, v = (qkv_scr[c, pl.ds(r, padded, stride=share), :].astype(BF) for c in range(3))
            for c, part in enumerate((q, k, v)):
                qkv_ref[r, :, (3 * h + c) * HD : (3 * h + c + 1) * HD] = part
            p_ref[r, h] = feature_probabilities(q, k, feature_count)


def feature_again(t, cells, gains, shifts, weights, columns, share):
    width = cells.shape[2]
    padded = 4 * columns
    return call(
        feature_again_kernel, "feature_again", (1,), t,
        [(cells, row_block(cells, share))] + [(a, full(a)) for a in (gains, shifts, *weights)],
        [whole((padded * share, width)), whole((share, padded, 12 * HD)), whole((share, 4, padded, padded))],
        [pltpu.VMEM((padded, RB, width), F32), pltpu.VMEM((3, padded * share, HD), F32)], vmem=28, us=4
    )


def feature_backward_kernel(
    t_ref, d_ref, r0, r1, r2, r3, f0, f1, f2, f3, qkv_ref, p_ref, n1_ref,
    g1_ref, dqkv_ref, keep_ref, send_ref, low_scr, do_scr, dqkv_scr,
):
    width = g1_ref.shape[1]
    share, padded, _ = qkv_ref.shape
    for k, piece in enumerate((r0, r1, r2, r3)):
        count = piece.shape[0]
        at = pl.multiple_of(lax.bitwise_xor(t_ref[0], k) * count, count)
        low_scr[pl.ds(at, count), :] = piece[...]
        g1_ref[pl.ds(at, count), :] = piece[...].astype(F32)
    do = mm_nt(low_scr[...], wide((f0, f1, f2, f3)))
    for h in range(4):
        do_scr[h] = do[:, h * HD : (h + 1) * HD]
    n1_t = n1_ref[...].T
    for h in range(4):
        for r in range(share):
            every = pl.ds(r, padded, stride=share)
            q, k, v = (qkv_ref[r, :, (3 * h + c) * HD : (3 * h + c + 1) * HD] for c in range(3))
            parts = attention_backward(q, k, v, p_ref[r, h], do_scr[h, every, :].astype(BF))
            for c, part in enumerate(parts):
                dqkv_scr[3 * h + c, every, :] = part
        out = (keep_ref, send_ref)[h % 2]
        for c in range(3):
            dqkv_ref[:, (3 * h + c) * HD : (3 * h + c + 1) * HD] = dqkv_scr[3 * h + c].astype(BF)
        grad = mm(n1_t, dqkv_ref[:, 3 * HD * h : 3 * HD * (h + 1)]).astype(BF)
        for c in range(3):
            out[h // 2, c * width : (c + 1) * width, :] = grad[:, c * HD : (c + 1) * HD]


def feature_backward(t, pieces, packs, qkv, p, n1):
    share, _, padded, _ = p.shape
    width = pieces[0].shape[1]
    cells = share * padded
    return call(
        feature_backward_kernel, "feature_backward", (1,), t,
        [(a, full(a)) for a in pieces] + pack_parts(packs, "feat_out") + [(a, full(a)) for a in (qkv, p, n1)],
        [whole((cells, width), F32), whole((cells, 12 * HD))] + [whole((2, 3 * width, HD))] * 2,
        [pltpu.VMEM((cells, width), BF), pltpu.VMEM((4, cells, HD), F32), pltpu.VMEM((12, cells, HD), F32)], us=11
    )


def feature_input_kernel(
    t_ref, d_ref, cells_ref, g1_ref, dqkv_ref, gains_ref, w0, w1, w2, w3, stats_a, stats_b, b0, b1, b2, b3,
    out_ref, stats_ref, cell_scr, sums_scr,
):
    cells, width = g1_ref.shape
    share = cells // cell_scr.shape[0]
    normed, inverse = standardize(own_rows(t_ref, cells_ref, cell_scr, share))
    dn1 = mm_nt(dqkv_ref[...], jnp.concatenate([three(w) for w in (w0, w1, w2, w3)], axis=-1))
    g0 = g1_ref[...] + norm_backward(dn1, normed, inverse, gains_ref[...].astype(F32)[0:1])
    out_ref[...] = g0[: out_ref.shape[0]].astype(BF)
    sums_scr[0:8] = stats_a[...]
    sums_scr[8:16] = stats_b[...]
    sums_scr[4:5] = column_sum(dn1 * normed)
    sums_scr[5:6] = column_sum(dn1)
    sums_scr[16:32] = jnp.zeros((16, width), F32)
    for k, row in enumerate((b0, b1, b2, b3)):
        sums_scr[pl.ds(16 + lax.bitwise_xor(t_ref[0], k), 1), :] = row[...]
    for j in range(4):
        stats_ref[32 * j : 32 * (j + 1)] = sums_scr[:, j * HD : (j + 1) * HD]


def feature_input(t, cells, g1, dqkv, gains, weights, sums, share):
    count, width = g1.shape
    kept = (cells.shape[0] + 1) // 2 * 2 * share
    return call(
        feature_input_kernel, "feature_input", (1,), t,
        [(cells, row_block(cells, share))] + [(a, full(a)) for a in (g1, dqkv, gains, *weights, *sums)],
        [whole((kept, width)), whole((128, HD), F32)],
        [pltpu.VMEM((count // share, RB, width), F32), pltpu.VMEM((32, width), F32)], vmem=28, us=2
    )


def columns_home_kernel(t_ref, d_ref, p0, p1, p2, p3, out_ref):
    for k, piece in enumerate((p0, p1, p2, p3)):

        @pl.when(pl.program_id(0) == lax.bitwise_xor(t_ref[0], k))
        def _():
            out_ref[...] = piece[...]


def columns_home(t, pieces, feature_count):
    columns, rows, width = pieces[0].shape
    return call(
        columns_home_kernel, "columns_home", (4,), t, [(p, full(p)) for p in pieces],
        [(shaped((feature_count, rows, width)), pl.BlockSpec((columns, rows, width), lambda i, t, d: (i, 0, 0)))], vmem=16,
    )[0]


def rows_home_kernel(t_ref, d_ref, p0, p1, p2, p3, out_ref, scr):
    columns, rows, width = scr.shape
    share = rows // 4
    for k, piece in enumerate((p0, p1, p2, p3)):
        at = pl.multiple_of(lax.bitwise_xor(t_ref[0], k) * share, share)
        scr[:, pl.ds(at, share), :] = piece[...].astype(F32).reshape(columns, share, width)
    out_ref[...] = scr[...].astype(BF)


def rows_home(t, pieces, feature_count, rows):
    count, width = pieces[0].shape
    share = rows // 4
    columns = count // share // 5
    return call(
        rows_home_kernel, "rows_home", (5,), t,
        [(p, pl.BlockSpec((columns * share, width), lambda i, t, d: (i, 0))) for p in pieces],
        [(shaped((feature_count, rows, width)), pl.BlockSpec((columns, rows, width), lambda i, t, d: (i, 0, 0)))],
        [pltpu.VMEM((columns, rows, width), F32)], vmem=12,
    )[0]


def swap(values, axis, mask):
    count = lax.axis_size(axis)
    return lax.ppermute(values, axis, [(i, i ^ mask) for i in range(count)])


def gather_groups(own):
    far = swap(own, "tensor", 2)
    return own, swap(own, "tensor", 1), far, swap(far, "tensor", 1)


def held(values, *others):
    if isinstance(values, tuple):
        return lax.optimization_barrier((values[0], *others))[0], *values[1:]
    return lax.optimization_barrier((values, *others))[0]


def dp_masks():
    masks, mask = [], 1
    while mask < lax.axis_size("dp"):
        masks.append(mask)
        mask *= 2
    return masks


def digit(d_ref, mask):
    return lax.rem(lax.div(d_ref[0], mask), 2)


def merge_kernel(t_ref, d_ref, *refs, jobs):
    at = 0
    ins = []
    for job in jobs:
        count = len(job["parts"]) if job["parts"] else 1
        ins.append((refs[at : at + count], refs[at + count : at + 2 * count]))
        at += 2 * count
    for job, (own, other) in zip(jobs, ins):
        outs = refs[at : at + job["outs"]]
        at += job["outs"]
        kind, mask = job["next"]
        if job["join"] is not None:
            rows = own[0].shape[0]
            side = digit(d_ref, job["join"])
            for source, place in ((own[0], side), (other[0], 1 - side)):
                outs[0][pl.ds(pl.multiple_of(place * rows, rows), rows), :] = source[...].astype(outs[0].dtype)
            continue
        if job["parts"]:
            def total(group, to):
                base = 0
                for mine, got, (groups, start, rows) in zip(own, other, job["parts"]):
                    if group in groups:
                        a, b = (r.at[group] if len(r.shape) == 3 else r for r in (mine, got))
                        to[base : base + rows] = (
                            a[start : start + rows].astype(F32) + b[start : start + rows].astype(F32))
                        base += rows

            scr = refs[-1]
            for group in range(2):
                total(group, scr)
                place_sum(d_ref, scr, outs, kind, mask, group)
        elif kind == "half":
            rows = own[0].shape[-2] // 2
            for out, side in zip(outs, (digit(d_ref, mask), 1 - digit(d_ref, mask))):
                span = (Ellipsis, pl.ds(pl.multiple_of(side * rows, rows), rows), slice(None))
                out[...] = (own[0][span].astype(F32) + other[0][span].astype(F32)).astype(out.dtype)
        else:
            sums = (own[0][...].astype(F32) + other[0][...].astype(F32)).astype(outs[0].dtype)
            if kind == "group":
                outs[0][...] = sums[0]
                outs[1][...] = sums[1]
            else:
                outs[0][...] = sums


def place_sum(d_ref, scr, outs, kind, mask, group):
    if kind == "half":
        rows = outs[0].shape[1]
        for out, side in zip(outs, (digit(d_ref, mask), 1 - digit(d_ref, mask))):
            out[group] = scr[pl.ds(pl.multiple_of(side * rows, rows), rows), :].astype(BF)
    else:
        outs[group][...] = scr[0 : outs[group].shape[0], :].astype(BF)


class Chain:
    def __init__(self, own, other, parts, order):
        self.own, self.other, self.parts = tuple(own), tuple(other), parts
        dp = [m for m in order if m != "x"]
        halved = dp[:2]
        self.plan = []
        for m in order:
            self.plan.append(("group" if m == "x" else "half" if m in halved else "whole", m, None))
        self.plan += [("whole", m, m) for m in reversed(halved)]
        self.join = None
        self.ready = False

    def job(self):
        kind, mask, _ = self.plan[0]
        if self.parts:
            lead = (2,)
            rows = sum(count for groups, _, count in self.parts if 0 in groups)
            w = self.own[0].shape[-1]
        else:
            lead = self.own[0].shape[:-2]
            rows, w = self.own[0].shape[-2:]
        if self.join is not None:
            shape = (2 * rows, w)
        elif kind == "half":
            shape = lead + (rows // 2, w)
        elif kind == "group":
            shape = (rows, w)
        else:
            shape = lead + (rows, w)
        count = 2 if kind in ("half", "group") else 1
        spec = {"parts": self.parts, "next": (kind, mask), "join": self.join, "outs": count}
        scratch = [pltpu.VMEM((rows, w), F32)] if self.parts else []
        return spec, [shaped(shape)] * count, scratch

    def take(self, outs):
        kind, mask, join = self.plan.pop(0)
        self.own = (outs[0],)
        self.other = (swap(outs[-1], "tensor", 2) if mask == "x" else swap(outs[-1], "dp", mask),)
        self.join, self.parts = join, None
        self.ready = not self.plan


def merge(t, chains):
    jobs, outs, ins, scratch = [], [], [], []
    for chain in chains:
        spec, shapes, scr = chain.job()
        ins += [*chain.own, *chain.other]
        jobs.append(spec)
        outs.append(shapes)
        scratch = scratch or scr
    flat = [o for shapes in outs for o in shapes]
    results = call(
        partial(merge_kernel, jobs=jobs), "merge", (), t, [(a, VMEM) for a in ins], [(o, VMEM) for o in flat],
        scratch, vmem=16)
    at = 0
    for chain, shapes in zip(chains, outs):
        chain.take(results[at : at + len(shapes)])
        at += len(shapes)
    return results


def joined(d_ref, own, other, mask, scr):
    rows = own.shape[0]
    side = digit(d_ref, mask)
    for source, place in ((own, side), (other, 1 - side)):
        scr[pl.ds(pl.multiple_of(place * rows, rows), rows), :] = source[...].astype(F32)


def finish_kernel(t_ref, d_ref, a0, a1, b0, b1, up_ref, down_ref, qkv_ref, row_out_ref, feat_out_ref, scr_a, scr_b, tall, *, masks):
    joined(d_ref, a0, a1, masks[0], scr_a)
    joined(d_ref, b0, b1, masks[1], scr_b)
    width = up_ref.shape[0]
    half = scr_a.shape[0] - width
    up_ref[...] = scr_a[0:width]
    down_ref[...] = scr_b[0:width].T
    for at, first, count, lane in row_places(width):
        for scr, low, high in ((scr_a, 0, half), (scr_b, half, 2 * half)):
            begin, end = max(at, low), min(at + count, high)
            if begin < end:
                to = first + begin - at
                tall[to : to + end - begin, :] = scr[width + begin - low : width + end - low, lane * HD : (lane + 1) * HD]
    qkv_ref[...] = tall[0 : 3 * width]
    row_out_ref[...] = tall[3 * width : 4 * width].T
    feat_out_ref[...] = tall[4 * width : 5 * width].T


def finish(t, a, b, width):
    rows, w = a.own[0].shape
    scr = pltpu.VMEM((2 * rows, w), F32)
    outs = [shaped(s, F32) for s in ((width, w), (w, width), (3 * width, HD), (HD, width), (HD, width))]
    return call(
        partial(finish_kernel, masks=(a.join, b.join)), "finish", (), t,
        [(x, VMEM) for x in (*a.own, *a.other, *b.own, *b.other)], [(o, VMEM) for o in outs],
        [scr, scr, pltpu.VMEM((5 * width, HD), F32)], vmem=24)


def finish_feature_kernel(t_ref, d_ref, own, other, qkv_ref, sums_ref, scr, *, mask):
    joined(d_ref, own, other, mask, scr)
    rows = qkv_ref.shape[0]
    qkv_ref[...] = scr[0:rows]
    tall = sums_ref.shape[0]
    for j in range(4):
        sums_ref[:, j * HD : (j + 1) * HD] = scr[rows + j * tall : rows + (j + 1) * tall]


def finish_feature(t, chain, width, sums):
    rows, w = chain.own[0].shape
    return call(
        partial(finish_feature_kernel, mask=chain.join), "finish_feature", (), t,
        [(x, VMEM) for x in (*chain.own, *chain.other)],
        [(shaped((3 * width, w), F32), VMEM), (shaped((sums, 4 * HD), F32), VMEM)],
        [pltpu.VMEM((2 * rows, w), F32)], vmem=16)


def shards(
    table_cells, splits, feat_qkv, feat_out, feat_out_bias, row_qkv, row_out, row_out_bias,
    up_weight, up_bias, down_weight, down_bias, norm_gains, norm_biases, cotangent,
):
    shape = table_cells.shape
    _, row_count, feature_count, width = shape
    share = row_count // 4
    columns = -(-feature_count // (4 * FB)) * FB
    t = tuple(lax.axis_index(a).astype(jnp.int32).reshape(1) for a in ("tensor", "dp"))
    masks = dp_masks()
    cells = jnp.transpose(table_cells[0], (1, 0, 2))
    grads = jnp.transpose(cotangent[0], (1, 0, 2))
    fob, rob, dnb, upb = (b.reshape(1, width) for b in (feat_out_bias, row_out_bias, down_bias, up_bias))
    fq = jnp.transpose(feat_qkv, (1, 0, 2))
    rq = jnp.transpose(row_qkv, (1, 0, 2))

    own = pack(t, rq, feat_out, row_out, upb)
    own_far = swap(own, "tensor", 2)
    mixed = feature_forward(t, cells, norm_gains, norm_biases, fq, columns)
    packs = own, swap(own, "tensor", 1), own_far, swap(held(own_far, mixed[0]), "tensor", 1)
    mixed = [mixed[0]] + [swap(mixed[k], "tensor", k) for k in (1, 2, 3)]
    up_far, down_far = (swap(held(w, mixed[2], mixed[3]), "tensor", 2) for w in (up_weight, down_weight))

    first, n2, row_packed, row_p, o2, second, n3 = row_forward(
        t, splits, mixed, cells, packs, fob, rob, norm_gains, norm_biases, columns)
    ups, downs = [up_weight, swap(up_weight, "tensor", 1)], [down_weight, swap(down_weight, "tensor", 1)]
    out_a, dn3_a, hg0, hg1, bg0, bg1 = hidden_call(t, n3, grads, ups, packs[:2], downs, columns)
    ups, downs = ([far, swap(held(far, hg0), "tensor", 1)] for far in (up_far, down_far))
    fq_far = swap(held(fq, hg0), "tensor", 2)
    out_f, g2, gl2, stats_a, hg2, hg3, bg2, bg3 = hidden_call(
        t, n3, grads, ups, packs[2:], downs, columns, [out_a, dn3_a, second, dnb, norm_gains])
    dqkv_r, gl1, s0, s1, s2, s3, stats_b = row_backward(
        held(t, hg2), g2, first, row_packed, row_p, norm_gains, packs, row_count)
    pieces = [s0] + [swap(s, "tensor", k) for k, s in ((1, s1), (2, s2), (3, s3))]

    fqs = fq, swap(held(fq, s0), "tensor", 1), fq_far, swap(held(fq_far, s0), "tensor", 1)
    r1, r3 = swap(hg1, "tensor", 1), swap(hg3, "tensor", 1)
    row_keep, row_send = row_weights(t, n2, dqkv_r, gl2, o2, gl1, mixed)
    row_got = swap(row_send, "tensor", 1)
    n1, feat_packed, feat_p = feature_again(
        held(t, row_send), cells, norm_gains, norm_biases, fqs, columns, share)
    near, far = masks[:2], masks[2:]
    half = row_keep.shape[1] // 2

    def parts(first, at):
        return [((0,), first, width), ((1,), first, width), ((0, 1), at, half)]

    partials = (hg0, hg2, row_keep), (r1, r3, row_got)
    chain_a = Chain(*partials, parts(0, 0), [near[0], near[1], "x"] + far)
    chain_b = Chain(*partials, parts(width, half), [near[1], near[0], "x"] + far)
    sent = merge(held(t, feat_p), [chain_a, chain_b])
    out_pieces = gather_groups(held(out_f.reshape(columns, row_count, width), pieces[2], pieces[3]))

    g1, dqkv_f, feat_keep, feat_send = feature_backward(held(t, *sent), pieces, packs, feat_packed, feat_p, n1)
    g0, sums = feature_input(t, cells, g1, dqkv_f, norm_gains, fqs, (stats_a, stats_b, bg0, bg1, bg2, bg3), share)
    chain_f = Chain(
        (feat_keep, sums), (swap(feat_send, "tensor", 1), swap(sums, "tensor", 1)),
        [((0, 1), 0, 3 * width), ((0, 1), 0, sums.shape[0])], ["x"] + masks)

    sent = merge(held(t, sums), [chain_f])
    g0s = gather_groups(held(g0, *sent))
    step = 0
    grads_ab = None
    while True:
        if not chain_a.ready:
            sent = merge(held(t, *sent), [chain_a, chain_b])
        elif grads_ab is None:
            grads_ab = sent = finish(held(t, *sent), chain_a, chain_b, width)
        if step == 1:
            output = columns_home(held(t, *sent), out_pieces, feature_count)
            sent = (*sent, output)
        if step == 4:
            input_grad = rows_home(held(t, *sent), g0s, feature_count, row_count)
            sent = (*sent, input_grad)
        if not chain_f.ready:
            sent = merge(held(t, *sent), [chain_f])
        elif grads_ab is not None:
            break
        step += 1
    feat_grad, small = finish_feature(held(t, *sent), chain_f, width, sums.shape[0] // 4)
    up_grad, down_grad, row_grad, row_out_grad, feat_out_grad = grads_ab

    def qkv_shape(grad):
        return jnp.transpose(grad.reshape(3, width, HD), (1, 0, 2))

    home = lambda a: jnp.transpose(a, (1, 0, 2)).reshape(shape)
    return (
        home(output),
        home(input_grad),
        qkv_shape(feat_grad),
        feat_out_grad,
        small[8],
        qkv_shape(row_grad),
        row_out_grad,
        small[1],
        up_grad,
        lax.dynamic_index_in_dim(small, 16 + t[0][0], 0, keepdims=False),
        down_grad,
        small[0],
        jnp.stack([small[4], small[9], small[2]]),
        jnp.stack([small[5], small[10], small[3]]),
    )


def solution(mesh):
    return jax.shard_map(
        shards,
        mesh=mesh,
        in_specs=(
            P("dp", None, None, None), P("dp"), P(None, None, "tensor"), P("tensor", None), P(),
            P(None, None, "tensor"), P("tensor", None), P(), P(None, "tensor"), P("tensor"),
            P("tensor", None), P(), P(), P(), P("dp", None, None, None),
        ),
        out_specs=(
            P("dp", None, None, None), P("dp", None, None, None), P(None, None, "tensor"),
            P("tensor", None), P(), P(None, None, "tensor"), P("tensor", None), P(),
            P(None, "tensor"), P("tensor"), P("tensor", None), P(), P(), P(),
        ),
        check_vma=False,
    )
```

```python
from functools import partial

import jax
import jax.numpy as jnp
from jax import lax
from jax.experimental import pallas as pl
from jax.experimental.pallas import tpu as pltpu
from jax.sharding import PartitionSpec as P

HD = 128
EPSILON = 1e-05
NEGATIVE = -1e30
SCALE = HD**-0.5
BF = jnp.bfloat16
F32 = jnp.float32
MIB = 1 << 20
KNOBS = {'cost': 0, 'window': 'AM2', 'tail': 'OFpFOFOcFOgFOrF', 'out_tie': 'w', 'hs_tie': 's0', 'g_tie': 'O3', 'rb_need': 1}
FB = 8
RB = 16


def mm(a, b):
    return jnp.dot(a, b, preferred_element_type=F32)


def mm_nt(a, b):
    return lax.dot_general(a, b, (((1,), (1,)), ((), ())), preferred_element_type=F32)


def mm_tn(a, b):
    return lax.dot_general(a, b, (((0,), (0,)), ((), ())), preferred_element_type=F32)


def standardize(values):
    centered = values - jnp.mean(values, axis=-1, keepdims=True)
    inverse = lax.rsqrt(jnp.mean(centered * centered, axis=-1, keepdims=True) + EPSILON)
    return centered * inverse, inverse


def norm_backward(upstream, normed, inverse, gain):
    scaled = upstream * gain
    return inverse * (
        scaled
        - jnp.mean(scaled, axis=-1, keepdims=True)
        - normed * jnp.mean(scaled * normed, axis=-1, keepdims=True)
    )


def column_sum(values):
    return jnp.sum(values, axis=0, keepdims=True)


def softmax_keys(scores):
    grown = jnp.exp(scores - jnp.max(scores, axis=0, keepdims=True))
    return grown * (1.0 / jnp.sum(grown, axis=0, keepdims=True))


def gelu_parts(z):
    t = 1.0 / (1.0 + (0.3275911 * 0.7071067811865476) * jnp.abs(z))
    e = jnp.exp(-0.5 * z * z)
    poly = t * (
        0.127414796 + t * (-0.142248368 + t * (0.7107068705 + t * (-0.7265760135 + t * 0.5307027145)))
    )
    tail = poly * e
    cdf = jnp.where(z >= 0, 1.0 - tail, tail)
    return z * cdf, cdf + z * (e * 0.3989422804014327)


def feature_probabilities(q, k, feature_count):
    scores = mm_nt(k, q) * SCALE
    key = lax.broadcasted_iota(jnp.int32, scores.shape, 0)
    return softmax_keys(jnp.where(key < feature_count, scores, NEGATIVE)).astype(BF)


def three(w):
    return jnp.concatenate([w[0], w[1], w[2]], axis=-1)


def stacked(w):
    n = w.shape[0] // 3
    return jnp.concatenate([w[c * n : (c + 1) * n] for c in range(3)], axis=-1)


def unpacked(w):
    tall = jnp.concatenate([w[:, j * HD : (j + 1) * HD] for j in range(4)], axis=0)
    return stacked(tall)


def four_weights(fq, fq_far, near):
    tall = 3 * fq.shape[1] // 4
    packed = [(near, pl.BlockSpec((tall, 4 * HD), partial(lambda j, *_: (j, 0), j))) for j in range(2)]
    return [(fq, full(fq)), packed[0], (fq_far, full(fq_far)), packed[1]]


def wide(pieces):
    n = pieces[0].shape[0] // 4
    return jnp.concatenate(
        [jnp.concatenate([p[j * n : (j + 1) * n] for j in range(4)], axis=-1) for p in pieces], axis=0)


def live_columns(block, first, feature_count):
    values = block.astype(F32)
    index = first + lax.broadcasted_iota(jnp.int32, values.shape, 0)
    return jnp.where(index < feature_count, values, 0.0)


ANY = pl.BlockSpec(memory_space=pl.ANY)
VMEM = pl.BlockSpec(memory_space=pltpu.VMEM)


def full(a):
    zeros = (0,) * len(a.shape)
    return pl.BlockSpec(a.shape, lambda *_: zeros)


def shaped(shape, dtype=BF):
    return jax.ShapeDtypeStruct(shape, dtype)


def call(kernel, name, grid, t, ins, outs, scratch=(), vmem=32, us=1):
    t, after = t[:2], [a for a in t[2:]]
    count = 2 + len(ins)

    def body(*refs):
        kernel(*refs[:count], *refs[count + len(after) :])

    spec = pltpu.PrefetchScalarGridSpec(
        num_scalar_prefetch=2,
        grid=grid,
        in_specs=[s for _, s in ins] + [ANY] * len(after),
        out_specs=[s for _, s in outs],
        scratch_shapes=list(scratch),
    )
    return pl.pallas_call(
        body,
        grid_spec=spec,
        out_shape=[a for a, _ in outs],
        compiler_params=pltpu.CompilerParams(vmem_limit_bytes=vmem * MIB),
        cost_estimate=pl.CostEstimate(flops=us * KNOBS["cost"] * 1_000_000 + 1, bytes_accessed=1, transcendentals=0),
        name=name,
    )(*t, *[a for a, _ in ins], *after)


def pack_kernel(t_ref, d_ref, rq_ref, fo_ref, ro_ref, ub_ref, out_ref):
    width = rq_ref.shape[1]
    for c in range(3):
        out_ref[c * width : (c + 1) * width] = rq_ref[c]
    at = 3 * width
    for source in (fo_ref, ro_ref):
        for j in range(4):
            out_ref[at : at + HD] = source[:, j * HD : (j + 1) * HD]
            at += HD
    bias = [ub_ref[j * HD : (j + 1) * HD].astype(F32).reshape(1, HD) for j in range(4)]
    out_ref[at : at + 16] = jnp.concatenate(bias + [jnp.zeros((12, HD), F32)], axis=0).astype(BF)


def pack(t, rq, fo, ro, ub):
    out = shaped((3 * rq.shape[1] + 8 * HD + 16, HD))
    return call(pack_kernel, "pack", (), t, [(a, VMEM) for a in (rq, fo, ro, ub)], [(out, VMEM)], vmem=60)[0]


def pack_part(pack, what):
    rows = pack.shape[0] - 8 * HD - 16
    size, at = {"qkv": (rows, 0), "feat_out": (4 * HD, rows), "row_out": (4 * HD, rows + 4 * HD),
                "bias": (16, rows + 8 * HD)}[what]
    return pl.BlockSpec((size, HD), lambda *_: (at // size, 0))


def pack_parts(packs, what):
    return [(p, pack_part(p, what)) for p in packs]


def feature_forward_kernel(
    t_ref, d_ref, cells_ref, gains_ref, shifts_ref, w_ref, up_ref, down_ref, o0, o1, o2, o3, both_ref, qkv_scr, mix_scr
):
    feature_count, rows, width = cells_ref.shape
    padded = qkv_scr.shape[1] // rows

    @pl.when(pl.program_id(0) == 0)
    def _():
        qkv_scr[...] = jnp.zeros_like(qkv_scr)
        both_ref[: up_ref.shape[0]] = up_ref[...]
        both_ref[up_ref.shape[0] :] = down_ref[...]

    cells = cells_ref[...].astype(F32).reshape(feature_count * rows, width)
    normed, _ = standardize(cells)
    low = (normed * gains_ref[...].astype(F32)[0:1] + shifts_ref[...].astype(F32)[0:1]).astype(BF)
    qkv = mm(low, three(w_ref))
    for c in range(3):
        qkv_scr[c, 0 : feature_count * rows, :] = qkv[:, c * HD : (c + 1) * HD]
    for r in range(rows):
        every = pl.ds(r, padded, stride=rows)
        q, k, v = (qkv_scr[c, every, :].astype(BF) for c in range(3))
        mix_scr[every, :] = mm_tn(feature_probabilities(q, k, feature_count), v)
    count = o0.shape[1]
    for k, out in enumerate((o0, o1, o2, o3)):
        at = pl.multiple_of(lax.bitwise_xor(t_ref[0], k) * count, count)
        out[0] = mix_scr[pl.ds(at, count), :].astype(BF)


def feature_forward(t, cells, gains, shifts, weight, up, down, columns):
    feature_count, row_count, width = cells.shape
    padded = 4 * columns
    steps = row_count // RB
    out = (shaped((steps, columns * RB, HD)), pl.BlockSpec((1, columns * RB, HD), lambda i, t, d: (i, 0, 0)))
    return call(
        feature_forward_kernel, "feature_forward", (steps,), t,
        [(cells, pl.BlockSpec((feature_count, RB, width), lambda i, t, d: (0, i, 0)))]
        + [(a, full(a)) for a in (gains, shifts, weight, up, down)],
        [out] * 4 + [whole((up.shape[0] + down.shape[0], up.shape[1]))],
        [pltpu.VMEM((3, padded * RB, HD), F32), pltpu.VMEM((padded * RB, HD), F32)], vmem=60, us=11
    )


def column_block(array, columns):
    _, rows, width = array.shape
    return pl.BlockSpec((columns, rows, width), lambda i, t, d: (t[0], 0, 0))


def in_order(m, columns):
    steps = m.shape[0]
    halves = [m[i].reshape(columns, RB, HD) for i in range(steps)]
    return jnp.concatenate(halves, axis=1).reshape(columns * RB * steps, HD)


def row_forward_kernel(
    t_ref, d_ref, split_ref, m0, m1, m2, m3, cells_ref, f0, f1, f2, f3, r0, r1, r2, r3, w0, w1, w2, w3,
    wo_bias, wr_bias, gains_ref, shifts_ref,
    first_ref, n2_ref, qkv_ref, p_ref, o2_ref, second_ref, n3_ref, *, feature_count,
):
    columns, rows, width = cells_ref.shape
    cells = columns * rows
    side = p_ref.shape[2]
    key = lax.broadcasted_iota(jnp.int32, (side, side), 0)
    query = lax.broadcasted_iota(jnp.int32, (side, side), 1)
    same = lax.div(query, rows) == lax.div(key, rows)
    bias = jnp.where(jnp.logical_and(same, lax.rem(key, rows) < split_ref[0]), 0.0, NEGATIVE)

    gains = gains_ref[...].astype(F32)
    shifts = shifts_ref[...].astype(F32)
    stream = live_columns(cells_ref[...], t_ref[0] * columns, feature_count).reshape(cells, width)
    mixed = jnp.concatenate([in_order(m, columns) for m in (m0, m1, m2, m3)], axis=-1)
    first = stream + mm(mixed, wide((f0, f1, f2, f3))) + wo_bias[...].astype(F32)
    first_ref[...] = first
    normed, _ = standardize(first)
    low = (normed * gains[1:2] + shifts[1:2]).astype(BF)
    n2_ref[...] = low
    for h, w in enumerate((w0, w1, w2, w3)):
        base = 3 * HD * h
        qkv_ref[:, base : base + 3 * HD] = mm(low, stacked(w)).astype(BF)
        for b in range(0, cells, side):
            span = slice(b, b + side)
            q, k, v = (qkv_ref[span, base + c * HD : base + (c + 1) * HD] for c in range(3))
            p = softmax_keys(mm_nt(k, q) * SCALE + bias).astype(BF)
            p_ref[h, b // side] = p
            o2_ref[span, h * HD : (h + 1) * HD] = mm_tn(p, v).astype(BF)
    second = first + mm(o2_ref[...], wide((r0, r1, r2, r3))) + wr_bias[...].astype(F32)
    second_ref[...] = second
    normed, _ = standardize(second)
    n3_ref[...] = (normed * gains[2:3] + shifts[2:3]).astype(BF)


def whole(shape, dtype=BF):
    return shaped(shape, dtype), full(shaped(shape, dtype))


def row_forward(t, split, mixed, cells, packs, wo_bias, wr_bias, gains, shifts, columns):
    feature_count, rows, width = cells.shape
    n = columns * rows
    side = 4 * rows
    ins = [(split, pl.BlockSpec(memory_space=pltpu.SMEM))] + [(m, full(m)) for m in mixed]
    ins += [(cells, column_block(cells, columns))]
    ins += pack_parts(packs, "feat_out") + pack_parts(packs, "row_out") + pack_parts(packs, "qkv")
    ins += [(a, full(a)) for a in (wo_bias, wr_bias, gains, shifts)]
    return call(
        partial(row_forward_kernel, feature_count=feature_count), "row_forward", (1,), t, ins,
        [whole((n, width), F32), whole((n, width)), whole((n, 12 * HD)), whole((4, n // side, side, side)),
         whole((n, 4 * HD)), whole((n, width), F32), whole((n, width))], us=9
    )


def hidden_pair(t_ref, n3_ref, grad_ref, ups, packs, downs, grads, bias_grads, feature_count):
    columns, rows, width = grad_ref.shape
    g3 = live_columns(grad_ref[...], t_ref[0] * columns, feature_count).reshape(columns * rows, width)
    n3, gl = n3_ref[...], g3.astype(BF)
    n3_t, gl_t = n3.T, gl.T
    ms, dzs = [], []
    for up, pack, down, grad_ref, bias_grad in zip(ups, packs, downs, grads, bias_grads):
        bias = jnp.concatenate([pack[...].astype(F32)[j : j + 1] for j in range(4)], axis=-1)
        act, slope = gelu_parts(mm(n3, up[...]) + bias)
        m = act.astype(BF)
        dz = (mm_nt(gl, down[...]) * slope).astype(BF)
        grad_ref[:width] = mm(n3_t, dz).astype(BF)
        grad_ref[width:] = mm(gl_t, m).astype(BF)
        bias_grad[...] = column_sum(dz.astype(F32))
        ms.append(m)
        dzs.append(dz)
    out = mm(jnp.concatenate(ms, axis=-1), jnp.concatenate([d[...] for d in downs], axis=0))
    dn3 = mm_nt(jnp.concatenate(dzs, axis=-1), jnp.concatenate([u[...] for u in ups], axis=-1))
    return g3, out, dn3


def hidden_first_kernel(
    t_ref, d_ref, n3_ref, grad_ref, up0, up1, b0, b1, down0, down1, out_ref, dn3_ref, wg0, wg1, bg0, bg1,
    *, feature_count,
):
    _, out, dn3 = hidden_pair(
        t_ref, n3_ref, grad_ref, (up0, up1), (b0, b1), (down0, down1), (wg0, wg1), (bg0, bg1), feature_count)
    out_ref[...] = out
    dn3_ref[...] = dn3


def hidden_second_kernel(
    t_ref, d_ref, n3_ref, grad_ref, up0, up1, b0, b1, down0, down1, out_in, dn3_in, second_ref, down_bias, gains_ref,
    earlier_ref, out_ref, g2_ref, stats_ref, wg0, sent_ref, bg0, bg1, *, feature_count,
):
    tall = earlier_ref.shape[0]
    sent_ref[:tall] = earlier_ref[...]
    g3, out, dn3 = hidden_pair(
        t_ref, n3_ref, grad_ref, (up0, up1), (b0, b1), (down0, down1), (wg0, sent_ref.at[pl.ds(tall, tall)]), (bg0, bg1),
        feature_count)
    second = second_ref[...]
    out_ref[...] = (second + out_in[...] + out + down_bias[...].astype(F32)).astype(BF)
    dn3 = dn3_in[...] + dn3
    normed, inverse = standardize(second)
    g2 = g3 + norm_backward(dn3, normed, inverse, gains_ref[...].astype(F32)[2:3])
    g2_ref[...] = g2
    stats_ref[...] = rows_of([g3, g2, dn3 * normed, dn3])


def rows_of(arrays):
    return jnp.concatenate(
        [column_sum(a) for a in arrays] + [jnp.zeros((8 - len(arrays), arrays[0].shape[1]), F32)], axis=0)


def hidden_call(t, n3, grads, both, packs, columns, extra=None):
    n, width = n3.shape
    hidden = both[0].shape[1]
    ins = [(n3, full(n3)), (grads, column_block(grads, columns))]
    ins += [(a, pl.BlockSpec((width, hidden), lambda *_: (0, 0))) for a in both] + pack_parts(packs, "bias")
    ins += [(a, pl.BlockSpec((hidden, width), lambda *_: (1, 0))) for a in both]
    bias_grads = [whole((1, hidden), F32)] * 2
    if extra is None:
        kernel, name = hidden_first_kernel, "hidden_first"
        results = [whole((n, width), F32)] * 2 + [whole((2 * width, hidden))] * 2 + bias_grads
    else:
        kernel, name = hidden_second_kernel, "hidden_second"
        ins += [(a, full(a)) for a in extra]
        results = [whole((n, width)), whole((n, width), F32), whole((8, width), F32)]
        results += [whole((2 * width, hidden)), whole((4 * width, hidden))] + bias_grads
    return call(partial(kernel, feature_count=grads.shape[0]), name, (1,), t, ins, results, us=7)


def attention_backward(q, k, v, p, do):
    dp = mm_nt(v, do)
    pf = p.astype(F32)
    ds = (pf * (dp - jnp.sum(dp * pf, axis=0, keepdims=True))).astype(BF)
    return mm_tn(ds, k) * SCALE, mm(ds, q) * SCALE, mm(p, do)


def row_backward_kernel(
    t_ref, d_ref, g2_ref, first_ref, qkv_ref, p_ref, gains_ref, n2_ref, o2_ref, m0, m1, m2, m3, fq0, fq2,
    w0, w1, w2, w3, r0, r1, r2, r3, s0, near_ref, s2, s3, stats_ref, keep_ref, send_ref, g1_scr, dqkv_ref,
):
    width = fq0.shape[1]
    for j, weights in enumerate((fq0, fq2)):
        tall = 3 * width // 4
        for lane in range(4):
            for at, first, count in stretches(lane * tall, tall, width):
                near_ref[j * tall + at : j * tall + at + count, lane * HD : (lane + 1) * HD] = (
                    weights[first // width, first % width : first % width + count, :])
    g2 = g2_ref[...]
    cells, width = g2.shape
    side = p_ref.shape[2]
    gl2 = g2.astype(BF)
    do = mm_nt(gl2, wide((r0, r1, r2, r3))).astype(BF)
    for h in range(4):
        at = 3 * HD * h
        for b in range(0, cells, side):
            span = slice(b, b + side)
            q, k, v = (qkv_ref[span, at + c * HD : at + (c + 1) * HD] for c in range(3))
            parts = attention_backward(q, k, v, p_ref[h, b // side], do[span, HD * h : HD * (h + 1)])
            for c, part in enumerate(parts):
                dqkv_ref[span, at + c * HD : at + (c + 1) * HD] = part.astype(BF)
    dn2 = mm_nt(dqkv_ref[...], jnp.concatenate([stacked(w) for w in (w0, w1, w2, w3)], axis=-1))
    normed, inverse = standardize(first_ref[...])
    g1 = g2 + norm_backward(dn2, normed, inverse, gains_ref[...].astype(F32)[1:2])
    columns, rows, _ = g1_scr.shape
    g1_scr[...] = g1.reshape(columns, rows, width)
    share = rows // 4
    for k, out in enumerate((s0, near_ref.at[pl.ds(6 * width // 4, columns * share)], s2, s3)):
        at = pl.multiple_of(lax.bitwise_xor(t_ref[0], k) * share, share)
        out[...] = g1_scr[:, pl.ds(at, share), :].reshape(columns * share, width).astype(BF)
    stats_ref[...] = rows_of([g1, dn2 * normed, dn2])
    mixed = [in_order(m, columns) for m in (m0, m1, m2, m3)]
    row_grads(n2_ref[...], dqkv_ref[...], gl2, o2_ref[...], g1.astype(BF), mixed, keep_ref, send_ref)


def stretches(first, count, size):
    at = 0
    while at < count:
        rows = min(count - at, size - (first + at) % size)
        yield at, first + at, rows
        at += rows


def row_grads(n2, dqkv, gl2, o2, gl1, mixed, keep_ref, send_ref):
    width = n2.shape[1]
    grad = mm(n2.T, dqkv).astype(BF)
    out_grad = mm(gl2.T, o2).astype(BF)
    feat_grad = mm(gl1.T, jnp.concatenate(mixed, axis=-1)).astype(BF)
    for h in range(4):
        out = (keep_ref, send_ref)[h % 2].at[h // 2]
        blocks = [grad[:, (3 * h + c) * HD : (3 * h + c + 1) * HD] for c in range(3)]
        blocks += [out_grad[:, HD * h : HD * (h + 1)], feat_grad[:, HD * h : HD * (h + 1)]]
        for at, first, count, lane in row_places(width):
            out[at : at + count, lane * HD : (lane + 1) * HD] = blocks[first // width][first % width : first % width + count]


def row_backward(t, g2, first, qkv, p, gains, n2, o2, mixed, fq, fq_far, packs, rows):
    n, width = g2.shape
    ins = [(a, full(a)) for a in (g2, first, qkv, p, gains, n2, o2, *mixed, fq, fq_far)]
    ins += pack_parts(packs, "qkv") + pack_parts(packs, "row_out")
    piece = whole((n // 4, width))
    return call(
        row_backward_kernel, "row_backward", (1,), t, ins,
        [piece, whole((6 * width // 4 + n // 4, width)), piece, piece, whole((8, width), F32)]
        + [whole((2, 5 * width // 4, 4 * HD))] * 2,
        [pltpu.VMEM((n // rows, rows, width), F32), pltpu.VMEM(qkv.shape, BF)], us=11,
    )


def row_places(width):
    tall = 5 * width // 4
    first = 0
    while first < 5 * width:
        count = min(width - first % width, tall - first % tall)
        yield first % tall, first, count, first // tall
        first += count


def own_rows(t_ref, cells_ref, cell_scr, share):
    feature_count, block_rows, width = cells_ref.shape
    cell_scr[0:feature_count] = cells_ref[...].astype(F32)
    cell_scr[feature_count:] = jnp.zeros_like(cell_scr[feature_count:])
    at = pl.multiple_of(lax.rem(t_ref[0], block_rows // share) * share, share)
    return cell_scr[:, pl.ds(at, share), :].reshape(cell_scr.shape[0] * share, width)


def row_block(cells, share):
    feature_count, _, width = cells.shape
    per = RB // share
    return pl.BlockSpec((feature_count, RB, width), lambda i, t, d: (0, lax.div(t[0], per), 0))


def feature_again_kernel(
    t_ref, d_ref, cells_ref, gains_ref, shifts_ref, w0, w1, w2, w3, n1_ref, qkv_ref, p_ref, cell_scr, qkv_scr
):
    feature_count = cells_ref.shape[0]
    share, padded, _ = qkv_ref.shape
    normed, _ = standardize(own_rows(t_ref, cells_ref, cell_scr, share))
    low = (normed * gains_ref[...].astype(F32)[0:1] + shifts_ref[...].astype(F32)[0:1]).astype(BF)
    n1_ref[...] = low
    for h, w in enumerate((three(w0), unpacked(w1), three(w2), unpacked(w3))):
        packed = mm(low, w)
        for c in range(3):
            qkv_scr[c] = packed[:, c * HD : (c + 1) * HD]
        for r in range(share):
            q, k, v = (qkv_scr[c, pl.ds(r, padded, stride=share), :].astype(BF) for c in range(3))
            for c, part in enumerate((q, k, v)):
                qkv_ref[r, :, (3 * h + c) * HD : (3 * h + c + 1) * HD] = part
            p_ref[r, h] = feature_probabilities(q, k, feature_count)


def feature_again(t, cells, gains, shifts, fq, fq_far, near, columns, share):
    width = cells.shape[2]
    padded = 4 * columns
    return call(
        feature_again_kernel, "feature_again", (1,), t,
        [(cells, row_block(cells, share))] + [(a, full(a)) for a in (gains, shifts)] + four_weights(fq, fq_far, near),
        [whole((padded * share, width)), whole((share, padded, 12 * HD)), whole((share, 4, padded, padded))],
        [pltpu.VMEM((padded, RB, width), F32), pltpu.VMEM((3, padded * share, HD), F32)], vmem=28, us=4
    )


def feature_backward_kernel(
    t_ref, d_ref, r0, r1, r2, r3, f0, f1, f2, f3, qkv_ref, p_ref, n1_ref,
    g1_ref, dqkv_ref, keep0, keep1, send0, send1, low_scr, do_scr, dqkv_scr,
):
    width = g1_ref.shape[1]
    share, padded, _ = qkv_ref.shape
    for k, piece in enumerate((r0, r1, r2, r3)):
        count = piece.shape[0]
        at = pl.multiple_of(lax.bitwise_xor(t_ref[0], k) * count, count)
        low_scr[pl.ds(at, count), :] = piece[...]
        g1_ref[pl.ds(at, count), :] = piece[...].astype(F32)
    do = mm_nt(low_scr[...], wide((f0, f1, f2, f3)))
    for h in range(4):
        do_scr[h] = do[:, h * HD : (h + 1) * HD]
    n1_t = n1_ref[...].T
    for h in range(4):
        for r in range(share):
            every = pl.ds(r, padded, stride=share)
            q, k, v = (qkv_ref[r, :, (3 * h + c) * HD : (3 * h + c + 1) * HD] for c in range(3))
            parts = attention_backward(q, k, v, p_ref[r, h], do_scr[h, every, :].astype(BF))
            for c, part in enumerate(parts):
                dqkv_scr[3 * h + c, every, :] = part
        out = ((keep0, keep1), (send0, send1))[h % 2]
        for c in range(3):
            dqkv_ref[:, (3 * h + c) * HD : (3 * h + c + 1) * HD] = dqkv_scr[3 * h + c].astype(BF)
        grad = mm(n1_t, dqkv_ref[:, 3 * HD * h : 3 * HD * (h + 1)]).astype(BF)
        for c in range(3):
            out[h // 2][c * width : (c + 1) * width, :] = grad[:, c * HD : (c + 1) * HD]


def feature_backward(t, pieces, packs, qkv, p, n1):
    share, _, padded, _ = p.shape
    width = pieces[0].shape[1]
    cells = share * padded
    return call(
        feature_backward_kernel, "feature_backward", (1,), t,
        [(a, pl.BlockSpec(pieces[0].shape, partial(lambda j, *_: (j, 0), 0 if k != 1 else a.shape[0] // pieces[0].shape[0] - 1)))
         for k, a in enumerate(pieces)] + pack_parts(packs, "feat_out") + [(a, full(a)) for a in (qkv, p, n1)],
        [whole((cells, width), F32), whole((cells, 12 * HD))] + [whole((3 * width, HD))] * 4,
        [pltpu.VMEM((cells, width), BF), pltpu.VMEM((4, cells, HD), F32), pltpu.VMEM((12, cells, HD), F32)], us=11
    )


def feature_input_kernel(
    t_ref, d_ref, cells_ref, g1_ref, dqkv_ref, gains_ref, w0, w1, w2, w3, stats_a, stats_b, b0, b1, b2, b3,
    out_ref, stats_ref, cell_scr, sums_scr,
):
    cells, width = g1_ref.shape
    share = cells // cell_scr.shape[0]
    normed, inverse = standardize(own_rows(t_ref, cells_ref, cell_scr, share))
    dn1 = mm_nt(dqkv_ref[...], jnp.concatenate([three(w0), unpacked(w1), three(w2), unpacked(w3)], axis=-1))
    g0 = g1_ref[...] + norm_backward(dn1, normed, inverse, gains_ref[...].astype(F32)[0:1])
    out_ref[...] = g0[: out_ref.shape[0]].astype(BF)
    sums_scr[0:8] = stats_a[...]
    sums_scr[8:16] = stats_b[...]
    sums_scr[4:5] = column_sum(dn1 * normed)
    sums_scr[5:6] = column_sum(dn1)
    sums_scr[16:32] = jnp.zeros((16, width), F32)
    for k, row in enumerate((b0, b1, b2, b3)):
        sums_scr[pl.ds(16 + lax.bitwise_xor(t_ref[0], k), 1), :] = row[...]
    for j in range(4):
        stats_ref[32 * j : 32 * (j + 1)] = sums_scr[:, j * HD : (j + 1) * HD]


def feature_input(t, cells, g1, dqkv, gains, fq, fq_far, near, sums, share):
    count, width = g1.shape
    kept = (cells.shape[0] + 1) // 2 * 2 * share
    ins = [(cells, row_block(cells, share))] + [(a, full(a)) for a in (g1, dqkv, gains)]
    ins += four_weights(fq, fq_far, near) + [(a, full(a)) for a in sums]
    return call(
        feature_input_kernel, "feature_input", (1,), t, ins, [whole((kept, width)), whole((128, HD), F32)],
        [pltpu.VMEM((count // share, RB, width), F32), pltpu.VMEM((32, width), F32)], vmem=28, us=2,
    )


def pair_kernel(t_ref, d_ref, own, far, out_ref):
    out_ref[: own.shape[0]] = own[...]
    out_ref[own.shape[0] :] = far[...]


def pair(t, own, far):
    return call(pair_kernel, "pair", (), t, [(own, VMEM), (far, VMEM)], [(shaped((2 * own.shape[0], own.shape[1])), VMEM)], vmem=12)[0]


def columns_home_kernel(t_ref, d_ref, p0, p1, p2, p3, out_ref):
    for k, piece in enumerate((p0, p1, p2, p3)):

        @pl.when(pl.program_id(0) == lax.bitwise_xor(t_ref[0], k))
        def _():
            out_ref[...] = piece[...].reshape(out_ref.shape)


def columns_home(t, own, far, near, feature_count, rows):
    count, width = own.shape
    columns = count // rows
    block = lambda i: pl.BlockSpec((count, width), lambda *_: (i, 0))
    return call(
        columns_home_kernel, "columns_home", (4,), t,
        [(own, block(0)), (near, block(0)), (far, block(0)), (near, block(1))],
        [(shaped((feature_count, rows, width)), pl.BlockSpec((columns, rows, width), lambda i, t, d: (i, 0, 0)))], vmem=16,
    )[0]


def rows_home_kernel(t_ref, d_ref, p0, p1, p2, p3, out_ref, scr):
    columns, rows, width = scr.shape
    share = rows // 4
    for k, piece in enumerate((p0, p1, p2, p3)):
        at = pl.multiple_of(lax.bitwise_xor(t_ref[0], k) * share, share)
        scr[:, pl.ds(at, share), :] = piece[...].astype(F32).reshape(columns, share, width)
    out_ref[...] = scr[...].astype(BF)


def rows_home(t, own, far, near, feature_count, rows):
    count, width = own.shape
    share = rows // 4
    steps = 5
    columns = count // share // steps
    block = lambda first: pl.BlockSpec((columns * share, width), lambda i, t, d: (first + i, 0))
    return call(
        rows_home_kernel, "rows_home", (steps,), t,
        [(own, block(0)), (near, block(0)), (far, block(0)), (near, block(steps))],
        [(shaped((feature_count, rows, width)), pl.BlockSpec((columns, rows, width), lambda i, t, d: (i, 0, 0)))],
        [pltpu.VMEM((columns, rows, width), F32)], vmem=16,
    )[0]


def swap(values, axis, mask):
    count = lax.axis_size(axis)
    return lax.ppermute(values, axis, [(i, i ^ mask) for i in range(count)])


def gather_groups(own):
    far = swap(own, "tensor", 2)
    return own, swap(own, "tensor", 1), far, swap(far, "tensor", 1)


class Box:
    def __init__(self, value):
        self.value = value


def tied(values, *boxes):
    many = isinstance(values, tuple)
    values = values if many else (values,)
    out = lax.optimization_barrier((*values, *[b.value for b in boxes]))
    for box, value in zip(boxes, out[len(values) :]):
        box.value = value
    return out[: len(values)] if many else out[0]


def dp_masks():
    masks, mask = [], 1
    while mask < lax.axis_size("dp"):
        masks.append(mask)
        mask *= 2
    return masks


def digit(d_ref, mask):
    return lax.rem(lax.div(d_ref[0], mask), 2)


def halves(d_ref, mask, rows):
    side = digit(d_ref, mask)
    return [pl.multiple_of(s * rows, rows) for s in (side, 1 - side)]


def added(a, b):
    return a.astype(F32) + b.astype(F32)


def merge(name, kernel, t, ins, outs, scratch=(), vmem=16):
    return call(kernel, name, (), t, [(a, VMEM) for a in ins], [(shaped(o), VMEM) for o in outs], scratch, vmem=vmem)


def first_halves(t, hg0, hg2, row_keep, got, row_got, masks):
    hidden = hg0.shape[0] // 2
    half = row_keep.shape[1] // 2
    rows, width = hidden + half, hg0.shape[1]

    def kernel(t_ref, d_ref, g0, g2, keep, r, row_r, ak, as_, bk, bs, scr):
        for group, mine in enumerate((g0, g2)):
            for which, (kept, sent, mask) in enumerate(((ak, as_, masks[0]), (bk, bs, masks[1]))):
                at = which * hidden
                scr[:hidden] = added(mine[at : at + hidden], r[2 * hidden * group + at : 2 * hidden * group + at + hidden])
                at = which * half
                scr[hidden:] = added(keep[group, at : at + half], row_r[group, at : at + half])
                for out, first in zip((kept, sent), halves(d_ref, mask, rows // 2)):
                    out[group] = scr[pl.ds(first, rows // 2), :].astype(BF)

    return merge("ab_first", kernel, t, (hg0, hg2, row_keep, got, row_got), [(2, rows // 2, width)] * 4,
                 [pltpu.VMEM((rows, width), F32)], vmem=20)


def second_halves(t, a, ar, b, br, masks):
    _, rows, width = a.shape

    def kernel(t_ref, d_ref, a, ar, b, br, ak, as_, bk, bs):
        for x, y, kept, sent, mask in ((a, ar, ak, as_, masks[1]), (b, br, bk, bs, masks[0])):
            for out, first in zip((kept, sent), halves(d_ref, mask, rows // 2)):
                span = (slice(None), pl.ds(first, rows // 2), slice(None))
                out[...] = added(x[span], y[span]).astype(BF)

    return merge("ab_second", kernel, t, (a, ar, b, br), [(2, rows // 2, width)] * 4)


def groups_apart(t, a, ar, b, br):
    _, rows, width = a.shape

    def kernel(t_ref, d_ref, a, ar, b, br, kept, sent):
        for group, out in enumerate((kept, sent)):
            out[:rows] = added(a[group], ar[group]).astype(BF)
            out[rows:] = added(b[group], br[group]).astype(BF)

    return merge("ab_groups", kernel, t, (a, ar, b, br), [(2 * rows, width)] * 2)


def sums(t, k, r):
    def kernel(t_ref, d_ref, k, r, out):
        out[...] = added(k[...], r[...]).astype(BF)

    return merge("sums", kernel, t, (k, r), [k.shape])


def sums_apart(t, k, r):
    rows, width = k.shape[0] // 2, k.shape[1]

    def kernel(t_ref, d_ref, k, r, a, b):
        a[...] = added(k[:rows], r[:rows]).astype(BF)
        b[...] = added(k[rows:], r[rows:]).astype(BF)

    return merge("ab_apart", kernel, t, (k, r), [(rows, width)] * 2)


def joins(t, pairs, masks):
    def kernel(t_ref, d_ref, *refs):
        for j, mask in enumerate(masks):
            own, other, out = refs[2 * j], refs[2 * j + 1], refs[2 * len(masks) + j]
            for source, first in zip((own, other), halves(d_ref, mask, own.shape[0])):
                out[pl.ds(first, own.shape[0]), :] = source[...]

    return merge("joins", kernel, t, [a for p in pairs for a in p], [(2 * p[0].shape[0], p[0].shape[1]) for p in pairs])


def feature_groups(t, own, got, mine, theirs):
    rows, width = own[0].shape
    more = mine.shape[0]

    def kernel(t_ref, d_ref, a0, a2, b0, b2, sa, sb, kept, sent):
        small = added(sa[...], sb[...]).astype(BF)
        for out, a, b in ((kept, a0, b0), (sent, a2, b2)):
            out[:rows] = added(a[...], b[...]).astype(BF)
            out[rows:] = small

    return merge("f_groups", kernel, t, (*own, *got, mine, theirs), [(rows + more, width)] * 2)


def half_sums(t, k, r, mask):
    rows, width = k.shape[0] // 2, k.shape[1]

    def kernel(t_ref, d_ref, k, r, kept, sent):
        for out, first in zip((kept, sent), halves(d_ref, mask, rows)):
            span = (pl.ds(first, rows), slice(None))
            out[...] = added(k[span], r[span]).astype(BF)

    return merge("f_half", kernel, t, (k, r), [(rows, width)] * 2)


def joined(d_ref, own, other, mask, scr):
    rows = own.shape[0]
    side = digit(d_ref, mask)
    for source, place in ((own, side), (other, 1 - side)):
        scr[pl.ds(pl.multiple_of(place * rows, rows), rows), :] = source[...].astype(F32)


def finish_kernel(t_ref, d_ref, a0, a1, b0, b1, up_ref, down_ref, qkv_ref, row_out_ref, feat_out_ref, scr_a, scr_b, tall, *, masks):
    joined(d_ref, a0, a1, masks[0], scr_a)
    joined(d_ref, b0, b1, masks[1], scr_b)
    width = up_ref.shape[0]
    half = scr_a.shape[0] - width
    up_ref[...] = scr_a[0:width]
    down_ref[...] = scr_b[0:width].T
    for at, first, count, lane in row_places(width):
        for scr, low, high in ((scr_a, 0, half), (scr_b, half, 2 * half)):
            begin, end = max(at, low), min(at + count, high)
            if begin < end:
                to = first + begin - at
                tall[to : to + end - begin, :] = scr[width + begin - low : width + end - low, lane * HD : (lane + 1) * HD]
    qkv_ref[...] = tall[0 : 3 * width]
    row_out_ref[...] = tall[3 * width : 4 * width].T
    feat_out_ref[...] = tall[4 * width : 5 * width].T


def finish(t, a, b, masks, width):
    rows, w = a[0].shape
    scr = pltpu.VMEM((2 * rows, w), F32)
    outs = [shaped(s, F32) for s in ((width, w), (w, width), (3 * width, HD), (HD, width), (HD, width))]
    return call(
        partial(finish_kernel, masks=masks), "finish", (), t,
        [(x, VMEM) for x in (*a, *b)], [(o, VMEM) for o in outs],
        [scr, scr, pltpu.VMEM((5 * width, HD), F32)], vmem=24)


def finish_feature_kernel(t_ref, d_ref, own, other, qkv_ref, sums_ref, scr, *, mask):
    joined(d_ref, own, other, mask, scr)
    rows = qkv_ref.shape[0]
    qkv_ref[...] = scr[0:rows]
    tall = sums_ref.shape[0]
    for j in range(4):
        sums_ref[:, j * HD : (j + 1) * HD] = scr[rows + j * tall : rows + (j + 1) * tall]


def finish_feature(t, own, other, mask, width, small):
    rows, w = own.shape
    return call(
        partial(finish_feature_kernel, mask=mask), "finish_feature", (), t, [(own, VMEM), (other, VMEM)],
        [(shaped((3 * width, w), F32), VMEM), (shaped((small, 4 * HD), F32), VMEM)],
        [pltpu.VMEM((2 * rows, w), F32)], vmem=16)


def shards(
    table_cells, splits, feat_qkv, feat_out, feat_out_bias, row_qkv, row_out, row_out_bias,
    up_weight, up_bias, down_weight, down_bias, norm_gains, norm_biases, cotangent,
):
    shape = table_cells.shape
    _, row_count, feature_count, width = shape
    share = row_count // 4
    columns = -(-feature_count // (4 * FB)) * FB
    t = tuple(lax.axis_index(a).astype(jnp.int32).reshape(1) for a in ("tensor", "dp"))
    masks = dp_masks()
    cells = jnp.transpose(table_cells[0], (1, 0, 2))
    grads = jnp.transpose(cotangent[0], (1, 0, 2))
    fob, rob, dnb = (b.reshape(1, width) for b in (feat_out_bias, row_out_bias, down_bias))
    fq = jnp.transpose(feat_qkv, (1, 0, 2))
    rq = jnp.transpose(row_qkv, (1, 0, 2))

    near, far = masks[:2], masks[2:]
    over = lambda v, mask: swap(v, "tensor", 2) if mask == "x" else swap(v, "dp", mask)
    core = lambda v: swap(v, "tensor", 1)

    own = pack(t, rq, feat_out, row_out, up_bias)
    own_far = swap(own, "tensor", 2)
    *mixed, both = feature_forward(t, cells, norm_gains, norm_biases, fq, up_weight, down_weight, columns)
    kept = Box(mixed[0])
    own_far = tied(own_far, kept)
    packs = own, core(own), own_far, core(own_far)
    mixed = [kept.value] + [swap(mixed[k], "tensor", k) for k in (1, 2, 3)]
    a2, a3 = Box(mixed[2]), Box(mixed[3])
    both_far = swap(tied(both, a2, a3), "tensor", 2)
    mixed[2:] = a2.value, a3.value

    first, n2, row_packed, row_p, o2, second, n3 = row_forward(
        t, splits, mixed, cells, packs, fob, rob, norm_gains, norm_biases, columns)
    out_a, dn3_a, hg0, hg1, bg0, bg1 = hidden_call(t, n3, grads, (both, core(both)), packs[:2], columns)
    kept, fq_kept = Box(out_a), Box(hg0)
    both_far = tied(both_far, kept)
    fq_far = swap(tied(fq, fq_kept), "tensor", 2)
    hg0 = fq_kept.value
    out_f, g2, stats_a, hg2, hidden_send, bg2, bg3 = hidden_call(
        t, n3, grads, (both_far, core(both_far)), packs[2:], columns,
        [kept.value, dn3_a, second, dnb, norm_gains, hg1])
    s0, near_send, s2, s3, stats_b, row_keep, row_send = row_backward(
        (*t, out_f), g2, first, row_packed, row_p, norm_gains, n2, o2, mixed, fq, fq_far, packs, row_count)
    pieces = [s0, core(near_send), swap(s2, "tensor", 2), swap(s3, "tensor", 3)]
    near_got = pieces[1]
    K = KNOBS
    boxes = {"s0": Box(s0), "rs": Box(row_send)}
    hidden_got = core(tied(hidden_send, boxes[K["hs_tie"]]) if K["hs_tie"] else hidden_send)
    pieces[0] = boxes["s0"].value
    row_got = core(boxes["rs"].value)

    last = [s0]
    boxes.update(out=Box(out_f), w=Box(pieces[3]), w2=Box(pieces[2]))
    out_far = None
    if K["out_tie"] == "s0":
        out_far = swap(tied(out_f, boxes["s0"]), "tensor", 2)
        pieces[0] = boxes["s0"].value
    if K["out_tie"] == "hs":
        out_far = swap(out_f, "tensor", 2)
    for what in K["window"]:
        if what == "A":
            n1, feat_packed, feat_p = feature_again(
                (*t, *last), cells, norm_gains, norm_biases, fq, fq_far, near_got, columns, share)
            last = [feat_p]
        elif what == "M":
            ak, a_sent, bk, b_sent = first_halves((*t, *last), hg0, hg2, row_keep, hidden_got, row_got, near)
            last = [ak]
            ar, br = over(a_sent, near[0]), over(b_sent, near[1])
        else:
            last = [*last, pieces[2], pieces[3]]
    if K["out_tie"] == "w":
        out_far = swap(tied(out_f, boxes["w"], boxes["w2"]), "tensor", 2)
        pieces[2:] = boxes["w2"].value, boxes["w"].value

    g1, dqkv_f, f0, f2, f1, f3 = feature_backward((*t, *last), pieces, packs, feat_packed, feat_p, n1)
    g0, small = feature_input(
        t, cells, g1, dqkv_f, norm_gains, fq, fq_far, near_got, (stats_a, stats_b, bg0, bg1, bg2, bg3), share)
    f_got = core(f1), core(f3)
    small_got = core(small)
    last = [small]

    state = {"O": 0, "F": 0}
    grads_other = feat_grad = None

    def step_other(last):
        nonlocal ak, ar, bk, br, ab, abr, grads_other
        here = state["O"]
        tt = (*t, *last)
        if here == 0:
            ak, a_sent, bk, b_sent = out = second_halves(tt, ak, ar, bk, br, near)
            ar, br = over(a_sent, near[1]), over(b_sent, near[0])
        elif here == 1:
            ab, sent = out = groups_apart(tt, ak, ar, bk, br)
            abr = over(sent, "x")
        elif here < 2 + len(far):
            ab, = out = sums(tt, ab, abr)
            abr = over(ab, far[here - 2])
        elif here == 2 + len(far):
            ak, bk = out = sums_apart(tt, ab, abr)
            ar, br = over(ak, near[1]), over(bk, near[0])
        elif here == 3 + len(far):
            ak, bk = out = joins(tt, ((ak, ar), (bk, br)), (near[1], near[0]))
            ar, br = over(ak, near[0]), over(bk, near[1])
        else:
            grads_other = out = finish(tt, (ak, ar), (bk, br), near, width)
        state["O"] += 1
        return out[:1]

    def step_feature(last):
        nonlocal fk, fr, feat_grad, small_sums
        here = state["F"]
        tt = (*t, *last)
        if here == 0:
            fk, sent = out = feature_groups(tt, (f0, f2), f_got, small, small_got)
            fr = over(sent, "x")
        elif here < 3:
            fk, sent = out = half_sums(tt, fk, fr, near[here - 1])
            fr = over(sent, near[here - 1])
        elif here < 3 + len(far):
            fk, = out = sums(tt, fk, fr)
            fr = over(fk, far[here - 3])
        elif here == 3 + len(far):
            fk, = out = sums(tt, fk, fr)
            fr = over(fk, near[1])
        elif here == 4 + len(far):
            fk, = out = joins(tt, ((fk, fr),), (near[1],))
            fr = over(fk, near[0])
        else:
            feat_grad, small_sums = out = finish_feature(tt, fk, fr, near[0], width, small.shape[0] // 4)
        state["F"] += 1
        return out[:1]

    ab = abr = fk = fr = small_sums = g0_far = None
    steps = list(K["tail"])
    while steps or grads_other is None or feat_grad is None:
        what = steps.pop(0) if steps else ("O" if grads_other is None else "F")
        if what == "O" and grads_other is None:
            last = step_other(last)
        elif what == "F" and feat_grad is None:
            last = step_feature(last)
        elif what == "p":
            out_pair = pair((*t, *last), out_f, out_far)
            out_near = core(out_pair)
            last = [out_pair]
        elif what == "c":
            output = columns_home((*t, *last), out_f, out_far, out_near, feature_count, row_count)
            last = [output]
        elif what == "g":
            g0_pair = pair((*t, *last), g0, g0_far)
            g0_near = core(g0_pair)
            last = [g0_pair]
        elif what == "r":
            input_grad = rows_home((*t, *last), g0, g0_far, g0_near, feature_count, row_count)
            last = [input_grad]
        key = what + str(state.get(what, ""))
        if g0_far is None and key == K["g_tie"]:
            box = Box(last[0])
            g0_far = swap(tied(g0, box), "tensor", 2)
            last = [box.value]
    small = small_sums

    def qkv_shape(grad):
        return jnp.transpose(grad.reshape(3, width, HD), (1, 0, 2))

    home = lambda a: jnp.transpose(a, (1, 0, 2)).reshape(shape)
    return (
        home(output),
        home(input_grad),
        qkv_shape(feat_grad),
        grads_other[4],
        small[8],
        qkv_shape(grads_other[2]),
        grads_other[3],
        small[1],
        grads_other[0],
        lax.dynamic_index_in_dim(small, 16 + t[0][0], 0, keepdims=False),
        grads_other[1],
        small[0],
        jnp.stack([small[4], small[9], small[2]]),
        jnp.stack([small[5], small[10], small[3]]),
    )


def solution(mesh):
    return jax.shard_map(
        shards,
        mesh=mesh,
        in_specs=(
            P("dp", None, None, None), P("dp"), P(None, None, "tensor"), P("tensor", None), P(),
            P(None, None, "tensor"), P("tensor", None), P(), P(None, "tensor"), P("tensor"),
            P("tensor", None), P(), P(), P(), P("dp", None, None, None),
        ),
        out_specs=(
            P("dp", None, None, None), P("dp", None, None, None), P(None, None, "tensor"),
            P("tensor", None), P(), P(None, None, "tensor"), P("tensor", None), P(),
            P(None, "tensor"), P("tensor"), P("tensor", None), P(), P(), P(),
        ),
        check_vma=False,
    )
```

```python
from functools import partial

import jax
import jax.numpy as jnp
from jax import lax
from jax.experimental import pallas as pl
from jax.experimental.pallas import tpu as pltpu
from jax.sharding import PartitionSpec as P

HD = 128
EPSILON = 1e-05
NEGATIVE = -1e30
SCALE = HD**-0.5
BF = jnp.bfloat16
F32 = jnp.float32
MIB = 1 << 20
KNOBS = {'cost': 0, 'window': 'MA2', 'tail': 'OFpFOFOcFOgFrFO', 'out_tie': 'w', 'hs_tie': 'fq', 'rs_tie': '', 'g_tie': 'O3', 'vm': 18, 'vs': 16, 'vf': 60, 'vh': 16, 'vz': 24, 'ud_tie': 'a'}
FB = 8
GROUP = 16
HEADS = 4
RB = 16


def mm(a, b):
    return jnp.dot(a, b, preferred_element_type=F32)


def mm_nt(a, b):
    return lax.dot_general(a, b, (((1,), (1,)), ((), ())), preferred_element_type=F32)


def mm_tn(a, b):
    return lax.dot_general(a, b, (((0,), (0,)), ((), ())), preferred_element_type=F32)


def standardize(values):
    centered = values - jnp.mean(values, axis=-1, keepdims=True)
    inverse = lax.rsqrt(jnp.mean(centered * centered, axis=-1, keepdims=True) + EPSILON)
    return centered * inverse, inverse


def norm_backward(upstream, normed, inverse, gain):
    scaled = upstream * gain
    return inverse * (
        scaled
        - jnp.mean(scaled, axis=-1, keepdims=True)
        - normed * jnp.mean(scaled * normed, axis=-1, keepdims=True)
    )


def column_sum(values):
    return jnp.sum(values, axis=0, keepdims=True)


def softmax_keys(scores):
    grown = jnp.exp(scores - jnp.max(scores, axis=0, keepdims=True))
    return grown * (1.0 / jnp.sum(grown, axis=0, keepdims=True))


def gelu_parts(z):
    t = 1.0 / (1.0 + (0.3275911 * 0.7071067811865476) * jnp.abs(z))
    e = jnp.exp(-0.5 * z * z)
    poly = t * (
        0.127414796 + t * (-0.142248368 + t * (0.7107068705 + t * (-0.7265760135 + t * 0.5307027145)))
    )
    tail = poly * e
    cdf = jnp.where(z >= 0, 1.0 - tail, tail)
    return z * cdf, cdf + z * (e * 0.3989422804014327)


def masked_softmax(scores, feature_count):
    key = lax.broadcasted_iota(jnp.int32, scores.shape, 0)
    return softmax_keys(jnp.where(key < feature_count, scores, NEGATIVE)).astype(BF)


def three(w):
    return jnp.concatenate([w[0], w[1], w[2]], axis=-1)


def stacked(w):
    n = w.shape[0] // 3
    return jnp.concatenate([w[c * n : (c + 1) * n] for c in range(3)], axis=-1)


def unpacked(w):
    tall = jnp.concatenate([w[:, j * HD : (j + 1) * HD] for j in range(4)], axis=0)
    return stacked(tall)


def four_weights(fq, fq_far, near):
    tall = 3 * fq.shape[1] // 4
    packed = [(near, pl.BlockSpec((tall, 4 * HD), partial(lambda j, *_: (j, 0), j))) for j in range(2)]
    return [(fq, full(fq)), packed[0], (fq_far, full(fq_far)), packed[1]]


def wide(pieces):
    n = pieces[0].shape[0] // 4
    return jnp.concatenate(
        [jnp.concatenate([p[j * n : (j + 1) * n] for j in range(4)], axis=-1) for p in pieces], axis=0)


def live_columns(block, first, feature_count):
    values = block.astype(F32)
    index = first + lax.broadcasted_iota(jnp.int32, values.shape, 0)
    return jnp.where(index < feature_count, values, 0.0)


ANY = pl.BlockSpec(memory_space=pl.ANY)
VMEM = pl.BlockSpec(memory_space=pltpu.VMEM)


def full(a):
    zeros = (0,) * len(a.shape)
    return pl.BlockSpec(a.shape, lambda *_: zeros)


def shaped(shape, dtype=BF):
    return jax.ShapeDtypeStruct(shape, dtype)


def call(kernel, name, grid, t, ins, outs, scratch=(), vmem=KNOBS["vm"], us=1):
    t, after = t[:2], [a for a in t[2:]]
    count = 2 + len(ins)

    def body(*refs):
        kernel(*refs[:count], *refs[count + len(after) :])

    spec = pltpu.PrefetchScalarGridSpec(
        num_scalar_prefetch=2,
        grid=grid,
        in_specs=[s for _, s in ins] + [ANY] * len(after),
        out_specs=[s for _, s in outs],
        scratch_shapes=list(scratch),
    )
    return pl.pallas_call(
        body,
        grid_spec=spec,
        out_shape=[a for a, _ in outs],
        compiler_params=pltpu.CompilerParams(vmem_limit_bytes=vmem * MIB),
        cost_estimate=pl.CostEstimate(flops=us * KNOBS["cost"] * 1_000_000 + 1, bytes_accessed=1, transcendentals=0),
        name=name,
    )(*t, *[a for a, _ in ins], *after)


def pack_kernel(t_ref, d_ref, rq_ref, fo_ref, ro_ref, ub_ref, out_ref):
    width = rq_ref.shape[1]
    for c in range(3):
        out_ref[c * width : (c + 1) * width] = rq_ref[c]
    at = 3 * width
    for source in (fo_ref, ro_ref):
        for j in range(4):
            out_ref[at : at + HD] = source[:, j * HD : (j + 1) * HD]
            at += HD
    bias = [ub_ref[j * HD : (j + 1) * HD].astype(F32).reshape(1, HD) for j in range(4)]
    out_ref[at : at + 16] = jnp.concatenate(bias + [jnp.zeros((12, HD), F32)], axis=0).astype(BF)


def pack(t, rq, fo, ro, ub):
    out = shaped((3 * rq.shape[1] + 8 * HD + 16, HD))
    return call(pack_kernel, "pack", (), t, [(a, VMEM) for a in (rq, fo, ro, ub)], [(out, VMEM)], vmem=60)[0]


def pack_part(pack, what):
    rows = pack.shape[0] - 8 * HD - 16
    size, at = {"qkv": (rows, 0), "feat_out": (4 * HD, rows), "row_out": (4 * HD, rows + 4 * HD),
                "bias": (16, rows + 8 * HD)}[what]
    return pl.BlockSpec((size, HD), lambda *_: (at // size, 0))


def pack_parts(packs, what):
    return [(p, pack_part(p, what)) for p in packs]


def feature_forward_kernel(
    t_ref, d_ref, cells_ref, gains_ref, shifts_ref, w_ref, up_ref, down_ref, o0, o1, o2, o3, both_ref, qkv_scr, mix_scr
):
    feature_count, rows, width = cells_ref.shape
    padded = qkv_scr.shape[1] // rows

    @pl.when(pl.program_id(0) == 0)
    def _():
        qkv_scr[...] = jnp.zeros_like(qkv_scr)
        both_ref[: up_ref.shape[0]] = up_ref[...]
        both_ref[up_ref.shape[0] :] = down_ref[...]

    cells = cells_ref[...].astype(F32).reshape(feature_count * rows, width)
    normed, _ = standardize(cells)
    low = (normed * gains_ref[...].astype(F32)[0:1] + shifts_ref[...].astype(F32)[0:1]).astype(BF)
    qkv = mm(low, three(w_ref))
    for c in range(3):
        qkv_scr[c, 0 : feature_count * rows, :] = qkv[:, c * HD : (c + 1) * HD]
    for first in range(0, rows, GROUP):
        places = [pl.ds(r, padded, stride=rows) for r in range(first, first + GROUP)]
        parts = [[qkv_scr[c, every, :].astype(BF) for c in range(3)] for every in places]
        scores = [mm_nt(k, q) * SCALE for q, k, _ in parts]
        ps = [masked_softmax(x, feature_count) for x in scores]
        for every, p, (_, _, v) in zip(places, ps, parts):
            mix_scr[every, :] = mm_tn(p, v)
    count = o0.shape[1]
    for k, out in enumerate((o0, o1, o2, o3)):
        at = pl.multiple_of(lax.bitwise_xor(t_ref[0], k) * count, count)
        out[0] = mix_scr[pl.ds(at, count), :].astype(BF)


def feature_forward(t, cells, gains, shifts, weight, up, down, columns):
    feature_count, row_count, width = cells.shape
    padded = 4 * columns
    steps = row_count // RB
    out = (shaped((steps, columns * RB, HD)), pl.BlockSpec((1, columns * RB, HD), lambda i, t, d: (i, 0, 0)))
    return call(
        feature_forward_kernel, "feature_forward", (steps,), t,
        [(cells, pl.BlockSpec((feature_count, RB, width), lambda i, t, d: (0, i, 0)))]
        + [(a, full(a)) for a in (gains, shifts, weight, up, down)],
        [out] * 4 + [whole((up.shape[0] + down.shape[0], up.shape[1]))],
        [pltpu.VMEM((3, padded * RB, HD), F32), pltpu.VMEM((padded * RB, HD), F32)], vmem=KNOBS["vf"], us=11
    )


def column_block(array, columns):
    _, rows, width = array.shape
    return pl.BlockSpec((columns, rows, width), lambda i, t, d: (t[0], 0, 0))


def in_order(m, columns):
    steps = m.shape[0]
    halves = [m[i].reshape(columns, RB, HD) for i in range(steps)]
    return jnp.concatenate(halves, axis=1).reshape(columns * RB * steps, HD)


def row_forward_kernel(
    t_ref, d_ref, split_ref, m0, m1, m2, m3, cells_ref, f0, f1, f2, f3, r0, r1, r2, r3, w0, w1, w2, w3,
    wo_bias, wr_bias, gains_ref, shifts_ref,
    first_ref, n2_ref, qkv_ref, p_ref, o2_ref, second_ref, n3_ref, *, feature_count,
):
    columns, rows, width = cells_ref.shape
    cells = columns * rows
    side = p_ref.shape[2]
    key = lax.broadcasted_iota(jnp.int32, (side, side), 0)
    query = lax.broadcasted_iota(jnp.int32, (side, side), 1)
    same = lax.div(query, rows) == lax.div(key, rows)
    bias = jnp.where(jnp.logical_and(same, lax.rem(key, rows) < split_ref[0]), 0.0, NEGATIVE)

    gains = gains_ref[...].astype(F32)
    shifts = shifts_ref[...].astype(F32)
    stream = live_columns(cells_ref[...], t_ref[0] * columns, feature_count).reshape(cells, width)
    mixed = jnp.concatenate([in_order(m, columns) for m in (m0, m1, m2, m3)], axis=-1)
    first = stream + mm(mixed, wide((f0, f1, f2, f3))) + wo_bias[...].astype(F32)
    first_ref[...] = first
    normed, _ = standardize(first)
    low = (normed * gains[1:2] + shifts[1:2]).astype(BF)
    n2_ref[...] = low
    spans = [slice(b, b + side) for b in range(0, cells, side)]
    part = lambda h, span, c: qkv_ref[span, (3 * h + c) * HD : (3 * h + c + 1) * HD]
    weights = (w0, w1, w2, w3)
    for first_head in range(0, 4, HEADS):
        heads = range(first_head, first_head + HEADS)
        qkv_ref[:, 3 * HD * first_head : 3 * HD * (first_head + HEADS)] = mm(
            low, jnp.concatenate([stacked(weights[h]) for h in heads], axis=-1)).astype(BF)
        places = [(h, j, span) for h in heads for j, span in enumerate(spans)]
        scores = [mm_nt(part(h, span, 1), part(h, span, 0)) * SCALE + bias for h, _, span in places]
        ps = [softmax_keys(x).astype(BF) for x in scores]
        for (h, j, span), p in zip(places, ps):
            p_ref[h, j] = p
            o2_ref[span, h * HD : (h + 1) * HD] = mm_tn(p, part(h, span, 2)).astype(BF)
    second = first + mm(o2_ref[...], wide((r0, r1, r2, r3))) + wr_bias[...].astype(F32)
    second_ref[...] = second
    normed, _ = standardize(second)
    n3_ref[...] = (normed * gains[2:3] + shifts[2:3]).astype(BF)


def whole(shape, dtype=BF):
    return shaped(shape, dtype), full(shaped(shape, dtype))


def row_forward(t, split, mixed, cells, packs, wo_bias, wr_bias, gains, shifts, columns):
    feature_count, rows, width = cells.shape
    n = columns * rows
    side = 4 * rows
    ins = [(split, pl.BlockSpec(memory_space=pltpu.SMEM))] + [(m, full(m)) for m in mixed]
    ins += [(cells, column_block(cells, columns))]
    ins += pack_parts(packs, "feat_out") + pack_parts(packs, "row_out") + pack_parts(packs, "qkv")
    ins += [(a, full(a)) for a in (wo_bias, wr_bias, gains, shifts)]
    return call(
        partial(row_forward_kernel, feature_count=feature_count), "row_forward", (1,), t, ins,
        [whole((n, width), F32), whole((n, width)), whole((n, 12 * HD)), whole((4, n // side, side, side)),
         whole((n, 4 * HD)), whole((n, width), F32), whole((n, width))], us=9
    )


def hidden_pair(t_ref, n3_ref, grad_ref, ups, packs, downs, grads, bias_grads, feature_count):
    columns, rows, width = grad_ref.shape
    g3 = live_columns(grad_ref[...], t_ref[0] * columns, feature_count).reshape(columns * rows, width)
    n3, gl = n3_ref[...], g3.astype(BF)
    n3_t, gl_t = n3.T, gl.T
    hidden = ups[0].shape[1]
    up = jnp.concatenate([u[...] for u in ups], axis=-1)
    down = jnp.concatenate([d[...] for d in downs], axis=0)
    bias = jnp.concatenate([p[...].astype(F32)[j : j + 1] for p in packs for j in range(4)], axis=-1)
    ms, dzs = [], []
    step = 256
    count = 2 * hidden // step
    ahead = []

    def begin(c):
        span = slice(c * step, (c + 1) * step)
        return mm(n3, up[:, span]) + bias[:, span], mm_nt(gl, down[span])

    ahead = begin(0)
    for c in range(count):
        z, dm = ahead
        if c + 1 < count:
            ahead = begin(c + 1)
        act, slope = gelu_parts(z)
        m = act.astype(BF)
        dz = (dm * slope).astype(BF)
        j, at = divmod(c * step, hidden)
        span = slice(at, at + step)
        grads[j][:width, span] = mm(n3_t, dz).astype(BF)
        grads[j][width:, span] = mm(gl_t, m).astype(BF)
        bias_grads[j][:, span] = column_sum(dz.astype(F32))
        ms.append(m)
        dzs.append(dz)
    out = mm(jnp.concatenate(ms, axis=-1), down)
    dn3 = mm_nt(jnp.concatenate(dzs, axis=-1), up)
    return g3, out, dn3


def hidden_first_kernel(
    t_ref, d_ref, n3_ref, grad_ref, up0, up1, b0, b1, down0, down1, out_ref, dn3_ref, wg0, wg1, bg0, bg1,
    *, feature_count,
):
    _, out, dn3 = hidden_pair(
        t_ref, n3_ref, grad_ref, (up0, up1), (b0, b1), (down0, down1), (wg0, wg1), (bg0, bg1), feature_count)
    out_ref[...] = out
    dn3_ref[...] = dn3


def hidden_second_kernel(
    t_ref, d_ref, n3_ref, grad_ref, up0, up1, b0, b1, down0, down1, out_in, dn3_in, second_ref, down_bias, gains_ref,
    earlier_ref, out_ref, g2_ref, stats_ref, wg0, sent_ref, bg0, bg1, *, feature_count,
):
    tall = earlier_ref.shape[0]
    sent_ref[:tall] = earlier_ref[...]
    g3, out, dn3 = hidden_pair(
        t_ref, n3_ref, grad_ref, (up0, up1), (b0, b1), (down0, down1), (wg0, sent_ref.at[pl.ds(tall, tall)]), (bg0, bg1),
        feature_count)
    second = second_ref[...]
    out_ref[...] = (second + out_in[...] + out + down_bias[...].astype(F32)).astype(BF)
    dn3 = dn3_in[...] + dn3
    normed, inverse = standardize(second)
    g2 = g3 + norm_backward(dn3, normed, inverse, gains_ref[...].astype(F32)[2:3])
    g2_ref[...] = g2
    stats_ref[...] = rows_of([g3, g2, dn3 * normed, dn3])


def rows_of(arrays):
    return jnp.concatenate(
        [column_sum(a) for a in arrays] + [jnp.zeros((8 - len(arrays), arrays[0].shape[1]), F32)], axis=0)


def hidden_call(t, n3, grads, both, packs, columns, extra=None):
    n, width = n3.shape
    hidden = both[0].shape[1]
    ins = [(n3, full(n3)), (grads, column_block(grads, columns))]
    ins += [(a, pl.BlockSpec((width, hidden), lambda *_: (0, 0))) for a in both] + pack_parts(packs, "bias")
    ins += [(a, pl.BlockSpec((hidden, width), lambda *_: (1, 0))) for a in both]
    bias_grads = [whole((1, hidden), F32)] * 2
    if extra is None:
        kernel, name = hidden_first_kernel, "hidden_first"
        results = [whole((n, width), F32)] * 2 + [whole((2 * width, hidden))] * 2 + bias_grads
    else:
        kernel, name = hidden_second_kernel, "hidden_second"
        ins += [(a, full(a)) for a in extra]
        results = [whole((n, width)), whole((n, width), F32), whole((8, width), F32)]
        results += [whole((2 * width, hidden)), whole((4 * width, hidden))] + bias_grads
    return call(partial(kernel, feature_count=grads.shape[0]), name, (1,), t, ins, results, us=7)


def attentions_backward(blocks):
    dps = [mm_nt(v, do) for _, _, v, _, do in blocks]
    pfs = [b[3].astype(F32) for b in blocks]
    dss = [(pf * (dp - jnp.sum(dp * pf, axis=0, keepdims=True))).astype(BF) for dp, pf in zip(dps, pfs)]
    dvs = [mm(p, do) for _, _, _, p, do in blocks]
    dks = [mm(ds, b[0]) * SCALE for ds, b in zip(dss, blocks)]
    dqs = [mm_tn(ds, b[1]) * SCALE for ds, b in zip(dss, blocks)]
    return list(zip(dqs, dks, dvs))


def row_backward_kernel(
    t_ref, d_ref, g2_ref, first_ref, qkv_ref, p_ref, gains_ref, n2_ref, o2_ref, m0, m1, m2, m3, fq0, fq2,
    w0, w1, w2, w3, r0, r1, r2, r3, s0, near_ref, s2, s3, stats_ref, keep_ref, send_ref, g1_scr, dqkv_ref,
):
    width = fq0.shape[1]
    for j, weights in enumerate((fq0, fq2)):
        tall = 3 * width // 4
        for lane in range(4):
            for at, first, count in stretches(lane * tall, tall, width):
                near_ref[j * tall + at : j * tall + at + count, lane * HD : (lane + 1) * HD] = (
                    weights[first // width, first % width : first % width + count, :])
    g2 = g2_ref[...]
    cells, width = g2.shape
    side = p_ref.shape[2]
    gl2 = g2.astype(BF)
    do = mm_nt(gl2, wide((r0, r1, r2, r3))).astype(BF)
    spans = [slice(b, b + side) for b in range(0, cells, side)]
    for first in range(0, 4, 2):
        heads = range(first, first + 2)
        blocks = [
            [qkv_ref[span, (3 * h + c) * HD : (3 * h + c + 1) * HD] for c in range(3)]
            + [p_ref[h, j], do[span, HD * h : HD * (h + 1)]] for h in heads for j, span in enumerate(spans)]
        places = [(h, span) for h in heads for span in spans]
        for (h, span), parts in zip(places, attentions_backward(blocks)):
            for c, part in enumerate(parts):
                dqkv_ref[span, (3 * h + c) * HD : (3 * h + c + 1) * HD] = part.astype(BF)
    dn2 = mm_nt(dqkv_ref[...], jnp.concatenate([stacked(w) for w in (w0, w1, w2, w3)], axis=-1))
    normed, inverse = standardize(first_ref[...])
    g1 = g2 + norm_backward(dn2, normed, inverse, gains_ref[...].astype(F32)[1:2])
    columns, rows, _ = g1_scr.shape
    g1_scr[...] = g1.reshape(columns, rows, width)
    share = rows // 4
    for k, out in enumerate((s0, near_ref.at[pl.ds(6 * width // 4, columns * share)], s2, s3)):
        at = pl.multiple_of(lax.bitwise_xor(t_ref[0], k) * share, share)
        out[...] = g1_scr[:, pl.ds(at, share), :].reshape(columns * share, width).astype(BF)
    stats_ref[...] = rows_of([g1, dn2 * normed, dn2])
    mixed = [in_order(m, columns) for m in (m0, m1, m2, m3)]
    row_grads(n2_ref[...], dqkv_ref[...], gl2, o2_ref[...], g1.astype(BF), mixed, keep_ref, send_ref)


def stretches(first, count, size):
    at = 0
    while at < count:
        rows = min(count - at, size - (first + at) % size)
        yield at, first + at, rows
        at += rows


def row_grads(n2, dqkv, gl2, o2, gl1, mixed, keep_ref, send_ref):
    width = n2.shape[1]
    grad = mm(n2.T, dqkv).astype(BF)
    out_grad = mm(gl2.T, o2).astype(BF)
    feat_grad = mm(gl1.T, jnp.concatenate(mixed, axis=-1)).astype(BF)
    for h in range(4):
        out = (keep_ref, send_ref)[h % 2].at[h // 2]
        blocks = [grad[:, (3 * h + c) * HD : (3 * h + c + 1) * HD] for c in range(3)]
        blocks += [out_grad[:, HD * h : HD * (h + 1)], feat_grad[:, HD * h : HD * (h + 1)]]
        for at, first, count, lane in row_places(width):
            out[at : at + count, lane * HD : (lane + 1) * HD] = blocks[first // width][first % width : first % width + count]


def row_backward(t, g2, first, qkv, p, gains, n2, o2, mixed, fq, fq_far, packs, rows):
    n, width = g2.shape
    ins = [(a, full(a)) for a in (g2, first, qkv, p, gains, n2, o2, *mixed, fq, fq_far)]
    ins += pack_parts(packs, "qkv") + pack_parts(packs, "row_out")
    piece = whole((n // 4, width))
    return call(
        row_backward_kernel, "row_backward", (1,), t, ins,
        [piece, whole((6 * width // 4 + n // 4, width)), piece, piece, whole((8, width), F32)]
        + [whole((2, 5 * width // 4, 4 * HD))] * 2,
        [pltpu.VMEM((n // rows, rows, width), F32), pltpu.VMEM(qkv.shape, BF)], us=11,
    )


def row_places(width):
    tall = 5 * width // 4
    first = 0
    while first < 5 * width:
        count = min(width - first % width, tall - first % tall)
        yield first % tall, first, count, first // tall
        first += count


def own_rows(t_ref, cells_ref, cell_scr, share):
    feature_count, block_rows, width = cells_ref.shape
    cell_scr[0:feature_count] = cells_ref[...].astype(F32)
    cell_scr[feature_count:] = jnp.zeros_like(cell_scr[feature_count:])
    at = pl.multiple_of(lax.rem(t_ref[0], block_rows // share) * share, share)
    return cell_scr[:, pl.ds(at, share), :].reshape(cell_scr.shape[0] * share, width)


def row_block(cells, share):
    feature_count, _, width = cells.shape
    per = RB // share
    return pl.BlockSpec((feature_count, RB, width), lambda i, t, d: (0, lax.div(t[0], per), 0))


def feature_again_kernel(
    t_ref, d_ref, cells_ref, gains_ref, shifts_ref, w0, w1, w2, w3, n1_ref, qkv_ref, p_ref, cell_scr, qkv_scr
):
    feature_count = cells_ref.shape[0]
    share, padded, _ = qkv_ref.shape
    normed, _ = standardize(own_rows(t_ref, cells_ref, cell_scr, share))
    low = (normed * gains_ref[...].astype(F32)[0:1] + shifts_ref[...].astype(F32)[0:1]).astype(BF)
    n1_ref[...] = low
    packed = mm(low, jnp.concatenate([three(w0), unpacked(w1), three(w2), unpacked(w3)], axis=-1))
    for c in range(12):
        qkv_scr[c] = packed[:, c * HD : (c + 1) * HD]
    for h in range(4):
        parts = [[qkv_scr[3 * h + c, pl.ds(r, padded, stride=share), :].astype(BF) for c in range(3)] for r in range(share)]
        scores = [mm_nt(k, q) * SCALE for q, k, _ in parts]
        for r in range(share):
            for c, part in enumerate(parts[r]):
                qkv_ref[r, :, (3 * h + c) * HD : (3 * h + c + 1) * HD] = part
            p_ref[r, h] = masked_softmax(scores[r], feature_count)


def feature_again(t, cells, gains, shifts, fq, fq_far, near, columns, share):
    width = cells.shape[2]
    padded = 4 * columns
    return call(
        feature_again_kernel, "feature_again", (1,), t,
        [(cells, row_block(cells, share))] + [(a, full(a)) for a in (gains, shifts)] + four_weights(fq, fq_far, near),
        [whole((padded * share, width)), whole((share, padded, 12 * HD)), whole((share, 4, padded, padded))],
        [pltpu.VMEM((padded, RB, width), F32), pltpu.VMEM((12, padded * share, HD), F32)], vmem=KNOBS["vs"], us=4
    )


def feature_backward_kernel(
    t_ref, d_ref, r0, r1, r2, r3, f0, f1, f2, f3, qkv_ref, p_ref, n1_ref,
    g1_ref, dqkv_ref, keep0, keep1, send0, send1, low_scr, do_scr, dqkv_scr,
):
    width = g1_ref.shape[1]
    share, padded, _ = qkv_ref.shape
    for k, piece in enumerate((r0, r1, r2, r3)):
        count = piece.shape[0]
        at = pl.multiple_of(lax.bitwise_xor(t_ref[0], k) * count, count)
        low_scr[pl.ds(at, count), :] = piece[...]
        g1_ref[pl.ds(at, count), :] = piece[...].astype(F32)
    do = mm_nt(low_scr[...], wide((f0, f1, f2, f3)))
    for h in range(4):
        do_scr[h] = do[:, h * HD : (h + 1) * HD]
    n1_t = n1_ref[...].T
    for h in range(4):
        rows = [pl.ds(r, padded, stride=share) for r in range(share)]
        heads = range(h, h + HEADS) if h % HEADS == 0 else ()
        blocks = [
            [qkv_ref[r, :, (3 * g + c) * HD : (3 * g + c + 1) * HD] for c in range(3)]
            + [p_ref[r, g], do_scr[g, every, :].astype(BF)] for g in heads for r, every in enumerate(rows)]
        places = [(g, every) for g in heads for every in rows]
        for (g, every), parts in zip(places, attentions_backward(blocks)):
            for c, part in enumerate(parts):
                dqkv_scr[3 * g + c, every, :] = part
        out = ((keep0, keep1), (send0, send1))[h % 2]
        for c in range(3):
            dqkv_ref[:, (3 * h + c) * HD : (3 * h + c + 1) * HD] = dqkv_scr[3 * h + c].astype(BF)
        grad = mm(n1_t, dqkv_ref[:, 3 * HD * h : 3 * HD * (h + 1)]).astype(BF)
        for c in range(3):
            out[h // 2][c * width : (c + 1) * width, :] = grad[:, c * HD : (c + 1) * HD]


def feature_backward(t, pieces, packs, qkv, p, n1):
    share, _, padded, _ = p.shape
    width = pieces[0].shape[1]
    cells = share * padded
    return call(
        feature_backward_kernel, "feature_backward", (1,), t,
        [(a, pl.BlockSpec(pieces[0].shape, partial(lambda j, *_: (j, 0), 0 if k != 1 else a.shape[0] // pieces[0].shape[0] - 1)))
         for k, a in enumerate(pieces)] + pack_parts(packs, "feat_out") + [(a, full(a)) for a in (qkv, p, n1)],
        [whole((cells, width), F32), whole((cells, 12 * HD))] + [whole((3 * width, HD))] * 4,
        [pltpu.VMEM((cells, width), BF), pltpu.VMEM((4, cells, HD), F32), pltpu.VMEM((12, cells, HD), F32)], us=11
    )


def feature_input_kernel(
    t_ref, d_ref, cells_ref, g1_ref, dqkv_ref, gains_ref, w0, w1, w2, w3, stats_a, stats_b, b0, b1, b2, b3,
    out_ref, stats_ref, cell_scr, sums_scr,
):
    cells, width = g1_ref.shape
    share = cells // cell_scr.shape[0]
    normed, inverse = standardize(own_rows(t_ref, cells_ref, cell_scr, share))
    dn1 = mm_nt(dqkv_ref[...], jnp.concatenate([three(w0), unpacked(w1), three(w2), unpacked(w3)], axis=-1))
    g0 = g1_ref[...] + norm_backward(dn1, normed, inverse, gains_ref[...].astype(F32)[0:1])
    out_ref[...] = g0[: out_ref.shape[0]].astype(BF)
    sums_scr[0:8] = stats_a[...]
    sums_scr[8:16] = stats_b[...]
    sums_scr[4:5] = column_sum(dn1 * normed)
    sums_scr[5:6] = column_sum(dn1)
    sums_scr[16:32] = jnp.zeros((16, width), F32)
    for k, row in enumerate((b0, b1, b2, b3)):
        sums_scr[pl.ds(16 + lax.bitwise_xor(t_ref[0], k), 1), :] = row[...]
    for j in range(4):
        stats_ref[32 * j : 32 * (j + 1)] = sums_scr[:, j * HD : (j + 1) * HD]


def feature_input(t, cells, g1, dqkv, gains, fq, fq_far, near, sums, share):
    count, width = g1.shape
    kept = (cells.shape[0] + 1) // 2 * 2 * share
    ins = [(cells, row_block(cells, share))] + [(a, full(a)) for a in (g1, dqkv, gains)]
    ins += four_weights(fq, fq_far, near) + [(a, full(a)) for a in sums]
    return call(
        feature_input_kernel, "feature_input", (1,), t, ins, [whole((kept, width)), whole((128, HD), F32)],
        [pltpu.VMEM((count // share, RB, width), F32), pltpu.VMEM((32, width), F32)], vmem=KNOBS["vs"], us=2,
    )


def pair_kernel(t_ref, d_ref, own, far, out_ref):
    out_ref[: own.shape[0]] = own[...]
    out_ref[own.shape[0] :] = far[...]


def pair(t, own, far):
    return call(pair_kernel, "pair", (), t, [(own, VMEM), (far, VMEM)], [(shaped((2 * own.shape[0], own.shape[1])), VMEM)], vmem=12)[0]


def columns_home_kernel(t_ref, d_ref, p0, p1, p2, p3, out_ref):
    for k, piece in enumerate((p0, p1, p2, p3)):

        @pl.when(pl.program_id(0) == lax.bitwise_xor(t_ref[0], k))
        def _():
            out_ref[...] = piece[...].reshape(out_ref.shape)


def columns_home(t, own, far, near, feature_count, rows):
    count, width = own.shape
    columns = count // rows
    block = lambda i: pl.BlockSpec((count, width), lambda *_: (i, 0))
    return call(
        columns_home_kernel, "columns_home", (4,), t,
        [(own, block(0)), (near, block(0)), (far, block(0)), (near, block(1))],
        [(shaped((feature_count, rows, width)), pl.BlockSpec((columns, rows, width), lambda i, t, d: (i, 0, 0)))], vmem=KNOBS["vh"],
    )[0]


def rows_home_kernel(t_ref, d_ref, p0, p1, p2, p3, out_ref, scr):
    columns, rows, width = scr.shape
    share = rows // 4
    for k, piece in enumerate((p0, p1, p2, p3)):
        at = pl.multiple_of(lax.bitwise_xor(t_ref[0], k) * share, share)
        scr[:, pl.ds(at, share), :] = piece[...].astype(F32).reshape(columns, share, width)
    out_ref[...] = scr[...].astype(BF)


def rows_home(t, own, far, near, feature_count, rows):
    count, width = own.shape
    share = rows // 4
    steps = 5
    columns = count // share // steps
    block = lambda first: pl.BlockSpec((columns * share, width), lambda i, t, d: (first + i, 0))
    return call(
        rows_home_kernel, "rows_home", (steps,), t,
        [(own, block(0)), (near, block(0)), (far, block(0)), (near, block(steps))],
        [(shaped((feature_count, rows, width)), pl.BlockSpec((columns, rows, width), lambda i, t, d: (i, 0, 0)))],
        [pltpu.VMEM((columns, rows, width), F32)], vmem=KNOBS["vh"],
    )[0]


def swap(values, axis, mask):
    count = lax.axis_size(axis)
    return lax.ppermute(values, axis, [(i, i ^ mask) for i in range(count)])


def gather_groups(own):
    far = swap(own, "tensor", 2)
    return own, swap(own, "tensor", 1), far, swap(far, "tensor", 1)


class Box:
    def __init__(self, value):
        self.value = value


def tied(values, *boxes):
    many = isinstance(values, tuple)
    values = values if many else (values,)
    out = lax.optimization_barrier((*values, *[b.value for b in boxes]))
    for box, value in zip(boxes, out[len(values) :]):
        box.value = value
    return out[: len(values)] if many else out[0]


def dp_masks():
    masks, mask = [], 1
    while mask < lax.axis_size("dp"):
        masks.append(mask)
        mask *= 2
    return masks


def digit(d_ref, mask):
    return lax.rem(lax.div(d_ref[0], mask), 2)


def halves(d_ref, mask, rows):
    side = digit(d_ref, mask)
    return [pl.multiple_of(s * rows, rows) for s in (side, 1 - side)]


def added(a, b):
    return a.astype(F32) + b.astype(F32)


def merge(name, kernel, t, ins, outs, scratch=(), vmem=16):
    return call(kernel, name, (), t, [(a, VMEM) for a in ins], [(shaped(o), VMEM) for o in outs], scratch, vmem=vmem)


def first_halves(t, hg0, hg2, row_keep, got, row_got, masks):
    hidden = hg0.shape[0] // 2
    half = row_keep.shape[1] // 2
    rows, width = hidden + half, hg0.shape[1]

    def kernel(t_ref, d_ref, g0, g2, keep, r, row_r, ak, as_, bk, bs, scr):
        for group, mine in enumerate((g0, g2)):
            for which, (kept, sent, mask) in enumerate(((ak, as_, masks[0]), (bk, bs, masks[1]))):
                at = which * hidden
                scr[:hidden] = added(mine[at : at + hidden], r[2 * hidden * group + at : 2 * hidden * group + at + hidden])
                at = which * half
                scr[hidden:] = added(keep[group, at : at + half], row_r[group, at : at + half])
                for out, first in zip((kept, sent), halves(d_ref, mask, rows // 2)):
                    out[group] = scr[pl.ds(first, rows // 2), :].astype(BF)

    return merge("ab_first", kernel, t, (hg0, hg2, row_keep, got, row_got), [(2, rows // 2, width)] * 4,
                 [pltpu.VMEM((rows, width), F32)], vmem=20)


def second_halves(t, a, ar, b, br, masks):
    _, rows, width = a.shape

    def kernel(t_ref, d_ref, a, ar, b, br, ak, as_, bk, bs):
        for x, y, kept, sent, mask in ((a, ar, ak, as_, masks[1]), (b, br, bk, bs, masks[0])):
            for out, first in zip((kept, sent), halves(d_ref, mask, rows // 2)):
                span = (slice(None), pl.ds(first, rows // 2), slice(None))
                out[...] = added(x[span], y[span]).astype(BF)

    return merge("ab_second", kernel, t, (a, ar, b, br), [(2, rows // 2, width)] * 4)


def groups_apart(t, a, ar, b, br):
    _, rows, width = a.shape

    def kernel(t_ref, d_ref, a, ar, b, br, kept, sent):
        for group, out in enumerate((kept, sent)):
            out[:rows] = added(a[group], ar[group]).astype(BF)
            out[rows:] = added(b[group], br[group]).astype(BF)

    return merge("ab_groups", kernel, t, (a, ar, b, br), [(2 * rows, width)] * 2)


def sums(t, k, r):
    def kernel(t_ref, d_ref, k, r, out):
        out[...] = added(k[...], r[...]).astype(BF)

    return merge("sums", kernel, t, (k, r), [k.shape])


def sums_apart(t, k, r):
    rows, width = k.shape[0] // 2, k.shape[1]

    def kernel(t_ref, d_ref, k, r, a, b):
        a[...] = added(k[:rows], r[:rows]).astype(BF)
        b[...] = added(k[rows:], r[rows:]).astype(BF)

    return merge("ab_apart", kernel, t, (k, r), [(rows, width)] * 2)


def joins(t, pairs, masks):
    def kernel(t_ref, d_ref, *refs):
        for j, mask in enumerate(masks):
            own, other, out = refs[2 * j], refs[2 * j + 1], refs[2 * len(masks) + j]
            for source, first in zip((own, other), halves(d_ref, mask, own.shape[0])):
                out[pl.ds(first, own.shape[0]), :] = source[...]

    return merge("joins", kernel, t, [a for p in pairs for a in p], [(2 * p[0].shape[0], p[0].shape[1]) for p in pairs])


def feature_groups(t, own, got, mine, theirs):
    rows, width = own[0].shape
    more = mine.shape[0]

    def kernel(t_ref, d_ref, a0, a2, b0, b2, sa, sb, kept, sent):
        small = added(sa[...], sb[...]).astype(BF)
        for out, a, b in ((kept, a0, b0), (sent, a2, b2)):
            out[:rows] = added(a[...], b[...]).astype(BF)
            out[rows:] = small

    return merge("f_groups", kernel, t, (*own, *got, mine, theirs), [(rows + more, width)] * 2)


def half_sums(t, k, r, mask):
    rows, width = k.shape[0] // 2, k.shape[1]

    def kernel(t_ref, d_ref, k, r, kept, sent):
        for out, first in zip((kept, sent), halves(d_ref, mask, rows)):
            span = (pl.ds(first, rows), slice(None))
            out[...] = added(k[span], r[span]).astype(BF)

    return merge("f_half", kernel, t, (k, r), [(rows, width)] * 2)


def joined(d_ref, own, other, mask, scr):
    rows = own.shape[0]
    side = digit(d_ref, mask)
    for source, place in ((own, side), (other, 1 - side)):
        scr[pl.ds(pl.multiple_of(place * rows, rows), rows), :] = source[...].astype(F32)


def finish_kernel(t_ref, d_ref, a0, a1, b0, b1, up_ref, down_ref, qkv_ref, row_out_ref, feat_out_ref, scr_a, scr_b, tall, *, masks):
    joined(d_ref, a0, a1, masks[0], scr_a)
    joined(d_ref, b0, b1, masks[1], scr_b)
    width = up_ref.shape[0]
    half = scr_a.shape[0] - width
    up_ref[...] = scr_a[0:width]
    down_ref[...] = scr_b[0:width].T
    for at, first, count, lane in row_places(width):
        for scr, low, high in ((scr_a, 0, half), (scr_b, half, 2 * half)):
            begin, end = max(at, low), min(at + count, high)
            if begin < end:
                to = first + begin - at
                tall[to : to + end - begin, :] = scr[width + begin - low : width + end - low, lane * HD : (lane + 1) * HD]
    qkv_ref[...] = tall[0 : 3 * width]
    row_out_ref[...] = tall[3 * width : 4 * width].T
    feat_out_ref[...] = tall[4 * width : 5 * width].T


def finish(t, a, b, masks, width):
    rows, w = a[0].shape
    scr = pltpu.VMEM((2 * rows, w), F32)
    outs = [shaped(s, F32) for s in ((width, w), (w, width), (3 * width, HD), (HD, width), (HD, width))]
    return call(
        partial(finish_kernel, masks=masks), "finish", (), t,
        [(x, VMEM) for x in (*a, *b)], [(o, VMEM) for o in outs],
        [scr, scr, pltpu.VMEM((5 * width, HD), F32)], vmem=KNOBS["vz"])


def finish_feature_kernel(t_ref, d_ref, own, other, qkv_ref, sums_ref, scr, *, mask):
    joined(d_ref, own, other, mask, scr)
    rows = qkv_ref.shape[0]
    qkv_ref[...] = scr[0:rows]
    tall = sums_ref.shape[0]
    for j in range(4):
        sums_ref[:, j * HD : (j + 1) * HD] = scr[rows + j * tall : rows + (j + 1) * tall]


def finish_feature(t, own, other, mask, width, small):
    rows, w = own.shape
    return call(
        partial(finish_feature_kernel, mask=mask), "finish_feature", (), t, [(own, VMEM), (other, VMEM)],
        [(shaped((3 * width, w), F32), VMEM), (shaped((small, 4 * HD), F32), VMEM)],
        [pltpu.VMEM((2 * rows, w), F32)], vmem=16)


def shards(
    table_cells, splits, feat_qkv, feat_out, feat_out_bias, row_qkv, row_out, row_out_bias,
    up_weight, up_bias, down_weight, down_bias, norm_gains, norm_biases, cotangent,
):
    shape = table_cells.shape
    _, row_count, feature_count, width = shape
    share = row_count // 4
    columns = -(-feature_count // (4 * FB)) * FB
    t = tuple(lax.axis_index(a).astype(jnp.int32).reshape(1) for a in ("tensor", "dp"))
    masks = dp_masks()
    cells = jnp.transpose(table_cells[0], (1, 0, 2))
    grads = jnp.transpose(cotangent[0], (1, 0, 2))
    fob, rob, dnb = (b.reshape(1, width) for b in (feat_out_bias, row_out_bias, down_bias))
    fq = jnp.transpose(feat_qkv, (1, 0, 2))
    rq = jnp.transpose(row_qkv, (1, 0, 2))

    near, far = masks[:2], masks[2:]
    over = lambda v, mask: swap(v, "tensor", 2) if mask == "x" else swap(v, "dp", mask)
    core = lambda v: swap(v, "tensor", 1)

    own = pack(t, rq, feat_out, row_out, up_bias)
    own_far = swap(own, "tensor", 2)
    *mixed, both = feature_forward(t, cells, norm_gains, norm_biases, fq, up_weight, down_weight, columns)
    kept = Box(mixed[0])
    own_far = tied(own_far, kept)
    packs = own, core(own), own_far, core(own_far)
    mixed = [kept.value] + [swap(mixed[k], "tensor", k) for k in (1, 2, 3)]
    a2, a3 = Box(mixed[2]), Box(mixed[3])
    both_far = swap({"a": lambda: tied(both, a2, a3), "2": lambda: tied(both, a2), "": lambda: both}[KNOBS["ud_tie"]](), "tensor", 2)
    mixed[2:] = a2.value, a3.value

    first, n2, row_packed, row_p, o2, second, n3 = row_forward(
        t, splits, mixed, cells, packs, fob, rob, norm_gains, norm_biases, columns)
    out_a, dn3_a, hg0, hg1, bg0, bg1 = hidden_call(t, n3, grads, (both, core(both)), packs[:2], columns)
    kept, fq_kept = Box(out_a), Box(hg0)
    both_far = tied(both_far, kept)
    fq_far = swap(tied(fq, fq_kept), "tensor", 2)
    hg0 = fq_kept.value
    out_f, g2, stats_a, hg2, hidden_send, bg2, bg3 = hidden_call(
        t, n3, grads, (both_far, core(both_far)), packs[2:], columns,
        [kept.value, dn3_a, second, dnb, norm_gains, hg1])
    fq_box = Box(fq_far)
    if KNOBS["hs_tie"] == "fq":
        hidden_got = core(tied(hidden_send, fq_box))
    fq_far = fq_box.value
    s0, near_send, s2, s3, stats_b, row_keep, row_send = row_backward(
        (*t, out_f), g2, first, row_packed, row_p, norm_gains, n2, o2, mixed, fq, fq_far, packs, row_count)
    pieces = [s0, core(near_send), swap(s2, "tensor", 2), swap(s3, "tensor", 3)]
    near_got = pieces[1]
    K = KNOBS
    boxes = {"s0": Box(s0), "rs": Box(row_send), "near": Box(near_got)}
    if K["hs_tie"] != "fq":
        hidden_got = core(tied(hidden_send, boxes[K["hs_tie"]]) if K["hs_tie"] else hidden_send)
    row_got = core(tied(row_send, boxes[K["rs_tie"]]) if K["rs_tie"] else boxes["rs"].value)
    pieces[0] = boxes["s0"].value
    pieces[1] = near_got = boxes["near"].value

    last = [s0]
    boxes.update(out=Box(out_f), w=Box(pieces[3]), w2=Box(pieces[2]))
    out_far = None
    if K["out_tie"] == "s0":
        out_far = swap(tied(out_f, boxes["s0"]), "tensor", 2)
        pieces[0] = boxes["s0"].value
    if K["out_tie"] == "hs":
        out_far = swap(out_f, "tensor", 2)
    for what in K["window"]:
        if what == "A":
            n1, feat_packed, feat_p = feature_again(
                (*t, *last), cells, norm_gains, norm_biases, fq, fq_far, near_got, columns, share)
            last = [feat_p]
        elif what == "M":
            ak, a_sent, bk, b_sent = first_halves((*t, *last), hg0, hg2, row_keep, hidden_got, row_got, near)
            last = [ak]
            ar, br = over(a_sent, near[0]), over(b_sent, near[1])
        else:
            last = [*last, pieces[2], pieces[3]]
    if K["out_tie"] == "w":
        out_far = swap(tied(out_f, boxes["w"], boxes["w2"]), "tensor", 2)
        pieces[2:] = boxes["w2"].value, boxes["w"].value

    g1, dqkv_f, f0, f2, f1, f3 = feature_backward((*t, *last), pieces, packs, feat_packed, feat_p, n1)
    g0, small = feature_input(
        t, cells, g1, dqkv_f, norm_gains, fq, fq_far, near_got, (stats_a, stats_b, bg0, bg1, bg2, bg3), share)
    f_got = core(f1), core(f3)
    small_got = core(small)
    last = [small]

    state = {"O": 0, "F": 0}
    grads_other = feat_grad = None

    def step_other(last):
        nonlocal ak, ar, bk, br, ab, abr, grads_other
        here = state["O"]
        tt = (*t, *last)
        if here == 0:
            ak, a_sent, bk, b_sent = out = second_halves(tt, ak, ar, bk, br, near)
            ar, br = over(a_sent, near[1]), over(b_sent, near[0])
        elif here == 1:
            ab, sent = out = groups_apart(tt, ak, ar, bk, br)
            abr = over(sent, "x")
        elif here < 2 + len(far):
            ab, = out = sums(tt, ab, abr)
            abr = over(ab, far[here - 2])
        elif here == 2 + len(far):
            ak, bk = out = sums_apart(tt, ab, abr)
            ar, br = over(ak, near[1]), over(bk, near[0])
        elif here == 3 + len(far):
            ak, bk = out = joins(tt, ((ak, ar), (bk, br)), (near[1], near[0]))
            ar, br = over(ak, near[0]), over(bk, near[1])
        else:
            grads_other = out = finish(tt, (ak, ar), (bk, br), near, width)
        state["O"] += 1
        return out[:1]

    def step_feature(last):
        nonlocal fk, fr, feat_grad, small_sums
        here = state["F"]
        tt = (*t, *last)
        if here == 0:
            fk, sent = out = feature_groups(tt, (f0, f2), f_got, small, small_got)
            fr = over(sent, "x")
        elif here < 3:
            fk, sent = out = half_sums(tt, fk, fr, near[here - 1])
            fr = over(sent, near[here - 1])
        elif here < 3 + len(far):
            fk, = out = sums(tt, fk, fr)
            fr = over(fk, far[here - 3])
        elif here == 3 + len(far):
            fk, = out = sums(tt, fk, fr)
            fr = over(fk, near[1])
        elif here == 4 + len(far):
            fk, = out = joins(tt, ((fk, fr),), (near[1],))
            fr = over(fk, near[0])
        else:
            feat_grad, small_sums = out = finish_feature(tt, fk, fr, near[0], width, small.shape[0] // 4)
        state["F"] += 1
        return out[:1]

    ab = abr = fk = fr = small_sums = g0_far = None
    steps = list(K["tail"])
    while steps or grads_other is None or feat_grad is None:
        what = steps.pop(0) if steps else ("O" if grads_other is None else "F")
        if what == "O" and grads_other is None:
            last = step_other(last)
        elif what == "F" and feat_grad is None:
            last = step_feature(last)
        elif what == "p":
            out_pair = pair((*t, *last), out_f, out_far)
            out_near = core(out_pair)
            last = [out_pair]
        elif what == "c":
            output = columns_home((*t, *last), out_f, out_far, out_near, feature_count, row_count)
            last = [output]
        elif what == "g":
            g0_pair = pair((*t, *last), g0, g0_far)
            g0_near = core(g0_pair)
            last = [g0_pair]
        elif what == "r":
            input_grad = rows_home((*t, *last), g0, g0_far, g0_near, feature_count, row_count)
            last = [input_grad]
        key = what + str(state.get(what, ""))
        if g0_far is None and key == K["g_tie"]:
            box = Box(last[0])
            g0_far = swap(tied(g0, box), "tensor", 2)
            last = [box.value]
    small = small_sums

    def qkv_shape(grad):
        return jnp.transpose(grad.reshape(3, width, HD), (1, 0, 2))

    home = lambda a: jnp.transpose(a, (1, 0, 2)).reshape(shape)
    return (
        home(output),
        home(input_grad),
        qkv_shape(feat_grad),
        grads_other[4],
        small[8],
        qkv_shape(grads_other[2]),
        grads_other[3],
        small[1],
        grads_other[0],
        lax.dynamic_index_in_dim(small, 16 + t[0][0], 0, keepdims=False),
        grads_other[1],
        small[0],
        jnp.stack([small[4], small[9], small[2]]),
        jnp.stack([small[5], small[10], small[3]]),
    )


def solution(mesh):
    return jax.shard_map(
        shards,
        mesh=mesh,
        in_specs=(
            P("dp", None, None, None), P("dp"), P(None, None, "tensor"), P("tensor", None), P(),
            P(None, None, "tensor"), P("tensor", None), P(), P(None, "tensor"), P("tensor"),
            P("tensor", None), P(), P(), P(), P("dp", None, None, None),
        ),
        out_specs=(
            P("dp", None, None, None), P("dp", None, None, None), P(None, None, "tensor"),
            P("tensor", None), P(), P(None, None, "tensor"), P("tensor", None), P(),
            P(None, "tensor"), P("tensor"), P("tensor", None), P(), P(), P(),
        ),
        check_vma=False,
    )
```

```python
from functools import partial

import jax
import jax.numpy as jnp
from jax import lax
from jax.experimental import pallas as pl
from jax.experimental.pallas import tpu as pltpu
from jax.sharding import PartitionSpec as P

HD = 128
EPSILON = 1e-05
NEGATIVE = -1e30
SCALE = HD**-0.5
BF = jnp.bfloat16
F32 = jnp.float32
MIB = 1 << 20
KNOBS = {'cost': 0, 'window': 'MA2', 'tail': 'OFpFOFOcFOgFrFO', 'out_tie': 'Aw', 'hs_tie': 'fq', 'rs_tie': '', 'g_tie': 'O3', 'vm': 18, 'vs': 16, 'vf': 60, 'vh': 16, 'vz': 16, 'ud_tie': 'a'}
FB = 8
GROUP = 16
HEADS = 4
RB = 16


def mm(a, b):
    return jnp.dot(a, b, preferred_element_type=F32)


def mm_nt(a, b):
    return lax.dot_general(a, b, (((1,), (1,)), ((), ())), preferred_element_type=F32)


def mm_tn(a, b):
    return lax.dot_general(a, b, (((0,), (0,)), ((), ())), preferred_element_type=F32)


def standardize(values):
    centered = values - jnp.mean(values, axis=-1, keepdims=True)
    inverse = lax.rsqrt(jnp.mean(centered * centered, axis=-1, keepdims=True) + EPSILON)
    return centered * inverse, inverse


def norm_backward(upstream, normed, inverse, gain):
    scaled = upstream * gain
    return inverse * (
        scaled
        - jnp.mean(scaled, axis=-1, keepdims=True)
        - normed * jnp.mean(scaled * normed, axis=-1, keepdims=True)
    )


def column_sum(values):
    return jnp.sum(values, axis=0, keepdims=True)


def softmax_keys(scores):
    grown = jnp.exp(scores - jnp.max(scores, axis=0, keepdims=True))
    return grown * (1.0 / jnp.sum(grown, axis=0, keepdims=True))


def gelu_parts(z):
    t = 1.0 / (1.0 + (0.3275911 * 0.7071067811865476) * jnp.abs(z))
    e = jnp.exp(-0.5 * z * z)
    poly = t * (
        0.127414796 + t * (-0.142248368 + t * (0.7107068705 + t * (-0.7265760135 + t * 0.5307027145)))
    )
    tail = poly * e
    cdf = jnp.where(z >= 0, 1.0 - tail, tail)
    return z * cdf, cdf + z * (e * 0.3989422804014327)


def masked_softmax(scores, feature_count):
    key = lax.broadcasted_iota(jnp.int32, scores.shape, 0)
    return softmax_keys(jnp.where(key < feature_count, scores, NEGATIVE)).astype(BF)


def three(w):
    return jnp.concatenate([w[0], w[1], w[2]], axis=-1)


def stacked(w):
    n = w.shape[0] // 3
    return jnp.concatenate([w[c * n : (c + 1) * n] for c in range(3)], axis=-1)


def unpacked(w):
    tall = jnp.concatenate([w[:, j * HD : (j + 1) * HD] for j in range(4)], axis=0)
    return stacked(tall)


def four_weights(fq, fq_far, near):
    tall = 3 * fq.shape[1] // 4
    packed = [(near, pl.BlockSpec((tall, 4 * HD), partial(lambda j, *_: (j, 0), j))) for j in range(2)]
    return [(fq, full(fq)), packed[0], (fq_far, full(fq_far)), packed[1]]


def wide(pieces):
    n = pieces[0].shape[0] // 4
    return jnp.concatenate(
        [jnp.concatenate([p[j * n : (j + 1) * n] for j in range(4)], axis=-1) for p in pieces], axis=0)


def live_columns(block, first, feature_count):
    values = block.astype(F32)
    index = first + lax.broadcasted_iota(jnp.int32, values.shape, 0)
    return jnp.where(index < feature_count, values, 0.0)


ANY = pl.BlockSpec(memory_space=pl.ANY)
VMEM = pl.BlockSpec(memory_space=pltpu.VMEM)


def full(a):
    zeros = (0,) * len(a.shape)
    return pl.BlockSpec(a.shape, lambda *_: zeros)


def shaped(shape, dtype=BF):
    return jax.ShapeDtypeStruct(shape, dtype)


def call(kernel, name, grid, t, ins, outs, scratch=(), vmem=KNOBS["vm"], us=1):
    t, after = t[:2], [a for a in t[2:]]
    count = 2 + len(ins)

    def body(*refs):
        kernel(*refs[:count], *refs[count + len(after) :])

    spec = pltpu.PrefetchScalarGridSpec(
        num_scalar_prefetch=2,
        grid=grid,
        in_specs=[s for _, s in ins] + [ANY] * len(after),
        out_specs=[s for _, s in outs],
        scratch_shapes=list(scratch),
    )
    return pl.pallas_call(
        body,
        grid_spec=spec,
        out_shape=[a for a, _ in outs],
        compiler_params=pltpu.CompilerParams(vmem_limit_bytes=vmem * MIB),
        cost_estimate=pl.CostEstimate(flops=us * KNOBS["cost"] * 1_000_000 + 1, bytes_accessed=1, transcendentals=0),
        name=name,
    )(*t, *[a for a, _ in ins], *after)


def pack_kernel(t_ref, d_ref, rq_ref, fo_ref, ro_ref, ub_ref, out_ref):
    width = rq_ref.shape[1]
    for c in range(3):
        out_ref[c * width : (c + 1) * width] = rq_ref[c]
    at = 3 * width
    for source in (fo_ref, ro_ref):
        for j in range(4):
            out_ref[at : at + HD] = source[:, j * HD : (j + 1) * HD]
            at += HD
    bias = [ub_ref[j * HD : (j + 1) * HD].astype(F32).reshape(1, HD) for j in range(4)]
    out_ref[at : at + 16] = jnp.concatenate(bias + [jnp.zeros((12, HD), F32)], axis=0).astype(BF)


def pack(t, rq, fo, ro, ub):
    out = shaped((3 * rq.shape[1] + 8 * HD + 16, HD))
    return call(pack_kernel, "pack", (), t, [(a, VMEM) for a in (rq, fo, ro, ub)], [(out, VMEM)], vmem=60)[0]


def pack_part(pack, what):
    rows = pack.shape[0] - 8 * HD - 16
    size, at = {"qkv": (rows, 0), "feat_out": (4 * HD, rows), "row_out": (4 * HD, rows + 4 * HD),
                "bias": (16, rows + 8 * HD)}[what]
    return pl.BlockSpec((size, HD), lambda *_: (at // size, 0))


def pack_parts(packs, what):
    return [(p, pack_part(p, what)) for p in packs]


def feature_forward_kernel(
    t_ref, d_ref, cells_ref, gains_ref, shifts_ref, w_ref, up_ref, down_ref, o0, o1, o2, o3, both_ref, qkv_scr, mix_scr
):
    feature_count, rows, width = cells_ref.shape
    padded = qkv_scr.shape[1] // rows

    @pl.when(pl.program_id(0) == 0)
    def _():
        qkv_scr[...] = jnp.zeros_like(qkv_scr)
        both_ref[: up_ref.shape[0]] = up_ref[...]
        both_ref[up_ref.shape[0] :] = down_ref[...]

    cells = cells_ref[...].astype(F32).reshape(feature_count * rows, width)
    normed, _ = standardize(cells)
    low = (normed * gains_ref[...].astype(F32)[0:1] + shifts_ref[...].astype(F32)[0:1]).astype(BF)
    qkv = mm(low, three(w_ref))
    for c in range(3):
        qkv_scr[c, 0 : feature_count * rows, :] = qkv[:, c * HD : (c + 1) * HD]
    for first in range(0, rows, GROUP):
        places = [pl.ds(r, padded, stride=rows) for r in range(first, first + GROUP)]
        parts = [[qkv_scr[c, every, :].astype(BF) for c in range(3)] for every in places]
        scores = [mm_nt(k, q) * SCALE for q, k, _ in parts]
        ps = [masked_softmax(x, feature_count) for x in scores]
        for every, p, (_, _, v) in zip(places, ps, parts):
            mix_scr[every, :] = mm_tn(p, v)
    count = o0.shape[1]
    for k, out in enumerate((o0, o1, o2, o3)):
        at = pl.multiple_of(lax.bitwise_xor(t_ref[0], k) * count, count)
        out[0] = mix_scr[pl.ds(at, count), :].astype(BF)


def feature_forward(t, cells, gains, shifts, weight, up, down, columns):
    feature_count, row_count, width = cells.shape
    padded = 4 * columns
    steps = row_count // RB
    out = (shaped((steps, columns * RB, HD)), pl.BlockSpec((1, columns * RB, HD), lambda i, t, d: (i, 0, 0)))
    return call(
        feature_forward_kernel, "feature_forward", (steps,), t,
        [(cells, pl.BlockSpec((feature_count, RB, width), lambda i, t, d: (0, i, 0)))]
        + [(a, full(a)) for a in (gains, shifts, weight, up, down)],
        [out] * 4 + [whole((up.shape[0] + down.shape[0], up.shape[1]))],
        [pltpu.VMEM((3, padded * RB, HD), F32), pltpu.VMEM((padded * RB, HD), F32)], vmem=KNOBS["vf"], us=11
    )


def column_block(array, columns):
    _, rows, width = array.shape
    return pl.BlockSpec((columns, rows, width), lambda i, t, d: (t[0], 0, 0))


def in_order(m, columns):
    steps = m.shape[0]
    halves = [m[i].reshape(columns, RB, HD) for i in range(steps)]
    return jnp.concatenate(halves, axis=1).reshape(columns * RB * steps, HD)


def row_forward_kernel(
    t_ref, d_ref, split_ref, m0, m1, m2, m3, cells_ref, f0, f1, f2, f3, r0, r1, r2, r3, w0, w1, w2, w3,
    wo_bias, wr_bias, gains_ref, shifts_ref,
    first_ref, n2_ref, qkv_ref, p_ref, o2_ref, second_ref, n3_ref, *, feature_count,
):
    columns, rows, width = cells_ref.shape
    cells = columns * rows
    side = p_ref.shape[2]
    key = lax.broadcasted_iota(jnp.int32, (side, side), 0)
    query = lax.broadcasted_iota(jnp.int32, (side, side), 1)
    same = lax.div(query, rows) == lax.div(key, rows)
    bias = jnp.where(jnp.logical_and(same, lax.rem(key, rows) < split_ref[0]), 0.0, NEGATIVE)

    gains = gains_ref[...].astype(F32)
    shifts = shifts_ref[...].astype(F32)
    stream = live_columns(cells_ref[...], t_ref[0] * columns, feature_count).reshape(cells, width)
    mixed = jnp.concatenate([in_order(m, columns) for m in (m0, m1, m2, m3)], axis=-1)
    first = stream + mm(mixed, wide((f0, f1, f2, f3))) + wo_bias[...].astype(F32)
    first_ref[...] = first
    normed, _ = standardize(first)
    low = (normed * gains[1:2] + shifts[1:2]).astype(BF)
    n2_ref[...] = low
    spans = [slice(b, b + side) for b in range(0, cells, side)]
    part = lambda h, span, c: qkv_ref[span, (3 * h + c) * HD : (3 * h + c + 1) * HD]
    weights = (w0, w1, w2, w3)
    for first_head in range(0, 4, HEADS):
        heads = range(first_head, first_head + HEADS)
        qkv_ref[:, 3 * HD * first_head : 3 * HD * (first_head + HEADS)] = mm(
            low, jnp.concatenate([stacked(weights[h]) for h in heads], axis=-1)).astype(BF)
        places = [(h, j, span) for h in heads for j, span in enumerate(spans)]
        scores = [mm_nt(part(h, span, 1), part(h, span, 0)) * SCALE + bias for h, _, span in places]
        ps = [softmax_keys(x).astype(BF) for x in scores]
        for (h, j, span), p in zip(places, ps):
            p_ref[h, j] = p
            o2_ref[span, h * HD : (h + 1) * HD] = mm_tn(p, part(h, span, 2)).astype(BF)
    second = first + mm(o2_ref[...], wide((r0, r1, r2, r3))) + wr_bias[...].astype(F32)
    second_ref[...] = second
    normed, _ = standardize(second)
    n3_ref[...] = (normed * gains[2:3] + shifts[2:3]).astype(BF)


def whole(shape, dtype=BF):
    return shaped(shape, dtype), full(shaped(shape, dtype))


def row_forward(t, split, mixed, cells, packs, wo_bias, wr_bias, gains, shifts, columns):
    feature_count, rows, width = cells.shape
    n = columns * rows
    side = 4 * rows
    ins = [(split, pl.BlockSpec(memory_space=pltpu.SMEM))] + [(m, full(m)) for m in mixed]
    ins += [(cells, column_block(cells, columns))]
    ins += pack_parts(packs, "feat_out") + pack_parts(packs, "row_out") + pack_parts(packs, "qkv")
    ins += [(a, full(a)) for a in (wo_bias, wr_bias, gains, shifts)]
    return call(
        partial(row_forward_kernel, feature_count=feature_count), "row_forward", (1,), t, ins,
        [whole((n, width), F32), whole((n, width)), whole((n, 12 * HD)), whole((4, n // side, side, side)),
         whole((n, 4 * HD)), whole((n, width), F32), whole((n, width))], us=9
    )


def hidden_pair(t_ref, n3_ref, grad_ref, ups, packs, downs, grads, bias_grads, feature_count):
    columns, rows, width = grad_ref.shape
    g3 = live_columns(grad_ref[...], t_ref[0] * columns, feature_count).reshape(columns * rows, width)
    n3, gl = n3_ref[...], g3.astype(BF)
    n3_t, gl_t = n3.T, gl.T
    hidden = ups[0].shape[1]
    up = jnp.concatenate([u[...] for u in ups], axis=-1)
    down = jnp.concatenate([d[...] for d in downs], axis=0)
    bias = jnp.concatenate([p[...].astype(F32)[j : j + 1] for p in packs for j in range(4)], axis=-1)
    ms, dzs = [], []
    step = 256
    count = 2 * hidden // step
    ahead = []

    def begin(c):
        span = slice(c * step, (c + 1) * step)
        return mm(n3, up[:, span]) + bias[:, span], mm_nt(gl, down[span])

    ahead = begin(0)
    for c in range(count):
        z, dm = ahead
        if c + 1 < count:
            ahead = begin(c + 1)
        act, slope = gelu_parts(z)
        m = act.astype(BF)
        dz = (dm * slope).astype(BF)
        j, at = divmod(c * step, hidden)
        span = slice(at, at + step)
        grads[j][:width, span] = mm(n3_t, dz).astype(BF)
        grads[j][width:, span] = mm(gl_t, m).astype(BF)
        bias_grads[j][:, span] = column_sum(dz.astype(F32))
        ms.append(m)
        dzs.append(dz)
    out = mm(jnp.concatenate(ms, axis=-1), down)
    dn3 = mm_nt(jnp.concatenate(dzs, axis=-1), up)
    return g3, out, dn3


def hidden_first_kernel(
    t_ref, d_ref, n3_ref, grad_ref, up0, up1, b0, b1, down0, down1, out_ref, dn3_ref, wg0, wg1, bg0, bg1,
    *, feature_count,
):
    _, out, dn3 = hidden_pair(
        t_ref, n3_ref, grad_ref, (up0, up1), (b0, b1), (down0, down1), (wg0, wg1), (bg0, bg1), feature_count)
    out_ref[...] = out
    dn3_ref[...] = dn3


def hidden_second_kernel(
    t_ref, d_ref, n3_ref, grad_ref, up0, up1, b0, b1, down0, down1, out_in, dn3_in, second_ref, down_bias, gains_ref,
    earlier_ref, out_ref, g2_ref, stats_ref, wg0, sent_ref, bg0, bg1, *, feature_count,
):
    tall = earlier_ref.shape[0]
    sent_ref[:tall] = earlier_ref[...]
    g3, out, dn3 = hidden_pair(
        t_ref, n3_ref, grad_ref, (up0, up1), (b0, b1), (down0, down1), (wg0, sent_ref.at[pl.ds(tall, tall)]), (bg0, bg1),
        feature_count)
    second = second_ref[...]
    out_ref[...] = (second + out_in[...] + out + down_bias[...].astype(F32)).astype(BF)
    dn3 = dn3_in[...] + dn3
    normed, inverse = standardize(second)
    g2 = g3 + norm_backward(dn3, normed, inverse, gains_ref[...].astype(F32)[2:3])
    g2_ref[...] = g2
    stats_ref[...] = rows_of([g3, g2, dn3 * normed, dn3])


def rows_of(arrays):
    return jnp.concatenate(
        [column_sum(a) for a in arrays] + [jnp.zeros((8 - len(arrays), arrays[0].shape[1]), F32)], axis=0)


def hidden_call(t, n3, grads, both, packs, columns, extra=None):
    n, width = n3.shape
    hidden = both[0].shape[1]
    ins = [(n3, full(n3)), (grads, column_block(grads, columns))]
    ins += [(a, pl.BlockSpec((width, hidden), lambda *_: (0, 0))) for a in both] + pack_parts(packs, "bias")
    ins += [(a, pl.BlockSpec((hidden, width), lambda *_: (1, 0))) for a in both]
    bias_grads = [whole((1, hidden), F32)] * 2
    if extra is None:
        kernel, name = hidden_first_kernel, "hidden_first"
        results = [whole((n, width), F32)] * 2 + [whole((2 * width, hidden))] * 2 + bias_grads
    else:
        kernel, name = hidden_second_kernel, "hidden_second"
        ins += [(a, full(a)) for a in extra]
        results = [whole((n, width)), whole((n, width), F32), whole((8, width), F32)]
        results += [whole((2 * width, hidden)), whole((4 * width, hidden))] + bias_grads
    return call(partial(kernel, feature_count=grads.shape[0]), name, (1,), t, ins, results, us=7)


def attentions_backward(blocks):
    dps = [mm_nt(v, do) for _, _, v, _, do in blocks]
    pfs = [b[3].astype(F32) for b in blocks]
    dss = [(pf * (dp - jnp.sum(dp * pf, axis=0, keepdims=True))).astype(BF) for dp, pf in zip(dps, pfs)]
    dvs = [mm(p, do) for _, _, _, p, do in blocks]
    dks = [mm(ds, b[0]) * SCALE for ds, b in zip(dss, blocks)]
    dqs = [mm_tn(ds, b[1]) * SCALE for ds, b in zip(dss, blocks)]
    return list(zip(dqs, dks, dvs))


def row_backward_kernel(
    t_ref, d_ref, g2_ref, first_ref, qkv_ref, p_ref, gains_ref, n2_ref, o2_ref, m0, m1, m2, m3, fq0, fq2,
    w0, w1, w2, w3, r0, r1, r2, r3, s0, near_ref, s2, s3, stats_ref, keep_ref, send_ref, g1_scr, dqkv_ref,
):
    width = fq0.shape[1]
    for j, weights in enumerate((fq0, fq2)):
        tall = 3 * width // 4
        for lane in range(4):
            for at, first, count in stretches(lane * tall, tall, width):
                near_ref[j * tall + at : j * tall + at + count, lane * HD : (lane + 1) * HD] = (
                    weights[first // width, first % width : first % width + count, :])
    g2 = g2_ref[...]
    cells, width = g2.shape
    side = p_ref.shape[2]
    gl2 = g2.astype(BF)
    do = mm_nt(gl2, wide((r0, r1, r2, r3))).astype(BF)
    spans = [slice(b, b + side) for b in range(0, cells, side)]
    for first in range(0, 4, 2):
        heads = range(first, first + 2)
        blocks = [
            [qkv_ref[span, (3 * h + c) * HD : (3 * h + c + 1) * HD] for c in range(3)]
            + [p_ref[h, j], do[span, HD * h : HD * (h + 1)]] for h in heads for j, span in enumerate(spans)]
        places = [(h, span) for h in heads for span in spans]
        for (h, span), parts in zip(places, attentions_backward(blocks)):
            for c, part in enumerate(parts):
                dqkv_ref[span, (3 * h + c) * HD : (3 * h + c + 1) * HD] = part.astype(BF)
    dn2 = mm_nt(dqkv_ref[...], jnp.concatenate([stacked(w) for w in (w0, w1, w2, w3)], axis=-1))
    normed, inverse = standardize(first_ref[...])
    g1 = g2 + norm_backward(dn2, normed, inverse, gains_ref[...].astype(F32)[1:2])
    columns, rows, _ = g1_scr.shape
    g1_scr[...] = g1.reshape(columns, rows, width)
    share = rows // 4
    for k, out in enumerate((s0, near_ref.at[pl.ds(6 * width // 4, columns * share)], s2, s3)):
        at = pl.multiple_of(lax.bitwise_xor(t_ref[0], k) * share, share)
        out[...] = g1_scr[:, pl.ds(at, share), :].reshape(columns * share, width).astype(BF)
    stats_ref[...] = rows_of([g1, dn2 * normed, dn2])
    mixed = [in_order(m, columns) for m in (m0, m1, m2, m3)]
    row_grads(n2_ref[...], dqkv_ref[...], gl2, o2_ref[...], g1.astype(BF), mixed, keep_ref, send_ref)


def stretches(first, count, size):
    at = 0
    while at < count:
        rows = min(count - at, size - (first + at) % size)
        yield at, first + at, rows
        at += rows


def row_grads(n2, dqkv, gl2, o2, gl1, mixed, keep_ref, send_ref):
    width = n2.shape[1]
    grad = mm(n2.T, dqkv).astype(BF)
    out_grad = mm(gl2.T, o2).astype(BF)
    feat_grad = mm(gl1.T, jnp.concatenate(mixed, axis=-1)).astype(BF)
    for h in range(4):
        out = (keep_ref, send_ref)[h % 2].at[h // 2]
        blocks = [grad[:, (3 * h + c) * HD : (3 * h + c + 1) * HD] for c in range(3)]
        blocks += [out_grad[:, HD * h : HD * (h + 1)], feat_grad[:, HD * h : HD * (h + 1)]]
        for at, first, count, lane in row_places(width):
            out[at : at + count, lane * HD : (lane + 1) * HD] = blocks[first // width][first % width : first % width + count]


def row_backward(t, g2, first, qkv, p, gains, n2, o2, mixed, fq, fq_far, packs, rows):
    n, width = g2.shape
    ins = [(a, full(a)) for a in (g2, first, qkv, p, gains, n2, o2, *mixed, fq, fq_far)]
    ins += pack_parts(packs, "qkv") + pack_parts(packs, "row_out")
    piece = whole((n // 4, width))
    return call(
        row_backward_kernel, "row_backward", (1,), t, ins,
        [piece, whole((6 * width // 4 + n // 4, width)), piece, piece, whole((8, width), F32)]
        + [whole((2, 5 * width // 4, 4 * HD))] * 2,
        [pltpu.VMEM((n // rows, rows, width), F32), pltpu.VMEM(qkv.shape, BF)], us=11,
    )


def row_places(width):
    tall = 5 * width // 4
    first = 0
    while first < 5 * width:
        count = min(width - first % width, tall - first % tall)
        yield first % tall, first, count, first // tall
        first += count


def own_rows(t_ref, cells_ref, cell_scr, share):
    feature_count, block_rows, width = cells_ref.shape
    cell_scr[0:feature_count] = cells_ref[...].astype(F32)
    cell_scr[feature_count:] = jnp.zeros_like(cell_scr[feature_count:])
    at = pl.multiple_of(lax.rem(t_ref[0], block_rows // share) * share, share)
    return cell_scr[:, pl.ds(at, share), :].reshape(cell_scr.shape[0] * share, width)


def row_block(cells, share):
    feature_count, _, width = cells.shape
    per = RB // share
    return pl.BlockSpec((feature_count, RB, width), lambda i, t, d: (0, lax.div(t[0], per), 0))


def feature_again_kernel(
    t_ref, d_ref, cells_ref, gains_ref, shifts_ref, w0, w1, w2, w3, n1_ref, qkv_ref, p_ref, cell_scr, qkv_scr
):
    feature_count = cells_ref.shape[0]
    share, padded, _ = qkv_ref.shape
    normed, _ = standardize(own_rows(t_ref, cells_ref, cell_scr, share))
    low = (normed * gains_ref[...].astype(F32)[0:1] + shifts_ref[...].astype(F32)[0:1]).astype(BF)
    n1_ref[...] = low
    packed = mm(low, jnp.concatenate([three(w0), unpacked(w1), three(w2), unpacked(w3)], axis=-1))
    for c in range(12):
        qkv_scr[c] = packed[:, c * HD : (c + 1) * HD]
    for h in range(4):
        parts = [[qkv_scr[3 * h + c, pl.ds(r, padded, stride=share), :].astype(BF) for c in range(3)] for r in range(share)]
        scores = [mm_nt(k, q) * SCALE for q, k, _ in parts]
        for r in range(share):
            for c, part in enumerate(parts[r]):
                qkv_ref[r, :, (3 * h + c) * HD : (3 * h + c + 1) * HD] = part
            p_ref[r, h] = masked_softmax(scores[r], feature_count)


def feature_again(t, cells, gains, shifts, fq, fq_far, near, columns, share):
    width = cells.shape[2]
    padded = 4 * columns
    return call(
        feature_again_kernel, "feature_again", (1,), t,
        [(cells, row_block(cells, share))] + [(a, full(a)) for a in (gains, shifts)] + four_weights(fq, fq_far, near),
        [whole((padded * share, width)), whole((share, padded, 12 * HD)), whole((share, 4, padded, padded))],
        [pltpu.VMEM((padded, RB, width), F32), pltpu.VMEM((12, padded * share, HD), F32)], vmem=KNOBS["vs"], us=4
    )


def feature_backward_kernel(
    t_ref, d_ref, r0, r1, r2, r3, f0, f1, f2, f3, qkv_ref, p_ref, n1_ref,
    g1_ref, dqkv_ref, keep0, keep1, send0, send1, low_scr, do_scr, dqkv_scr,
):
    width = g1_ref.shape[1]
    share, padded, _ = qkv_ref.shape
    for k, piece in enumerate((r0, r1, r2, r3)):
        count = piece.shape[0]
        at = pl.multiple_of(lax.bitwise_xor(t_ref[0], k) * count, count)
        low_scr[pl.ds(at, count), :] = piece[...]
        g1_ref[pl.ds(at, count), :] = piece[...].astype(F32)
    do = mm_nt(low_scr[...], wide((f0, f1, f2, f3)))
    for h in range(4):
        do_scr[h] = do[:, h * HD : (h + 1) * HD]
    n1_t = n1_ref[...].T
    for h in range(4):
        rows = [pl.ds(r, padded, stride=share) for r in range(share)]
        heads = range(h, h + HEADS) if h % HEADS == 0 else ()
        blocks = [
            [qkv_ref[r, :, (3 * g + c) * HD : (3 * g + c + 1) * HD] for c in range(3)]
            + [p_ref[r, g], do_scr[g, every, :].astype(BF)] for g in heads for r, every in enumerate(rows)]
        places = [(g, every) for g in heads for every in rows]
        for (g, every), parts in zip(places, attentions_backward(blocks)):
            for c, part in enumerate(parts):
                dqkv_scr[3 * g + c, every, :] = part
        out = ((keep0, keep1), (send0, send1))[h % 2]
        for c in range(3):
            dqkv_ref[:, (3 * h + c) * HD : (3 * h + c + 1) * HD] = dqkv_scr[3 * h + c].astype(BF)
        grad = mm(n1_t, dqkv_ref[:, 3 * HD * h : 3 * HD * (h + 1)]).astype(BF)
        for c in range(3):
            out[h // 2][c * width : (c + 1) * width, :] = grad[:, c * HD : (c + 1) * HD]


def feature_backward(t, pieces, packs, qkv, p, n1):
    share, _, padded, _ = p.shape
    width = pieces[0].shape[1]
    cells = share * padded
    return call(
        feature_backward_kernel, "feature_backward", (1,), t,
        [(a, pl.BlockSpec(pieces[0].shape, partial(lambda j, *_: (j, 0), 0 if k != 1 else a.shape[0] // pieces[0].shape[0] - 1)))
         for k, a in enumerate(pieces)] + pack_parts(packs, "feat_out") + [(a, full(a)) for a in (qkv, p, n1)],
        [whole((cells, width), F32), whole((cells, 12 * HD))] + [whole((3 * width, HD))] * 4,
        [pltpu.VMEM((cells, width), BF), pltpu.VMEM((4, cells, HD), F32), pltpu.VMEM((12, cells, HD), F32)], us=11
    )


def feature_input_kernel(
    t_ref, d_ref, cells_ref, g1_ref, dqkv_ref, gains_ref, w0, w1, w2, w3, stats_a, stats_b, b0, b1, b2, b3,
    out_ref, stats_ref, cell_scr, sums_scr,
):
    cells, width = g1_ref.shape
    share = cells // cell_scr.shape[0]
    normed, inverse = standardize(own_rows(t_ref, cells_ref, cell_scr, share))
    dn1 = mm_nt(dqkv_ref[...], jnp.concatenate([three(w0), unpacked(w1), three(w2), unpacked(w3)], axis=-1))
    g0 = g1_ref[...] + norm_backward(dn1, normed, inverse, gains_ref[...].astype(F32)[0:1])
    out_ref[...] = g0[: out_ref.shape[0]].astype(BF)
    sums_scr[0:8] = stats_a[...]
    sums_scr[8:16] = stats_b[...]
    sums_scr[4:5] = column_sum(dn1 * normed)
    sums_scr[5:6] = column_sum(dn1)
    sums_scr[16:32] = jnp.zeros((16, width), F32)
    for k, row in enumerate((b0, b1, b2, b3)):
        sums_scr[pl.ds(16 + lax.bitwise_xor(t_ref[0], k), 1), :] = row[...]
    for j in range(4):
        stats_ref[32 * j : 32 * (j + 1)] = sums_scr[:, j * HD : (j + 1) * HD]


def feature_input(t, cells, g1, dqkv, gains, fq, fq_far, near, sums, share):
    count, width = g1.shape
    kept = (cells.shape[0] + 1) // 2 * 2 * share
    ins = [(cells, row_block(cells, share))] + [(a, full(a)) for a in (g1, dqkv, gains)]
    ins += four_weights(fq, fq_far, near) + [(a, full(a)) for a in sums]
    return call(
        feature_input_kernel, "feature_input", (1,), t, ins, [whole((kept, width)), whole((128, HD), F32)],
        [pltpu.VMEM((count // share, RB, width), F32), pltpu.VMEM((32, width), F32)], vmem=KNOBS["vs"], us=2,
    )


def pair_kernel(t_ref, d_ref, own, far, out_ref):
    out_ref[: own.shape[0]] = own[...]
    out_ref[own.shape[0] :] = far[...]


def pair(t, own, far):
    return call(pair_kernel, "pair", (), t, [(own, VMEM), (far, VMEM)], [(shaped((2 * own.shape[0], own.shape[1])), VMEM)], vmem=12)[0]


def columns_home_kernel(t_ref, d_ref, p0, p1, p2, p3, out_ref):
    for k, piece in enumerate((p0, p1, p2, p3)):

        @pl.when(pl.program_id(0) == lax.bitwise_xor(t_ref[0], k))
        def _():
            out_ref[...] = piece[...].reshape(out_ref.shape)


def columns_home(t, own, far, near, feature_count, rows):
    count, width = own.shape
    columns = count // rows
    block = lambda i: pl.BlockSpec((count, width), lambda *_: (i, 0))
    return call(
        columns_home_kernel, "columns_home", (4,), t,
        [(own, block(0)), (near, block(0)), (far, block(0)), (near, block(1))],
        [(shaped((feature_count, rows, width)), pl.BlockSpec((columns, rows, width), lambda i, t, d: (i, 0, 0)))], vmem=KNOBS["vh"],
    )[0]


def rows_home_kernel(t_ref, d_ref, p0, p1, p2, p3, out_ref, scr):
    columns, rows, width = scr.shape
    share = rows // 4
    for k, piece in enumerate((p0, p1, p2, p3)):
        at = pl.multiple_of(lax.bitwise_xor(t_ref[0], k) * share, share)
        scr[:, pl.ds(at, share), :] = piece[...].astype(F32).reshape(columns, share, width)
    out_ref[...] = scr[...].astype(BF)


def rows_home(t, own, far, near, feature_count, rows):
    count, width = own.shape
    share = rows // 4
    steps = 5
    columns = count // share // steps
    block = lambda first: pl.BlockSpec((columns * share, width), lambda i, t, d: (first + i, 0))
    return call(
        rows_home_kernel, "rows_home", (steps,), t,
        [(own, block(0)), (near, block(0)), (far, block(0)), (near, block(steps))],
        [(shaped((feature_count, rows, width)), pl.BlockSpec((columns, rows, width), lambda i, t, d: (i, 0, 0)))],
        [pltpu.VMEM((columns, rows, width), F32)], vmem=KNOBS["vh"],
    )[0]


def swap(values, axis, mask):
    count = lax.axis_size(axis)
    return lax.ppermute(values, axis, [(i, i ^ mask) for i in range(count)])


def gather_groups(own):
    far = swap(own, "tensor", 2)
    return own, swap(own, "tensor", 1), far, swap(far, "tensor", 1)


class Box:
    def __init__(self, value):
        self.value = value


def tied(values, *boxes):
    many = isinstance(values, tuple)
    values = values if many else (values,)
    out = lax.optimization_barrier((*values, *[b.value for b in boxes]))
    for box, value in zip(boxes, out[len(values) :]):
        box.value = value
    return out[: len(values)] if many else out[0]


def dp_masks():
    masks, mask = [], 1
    while mask < lax.axis_size("dp"):
        masks.append(mask)
        mask *= 2
    return masks


def digit(d_ref, mask):
    return lax.rem(lax.div(d_ref[0], mask), 2)


def halves(d_ref, mask, rows):
    side = digit(d_ref, mask)
    return [pl.multiple_of(s * rows, rows) for s in (side, 1 - side)]


def added(a, b):
    return a.astype(F32) + b.astype(F32)


def merge(name, kernel, t, ins, outs, scratch=(), vmem=16):
    return call(kernel, name, (), t, [(a, VMEM) for a in ins], [(shaped(o), VMEM) for o in outs], scratch, vmem=vmem)


def first_halves(t, hg0, hg2, row_keep, got, row_got, masks):
    hidden = hg0.shape[0] // 2
    half = row_keep.shape[1] // 2
    rows, width = hidden + half, hg0.shape[1]

    def kernel(t_ref, d_ref, g0, g2, keep, r, row_r, ak, as_, bk, bs, scr):
        for group, mine in enumerate((g0, g2)):
            for which, (kept, sent, mask) in enumerate(((ak, as_, masks[0]), (bk, bs, masks[1]))):
                at = which * hidden
                scr[:hidden] = added(mine[at : at + hidden], r[2 * hidden * group + at : 2 * hidden * group + at + hidden])
                at = which * half
                scr[hidden:] = added(keep[group, at : at + half], row_r[group, at : at + half])
                for out, first in zip((kept, sent), halves(d_ref, mask, rows // 2)):
                    out[group] = scr[pl.ds(first, rows // 2), :].astype(BF)

    return merge("ab_first", kernel, t, (hg0, hg2, row_keep, got, row_got), [(2, rows // 2, width)] * 4,
                 [pltpu.VMEM((rows, width), F32)], vmem=20)


def second_halves(t, a, ar, b, br, masks):
    _, rows, width = a.shape

    def kernel(t_ref, d_ref, a, ar, b, br, ak, as_, bk, bs):
        for x, y, kept, sent, mask in ((a, ar, ak, as_, masks[1]), (b, br, bk, bs, masks[0])):
            for out, first in zip((kept, sent), halves(d_ref, mask, rows // 2)):
                span = (slice(None), pl.ds(first, rows // 2), slice(None))
                out[...] = added(x[span], y[span]).astype(BF)

    return merge("ab_second", kernel, t, (a, ar, b, br), [(2, rows // 2, width)] * 4)


def groups_apart(t, a, ar, b, br):
    _, rows, width = a.shape

    def kernel(t_ref, d_ref, a, ar, b, br, kept, sent):
        for group, out in enumerate((kept, sent)):
            out[:rows] = added(a[group], ar[group]).astype(BF)
            out[rows:] = added(b[group], br[group]).astype(BF)

    return merge("ab_groups", kernel, t, (a, ar, b, br), [(2 * rows, width)] * 2)


def sums(t, k, r):
    def kernel(t_ref, d_ref, k, r, out):
        out[...] = added(k[...], r[...]).astype(BF)

    return merge("sums", kernel, t, (k, r), [k.shape])


def sums_apart(t, k, r):
    rows, width = k.shape[0] // 2, k.shape[1]

    def kernel(t_ref, d_ref, k, r, a, b):
        a[...] = added(k[:rows], r[:rows]).astype(BF)
        b[...] = added(k[rows:], r[rows:]).astype(BF)

    return merge("ab_apart", kernel, t, (k, r), [(rows, width)] * 2)


def joins(t, pairs, masks):
    def kernel(t_ref, d_ref, *refs):
        for j, mask in enumerate(masks):
            own, other, out = refs[2 * j], refs[2 * j + 1], refs[2 * len(masks) + j]
            for source, first in zip((own, other), halves(d_ref, mask, own.shape[0])):
                out[pl.ds(first, own.shape[0]), :] = source[...]

    return merge("joins", kernel, t, [a for p in pairs for a in p], [(2 * p[0].shape[0], p[0].shape[1]) for p in pairs])


def feature_groups(t, own, got, mine, theirs):
    rows, width = own[0].shape
    more = mine.shape[0]

    def kernel(t_ref, d_ref, a0, a2, b0, b2, sa, sb, kept, sent):
        small = added(sa[...], sb[...]).astype(BF)
        for out, a, b in ((kept, a0, b0), (sent, a2, b2)):
            out[:rows] = added(a[...], b[...]).astype(BF)
            out[rows:] = small

    return merge("f_groups", kernel, t, (*own, *got, mine, theirs), [(rows + more, width)] * 2)


def half_sums(t, k, r, mask):
    rows, width = k.shape[0] // 2, k.shape[1]

    def kernel(t_ref, d_ref, k, r, kept, sent):
        for out, first in zip((kept, sent), halves(d_ref, mask, rows)):
            span = (pl.ds(first, rows), slice(None))
            out[...] = added(k[span], r[span]).astype(BF)

    return merge("f_half", kernel, t, (k, r), [(rows, width)] * 2)


def joined(d_ref, own, other, mask, scr):
    rows = own.shape[0]
    side = digit(d_ref, mask)
    for source, place in ((own, side), (other, 1 - side)):
        scr[pl.ds(pl.multiple_of(place * rows, rows), rows), :] = source[...].astype(F32)


def finish_kernel(t_ref, d_ref, a0, a1, b0, b1, up_ref, down_ref, qkv_ref, row_out_ref, feat_out_ref, scr_a, scr_b, tall, *, masks):
    joined(d_ref, a0, a1, masks[0], scr_a)
    joined(d_ref, b0, b1, masks[1], scr_b)
    width = up_ref.shape[0]
    half = scr_a.shape[0] - width
    up_ref[...] = scr_a[0:width]
    down_ref[...] = scr_b[0:width].T
    for at, first, count, lane in row_places(width):
        for scr, low, high in ((scr_a, 0, half), (scr_b, half, 2 * half)):
            begin, end = max(at, low), min(at + count, high)
            if begin < end:
                to = first + begin - at
                tall[to : to + end - begin, :] = scr[width + begin - low : width + end - low, lane * HD : (lane + 1) * HD]
    qkv_ref[...] = tall[0 : 3 * width]
    row_out_ref[...] = tall[3 * width : 4 * width].T
    feat_out_ref[...] = tall[4 * width : 5 * width].T


def finish(t, a, b, masks, width):
    rows, w = a[0].shape
    scr = pltpu.VMEM((2 * rows, w), F32)
    outs = [shaped(s, F32) for s in ((width, w), (w, width), (3 * width, HD), (HD, width), (HD, width))]
    return call(
        partial(finish_kernel, masks=masks), "finish", (), t,
        [(x, VMEM) for x in (*a, *b)], [(o, VMEM) for o in outs],
        [scr, scr, pltpu.VMEM((5 * width, HD), F32)], vmem=KNOBS["vz"])


def finish_feature_kernel(
    t_ref, d_ref, own, other, qkv_ref, feat_bias, row_bias, up_bias, down_bias, gains, shifts, scr, sums, *, mask
):
    joined(d_ref, own, other, mask, scr)
    rows = qkv_ref.shape[0]
    qkv_ref[...] = scr[0:rows]
    tall = sums.shape[0]
    for j in range(4):
        sums[:, j * HD : (j + 1) * HD] = scr[rows + j * tall : rows + (j + 1) * tall]
    down_bias[...] = sums[0:1]
    row_bias[...] = sums[1:2]
    feat_bias[...] = sums[8:9]
    up_bias[...] = sums[pl.ds(16 + t_ref[0], 1), :]
    for out, places in ((gains, (4, 9, 2)), (shifts, (5, 10, 3))):
        for i, place in enumerate(places):
            out[i : i + 1] = sums[place : place + 1]


def finish_feature(t, own, other, mask, width, small):
    rows, w = own.shape
    return call(
        partial(finish_feature_kernel, mask=mask), "finish_feature", (), t, [(own, VMEM), (other, VMEM)],
        [(shaped((3 * width, w), F32), VMEM)] + [(shaped((n, width), F32), VMEM) for n in (1, 1, 1, 1, 3, 3)],
        [pltpu.VMEM((2 * rows, w), F32), pltpu.VMEM((small, width), F32)], vmem=16)


def shards(
    table_cells, splits, feat_qkv, feat_out, feat_out_bias, row_qkv, row_out, row_out_bias,
    up_weight, up_bias, down_weight, down_bias, norm_gains, norm_biases, cotangent,
):
    shape = table_cells.shape
    _, row_count, feature_count, width = shape
    share = row_count // 4
    columns = -(-feature_count // (4 * FB)) * FB
    t = tuple(lax.axis_index(a).astype(jnp.int32).reshape(1) for a in ("tensor", "dp"))
    masks = dp_masks()
    cells = jnp.transpose(table_cells[0], (1, 0, 2))
    grads = jnp.transpose(cotangent[0], (1, 0, 2))
    fob, rob, dnb = (b.reshape(1, width) for b in (feat_out_bias, row_out_bias, down_bias))
    fq = jnp.transpose(feat_qkv, (1, 0, 2))
    rq = jnp.transpose(row_qkv, (1, 0, 2))

    near, far = masks[:2], masks[2:]
    over = lambda v, mask: swap(v, "tensor", 2) if mask == "x" else swap(v, "dp", mask)
    core = lambda v: swap(v, "tensor", 1)

    own = pack(t, rq, feat_out, row_out, up_bias)
    own_far = swap(own, "tensor", 2)
    *mixed, both = feature_forward(t, cells, norm_gains, norm_biases, fq, up_weight, down_weight, columns)
    kept = Box(mixed[0])
    own_far = tied(own_far, kept)
    packs = own, core(own), own_far, core(own_far)
    mixed = [kept.value] + [swap(mixed[k], "tensor", k) for k in (1, 2, 3)]
    a1, a2, a3 = Box(mixed[1]), Box(mixed[2]), Box(mixed[3])
    both_far = swap({"c": lambda: tied(both, a1, a2, a3), "a": lambda: tied(both, a2, a3), "2": lambda: tied(both, a2), "": lambda: both}[KNOBS["ud_tie"]](), "tensor", 2)
    mixed[1:] = a1.value, a2.value, a3.value

    first, n2, row_packed, row_p, o2, second, n3 = row_forward(
        t, splits, mixed, cells, packs, fob, rob, norm_gains, norm_biases, columns)
    out_a, dn3_a, hg0, hg1, bg0, bg1 = hidden_call(t, n3, grads, (both, core(both)), packs[:2], columns)
    kept, fq_kept = Box(out_a), Box(hg0)
    both_far = tied(both_far, kept)
    fq_far = swap(tied(fq, fq_kept), "tensor", 2)
    hg0 = fq_kept.value
    out_f, g2, stats_a, hg2, hidden_send, bg2, bg3 = hidden_call(
        t, n3, grads, (both_far, core(both_far)), packs[2:], columns,
        [kept.value, dn3_a, second, dnb, norm_gains, hg1])
    fq_box = Box(fq_far)
    if KNOBS["hs_tie"] == "fq":
        hidden_got = core(tied(hidden_send, fq_box))
    fq_far = fq_box.value
    s0, near_send, s2, s3, stats_b, row_keep, row_send = row_backward(
        (*t, out_f), g2, first, row_packed, row_p, norm_gains, n2, o2, mixed, fq, fq_far, packs, row_count)
    pieces = [s0, core(near_send), swap(s2, "tensor", 2), swap(s3, "tensor", 3)]
    near_got = pieces[1]
    K = KNOBS
    boxes = {"s0": Box(s0), "rs": Box(row_send), "near": Box(near_got)}
    if K["hs_tie"] != "fq":
        hidden_got = core(tied(hidden_send, boxes[K["hs_tie"]]) if K["hs_tie"] else hidden_send)
    row_got = core(tied(row_send, boxes[K["rs_tie"]]) if K["rs_tie"] else boxes["rs"].value)
    pieces[0] = boxes["s0"].value
    pieces[1] = near_got = boxes["near"].value

    last = [s0]
    boxes.update(out=Box(out_f), w=Box(pieces[3]), w2=Box(pieces[2]))
    out_far = None
    if K["out_tie"] == "s0":
        out_far = swap(tied(out_f, boxes["s0"]), "tensor", 2)
        pieces[0] = boxes["s0"].value
    if K["out_tie"] == "hs":
        out_far = swap(out_f, "tensor", 2)
    for what in K["window"]:
        if what == "A":
            n1, feat_packed, feat_p = feature_again(
                (*t, *last), cells, norm_gains, norm_biases, fq, fq_far, near_got, columns, share)
            last = [feat_p]
        elif what == "M":
            ak, a_sent, bk, b_sent = first_halves((*t, *last), hg0, hg2, row_keep, hidden_got, row_got, near)
            last = [ak]
            ar, br = over(a_sent, near[0]), over(b_sent, near[1])
        else:
            last = [*last, pieces[2], pieces[3]]
    if K["out_tie"] in ("w", "Aw"):
        after = [Box(feat_p)] if K["out_tie"] == "Aw" else []
        out_far = swap(tied(out_f, boxes["w"], boxes["w2"], *after), "tensor", 2)
        if after:
            feat_p = after[0].value
            last = [feat_p]
        pieces[2:] = boxes["w2"].value, boxes["w"].value

    g1, dqkv_f, f0, f2, f1, f3 = feature_backward((*t, *last), pieces, packs, feat_packed, feat_p, n1)
    g0, small = feature_input(
        t, cells, g1, dqkv_f, norm_gains, fq, fq_far, near_got, (stats_a, stats_b, bg0, bg1, bg2, bg3), share)
    f_got = core(f1), core(f3)
    small_got = core(small)
    last = [small]

    state = {"O": 0, "F": 0}
    grads_other = feat_grad = None

    def step_other(last):
        nonlocal ak, ar, bk, br, ab, abr, grads_other
        here = state["O"]
        tt = (*t, *last)
        if here == 0:
            ak, a_sent, bk, b_sent = out = second_halves(tt, ak, ar, bk, br, near)
            ar, br = over(a_sent, near[1]), over(b_sent, near[0])
        elif here == 1:
            ab, sent = out = groups_apart(tt, ak, ar, bk, br)
            abr = over(sent, "x")
        elif here < 2 + len(far):
            ab, = out = sums(tt, ab, abr)
            abr = over(ab, far[here - 2])
        elif here == 2 + len(far):
            ak, bk = out = sums_apart(tt, ab, abr)
            ar, br = over(ak, near[1]), over(bk, near[0])
        elif here == 3 + len(far):
            ak, bk = out = joins(tt, ((ak, ar), (bk, br)), (near[1], near[0]))
            ar, br = over(ak, near[0]), over(bk, near[1])
        else:
            grads_other = out = finish(tt, (ak, ar), (bk, br), near, width)
        state["O"] += 1
        return out[:1]

    def step_feature(last):
        nonlocal fk, fr, feat_grad, small_sums
        here = state["F"]
        tt = (*t, *last)
        if here == 0:
            fk, sent = out = feature_groups(tt, (f0, f2), f_got, small, small_got)
            fr = over(sent, "x")
        elif here < 3:
            fk, sent = out = half_sums(tt, fk, fr, near[here - 1])
            fr = over(sent, near[here - 1])
        elif here < 3 + len(far):
            fk, = out = sums(tt, fk, fr)
            fr = over(fk, far[here - 3])
        elif here == 3 + len(far):
            fk, = out = sums(tt, fk, fr)
            fr = over(fk, near[1])
        elif here == 4 + len(far):
            fk, = out = joins(tt, ((fk, fr),), (near[1],))
            fr = over(fk, near[0])
        else:
            feat_grad, *small_sums = out = finish_feature(tt, fk, fr, near[0], width, small.shape[0] // 4)
        state["F"] += 1
        return out[:1]

    ab = abr = fk = fr = small_sums = g0_far = None
    steps = list(K["tail"])
    while steps or grads_other is None or feat_grad is None:
        what = steps.pop(0) if steps else ("O" if grads_other is None else "F")
        if what == "O" and grads_other is None:
            last = step_other(last)
        elif what == "F" and feat_grad is None:
            last = step_feature(last)
        elif what == "p":
            out_pair = pair((*t, *last), out_f, out_far)
            out_near = core(out_pair)
            last = [out_pair]
        elif what == "c":
            output = columns_home((*t, *last), out_f, out_far, out_near, feature_count, row_count)
            last = [output]
        elif what == "g":
            g0_pair = pair((*t, *last), g0, g0_far)
            g0_near = core(g0_pair)
            last = [g0_pair]
        elif what == "r":
            input_grad = rows_home((*t, *last), g0, g0_far, g0_near, feature_count, row_count)
            last = [input_grad]
        key = what + str(state.get(what, ""))
        if g0_far is None and key == K["g_tie"]:
            box = Box(last[0])
            g0_far = swap(tied(g0, box), "tensor", 2)
            last = [box.value]
    feat_bias, row_bias, up_bias_grad, down_bias_grad, gain_grad, shift_grad = small_sums

    def qkv_shape(grad):
        return jnp.transpose(grad.reshape(3, width, HD), (1, 0, 2))

    home = lambda a: jnp.transpose(a, (1, 0, 2)).reshape(shape)
    return (
        home(output),
        home(input_grad),
        qkv_shape(feat_grad),
        grads_other[4],
        feat_bias.reshape(width),
        qkv_shape(grads_other[2]),
        grads_other[3],
        row_bias.reshape(width),
        grads_other[0],
        up_bias_grad.reshape(up_bias.shape),
        grads_other[1],
        down_bias_grad.reshape(width),
        gain_grad,
        shift_grad,
    )


def solution(mesh):
    return jax.shard_map(
        shards,
        mesh=mesh,
        in_specs=(
            P("dp", None, None, None), P("dp"), P(None, None, "tensor"), P("tensor", None), P(),
            P(None, None, "tensor"), P("tensor", None), P(), P(None, "tensor"), P("tensor"),
            P("tensor", None), P(), P(), P(), P("dp", None, None, None),
        ),
        out_specs=(
            P("dp", None, None, None), P("dp", None, None, None), P(None, None, "tensor"),
            P("tensor", None), P(), P(None, None, "tensor"), P("tensor", None), P(),
            P(None, "tensor"), P("tensor"), P("tensor", None), P(), P(), P(),
        ),
        check_vma=False,
    )
```

```python
from functools import partial

import jax
import jax.numpy as jnp
from jax import lax
from jax.experimental import pallas as pl
from jax.experimental.pallas import tpu as pltpu
from jax.sharding import PartitionSpec as P

HD = 128
EPSILON = 1e-05
NEGATIVE = -1e30
SCALE = HD**-0.5
BF = jnp.bfloat16
F32 = jnp.float32
MIB = 1 << 20
KNOBS = {'cost': 0, 'window': 'MA2', 'tail': 'OFpFOFOcFOgFrFO', 'out_tie': 'Aw', 'hs_tie': 'fq', 'rs_tie': '', 'g_tie': 'O3', 'vm': 18, 'vs': 16, 'vf': 60, 'vh': 16, 'vz': 16, 'ud_tie': 'a'}
FB = 8
GROUP = 16
HEADS = 4
RB = 16


def mm(a, b):
    return jnp.dot(a, b, preferred_element_type=F32)


def mm_nt(a, b):
    return lax.dot_general(a, b, (((1,), (1,)), ((), ())), preferred_element_type=F32)


def mm_tn(a, b):
    return lax.dot_general(a, b, (((0,), (0,)), ((), ())), preferred_element_type=F32)


def standardize(values):
    centered = values - jnp.mean(values, axis=-1, keepdims=True)
    inverse = lax.rsqrt(jnp.mean(centered * centered, axis=-1, keepdims=True) + EPSILON)
    return centered * inverse, inverse


def norm_backward(upstream, normed, inverse, gain):
    scaled = upstream * gain
    return inverse * (
        scaled
        - jnp.mean(scaled, axis=-1, keepdims=True)
        - normed * jnp.mean(scaled * normed, axis=-1, keepdims=True)
    )


def column_sum(values):
    return jnp.sum(values, axis=0, keepdims=True)


def softmax_keys(scores):
    grown = jnp.exp(scores - jnp.max(scores, axis=0, keepdims=True))
    return grown * (1.0 / jnp.sum(grown, axis=0, keepdims=True))


def gelu_parts(z):
    t = 1.0 / (1.0 + (0.3275911 * 0.7071067811865476) * jnp.abs(z))
    e = jnp.exp(-0.5 * z * z)
    poly = t * (
        0.127414796 + t * (-0.142248368 + t * (0.7107068705 + t * (-0.7265760135 + t * 0.5307027145)))
    )
    tail = poly * e
    cdf = jnp.where(z >= 0, 1.0 - tail, tail)
    return z * cdf, cdf + z * (e * 0.3989422804014327)


def masked_softmax(scores, feature_count):
    key = lax.broadcasted_iota(jnp.int32, scores.shape, 0)
    return softmax_keys(jnp.where(key < feature_count, scores, NEGATIVE)).astype(BF)


def three(w):
    return jnp.concatenate([w[0], w[1], w[2]], axis=-1)


def stacked(w):
    n = w.shape[0] // 3
    return jnp.concatenate([w[c * n : (c + 1) * n] for c in range(3)], axis=-1)


def unpacked(w):
    tall = jnp.concatenate([w[:, j * HD : (j + 1) * HD] for j in range(4)], axis=0)
    return stacked(tall)


def four_weights(fq, fq_far, near):
    tall = 3 * fq.shape[1] // 4
    packed = [(near, pl.BlockSpec((tall, 4 * HD), partial(lambda j, *_: (j, 0), j))) for j in range(2)]
    return [(fq, full(fq)), packed[0], (fq_far, full(fq_far)), packed[1]]


def wide(pieces):
    n = pieces[0].shape[0] // 4
    return jnp.concatenate(
        [jnp.concatenate([p[j * n : (j + 1) * n] for j in range(4)], axis=-1) for p in pieces], axis=0)


def live_columns(block, first, feature_count):
    values = block.astype(F32)
    index = first + lax.broadcasted_iota(jnp.int32, values.shape, 0)
    return jnp.where(index < feature_count, values, 0.0)


ANY = pl.BlockSpec(memory_space=pl.ANY)
VMEM = pl.BlockSpec(memory_space=pltpu.VMEM)


def full(a):
    zeros = (0,) * len(a.shape)
    return pl.BlockSpec(a.shape, lambda *_: zeros)


def shaped(shape, dtype=BF):
    return jax.ShapeDtypeStruct(shape, dtype)


def call(kernel, name, grid, t, ins, outs, scratch=(), vmem=KNOBS["vm"], us=1):
    t, after = t[:2], [a for a in t[2:]]
    count = 2 + len(ins)

    def body(*refs):
        kernel(*refs[:count], *refs[count + len(after) :])

    spec = pltpu.PrefetchScalarGridSpec(
        num_scalar_prefetch=2,
        grid=grid,
        in_specs=[s for _, s in ins] + [ANY] * len(after),
        out_specs=[s for _, s in outs],
        scratch_shapes=list(scratch),
    )
    return pl.pallas_call(
        body,
        grid_spec=spec,
        out_shape=[a for a, _ in outs],
        compiler_params=pltpu.CompilerParams(vmem_limit_bytes=vmem * MIB),
        cost_estimate=pl.CostEstimate(flops=us * KNOBS["cost"] * 1_000_000 + 1, bytes_accessed=1, transcendentals=0),
        name=name,
    )(*t, *[a for a, _ in ins], *after)


def pack_kernel(t_ref, d_ref, rq_ref, fo_ref, ro_ref, ub_ref, out_ref):
    width = rq_ref.shape[1]
    for c in range(3):
        out_ref[c * width : (c + 1) * width] = rq_ref[c]
    at = 3 * width
    for source in (fo_ref, ro_ref):
        for j in range(4):
            out_ref[at : at + HD] = source[:, j * HD : (j + 1) * HD]
            at += HD
    bias = [ub_ref[j * HD : (j + 1) * HD].astype(F32).reshape(1, HD) for j in range(4)]
    out_ref[at : at + 16] = jnp.concatenate(bias + [jnp.zeros((12, HD), F32)], axis=0).astype(BF)


def pack(t, rq, fo, ro, ub):
    out = shaped((3 * rq.shape[1] + 8 * HD + 16, HD))
    return call(pack_kernel, "pack", (), t, [(a, VMEM) for a in (rq, fo, ro, ub)], [(out, VMEM)], vmem=60)[0]


def pack_part(pack, what):
    rows = pack.shape[0] - 8 * HD - 16
    size, at = {"qkv": (rows, 0), "feat_out": (4 * HD, rows), "row_out": (4 * HD, rows + 4 * HD),
                "bias": (16, rows + 8 * HD)}[what]
    return pl.BlockSpec((size, HD), lambda *_: (at // size, 0))


def pack_parts(packs, what):
    return [(p, pack_part(p, what)) for p in packs]


def feature_forward_kernel(
    t_ref, d_ref, cells_ref, gains_ref, shifts_ref, w_ref, up_ref, down_ref, o0, o1, o2, o3, both_ref, qkv_scr, mix_scr
):
    feature_count, rows, width = cells_ref.shape
    padded = qkv_scr.shape[1] // rows

    @pl.when(pl.program_id(0) == 0)
    def _():
        qkv_scr[...] = jnp.zeros_like(qkv_scr)
        both_ref[: up_ref.shape[0]] = up_ref[...]
        both_ref[up_ref.shape[0] :] = down_ref[...]

    cells = cells_ref[...].astype(F32).reshape(feature_count * rows, width)
    normed, _ = standardize(cells)
    low = (normed * gains_ref[...].astype(F32)[0:1] + shifts_ref[...].astype(F32)[0:1]).astype(BF)
    qkv = mm(low, three(w_ref))
    for c in range(3):
        qkv_scr[c, 0 : feature_count * rows, :] = qkv[:, c * HD : (c + 1) * HD]
    for first in range(0, rows, GROUP):
        places = [pl.ds(r, padded, stride=rows) for r in range(first, first + GROUP)]
        parts = [[qkv_scr[c, every, :].astype(BF) for c in range(3)] for every in places]
        scores = [mm_nt(k, q) * SCALE for q, k, _ in parts]
        ps = [masked_softmax(x, feature_count) for x in scores]
        for every, p, (_, _, v) in zip(places, ps, parts):
            mix_scr[every, :] = mm_tn(p, v)
    count = o0.shape[1]
    for k, out in enumerate((o0, o1, o2, o3)):
        at = pl.multiple_of(lax.bitwise_xor(t_ref[0], k) * count, count)
        out[0] = mix_scr[pl.ds(at, count), :].astype(BF)


def feature_forward(t, cells, gains, shifts, weight, up, down, columns):
    feature_count, row_count, width = cells.shape
    padded = 4 * columns
    steps = row_count // RB
    out = (shaped((steps, columns * RB, HD)), pl.BlockSpec((1, columns * RB, HD), lambda i, t, d: (i, 0, 0)))
    return call(
        feature_forward_kernel, "feature_forward", (steps,), t,
        [(cells, pl.BlockSpec((feature_count, RB, width), lambda i, t, d: (0, i, 0)))]
        + [(a, full(a)) for a in (gains, shifts, weight, up, down)],
        [out] * 4 + [whole((up.shape[0] + down.shape[0], up.shape[1]))],
        [pltpu.VMEM((3, padded * RB, HD), F32), pltpu.VMEM((padded * RB, HD), F32)], vmem=KNOBS["vf"], us=11
    )


def column_block(array, columns):
    _, rows, width = array.shape
    return pl.BlockSpec((columns, rows, width), lambda i, t, d: (t[0], 0, 0))


def in_order(m, columns):
    steps = m.shape[0]
    halves = [m[i].reshape(columns, RB, HD) for i in range(steps)]
    return jnp.concatenate(halves, axis=1).reshape(columns * RB * steps, HD)


def row_forward_kernel(
    t_ref, d_ref, split_ref, m0, m1, m2, m3, cells_ref, f0, f1, f2, f3, r0, r1, r2, r3, w0, w1, w2, w3,
    wo_bias, wr_bias, gains_ref, shifts_ref,
    first_ref, n2_ref, qkv_ref, p_ref, o2_ref, second_ref, n3_ref, *, feature_count,
):
    columns, rows, width = cells_ref.shape
    cells = columns * rows
    side = p_ref.shape[2]
    key = lax.broadcasted_iota(jnp.int32, (side, side), 0)
    query = lax.broadcasted_iota(jnp.int32, (side, side), 1)
    same = lax.div(query, rows) == lax.div(key, rows)
    bias = jnp.where(jnp.logical_and(same, lax.rem(key, rows) < split_ref[0]), 0.0, NEGATIVE)

    gains = gains_ref[...].astype(F32)
    shifts = shifts_ref[...].astype(F32)
    stream = live_columns(cells_ref[...], t_ref[0] * columns, feature_count).reshape(cells, width)
    mixed = jnp.concatenate([in_order(m, columns) for m in (m0, m1, m2, m3)], axis=-1)
    first = stream + mm(mixed, wide((f0, f1, f2, f3))) + wo_bias[...].astype(F32)
    first_ref[...] = first
    normed, _ = standardize(first)
    low = (normed * gains[1:2] + shifts[1:2]).astype(BF)
    n2_ref[...] = low
    spans = [slice(b, b + side) for b in range(0, cells, side)]
    part = lambda h, span, c: qkv_ref[span, (3 * h + c) * HD : (3 * h + c + 1) * HD]
    weights = (w0, w1, w2, w3)
    for first_head in range(0, 4, HEADS):
        heads = range(first_head, first_head + HEADS)
        qkv_ref[:, 3 * HD * first_head : 3 * HD * (first_head + HEADS)] = mm(
            low, jnp.concatenate([stacked(weights[h]) for h in heads], axis=-1)).astype(BF)
        places = [(h, j, span) for h in heads for j, span in enumerate(spans)]
        scores = [mm_nt(part(h, span, 1), part(h, span, 0)) * SCALE + bias for h, _, span in places]
        ps = [softmax_keys(x).astype(BF) for x in scores]
        for (h, j, span), p in zip(places, ps):
            p_ref[h, j] = p
            o2_ref[span, h * HD : (h + 1) * HD] = mm_tn(p, part(h, span, 2)).astype(BF)
    second = first + mm(o2_ref[...], wide((r0, r1, r2, r3))) + wr_bias[...].astype(F32)
    second_ref[...] = second
    normed, _ = standardize(second)
    n3_ref[...] = (normed * gains[2:3] + shifts[2:3]).astype(BF)


def whole(shape, dtype=BF):
    return shaped(shape, dtype), full(shaped(shape, dtype))


def row_forward(t, split, mixed, cells, packs, wo_bias, wr_bias, gains, shifts, columns):
    feature_count, rows, width = cells.shape
    n = columns * rows
    side = 4 * rows
    ins = [(split, pl.BlockSpec(memory_space=pltpu.SMEM))] + [(m, full(m)) for m in mixed]
    ins += [(cells, column_block(cells, columns))]
    ins += pack_parts(packs, "feat_out") + pack_parts(packs, "row_out") + pack_parts(packs, "qkv")
    ins += [(a, full(a)) for a in (wo_bias, wr_bias, gains, shifts)]
    return call(
        partial(row_forward_kernel, feature_count=feature_count), "row_forward", (1,), t, ins,
        [whole((n, width), F32), whole((n, width)), whole((n, 12 * HD)), whole((4, n // side, side, side)),
         whole((n, 4 * HD)), whole((n, width), F32), whole((n, width))], us=9
    )


def hidden_pair(t_ref, n3_ref, grad_ref, ups, packs, downs, grads, bias_grads, feature_count):
    columns, rows, width = grad_ref.shape
    g3 = live_columns(grad_ref[...], t_ref[0] * columns, feature_count).reshape(columns * rows, width)
    n3, gl = n3_ref[...], g3.astype(BF)
    n3_t, gl_t = n3.T, gl.T
    hidden = ups[0].shape[1]
    up = jnp.concatenate([u[...] for u in ups], axis=-1)
    down = jnp.concatenate([d[...] for d in downs], axis=0)
    bias = jnp.concatenate([p[...].astype(F32)[j : j + 1] for p in packs for j in range(4)], axis=-1)
    ms, dzs = [], []
    step = 256
    count = 2 * hidden // step
    ahead = []

    def begin(c):
        span = slice(c * step, (c + 1) * step)
        return mm(n3, up[:, span]) + bias[:, span], mm_nt(gl, down[span])

    ahead = begin(0)
    for c in range(count):
        z, dm = ahead
        if c + 1 < count:
            ahead = begin(c + 1)
        act, slope = gelu_parts(z)
        m = act.astype(BF)
        dz = (dm * slope).astype(BF)
        j, at = divmod(c * step, hidden)
        span = slice(at, at + step)
        grads[j][:width, span] = mm(n3_t, dz).astype(BF)
        grads[j][width:, span] = mm(gl_t, m).astype(BF)
        bias_grads[j][:, span] = column_sum(dz.astype(F32))
        ms.append(m)
        dzs.append(dz)
    out = mm(jnp.concatenate(ms, axis=-1), down)
    dn3 = mm_nt(jnp.concatenate(dzs, axis=-1), up)
    return g3, out, dn3


def hidden_first_kernel(
    t_ref, d_ref, n3_ref, grad_ref, up0, up1, b0, b1, down0, down1, out_ref, dn3_ref, wg0, wg1, bg0, bg1,
    *, feature_count,
):
    _, out, dn3 = hidden_pair(
        t_ref, n3_ref, grad_ref, (up0, up1), (b0, b1), (down0, down1), (wg0, wg1), (bg0, bg1), feature_count)
    out_ref[...] = out
    dn3_ref[...] = dn3


def hidden_second_kernel(
    t_ref, d_ref, n3_ref, grad_ref, up0, up1, b0, b1, down0, down1, out_in, dn3_in, second_ref, down_bias, gains_ref,
    earlier_ref, out_ref, g2_ref, stats_ref, wg0, sent_ref, bg0, bg1, *, feature_count,
):
    tall = earlier_ref.shape[0]
    sent_ref[:tall] = earlier_ref[...]
    g3, out, dn3 = hidden_pair(
        t_ref, n3_ref, grad_ref, (up0, up1), (b0, b1), (down0, down1), (wg0, sent_ref.at[pl.ds(tall, tall)]), (bg0, bg1),
        feature_count)
    second = second_ref[...]
    out_ref[...] = (second + out_in[...] + out + down_bias[...].astype(F32)).astype(BF)
    dn3 = dn3_in[...] + dn3
    normed, inverse = standardize(second)
    g2 = g3 + norm_backward(dn3, normed, inverse, gains_ref[...].astype(F32)[2:3])
    g2_ref[...] = g2
    stats_ref[...] = rows_of([g3, g2, dn3 * normed, dn3])


def rows_of(arrays):
    return jnp.concatenate(
        [column_sum(a) for a in arrays] + [jnp.zeros((8 - len(arrays), arrays[0].shape[1]), F32)], axis=0)


def hidden_call(t, n3, grads, both, packs, columns, extra=None):
    n, width = n3.shape
    hidden = both[0].shape[1]
    ins = [(n3, full(n3)), (grads, column_block(grads, columns))]
    ins += [(a, pl.BlockSpec((width, hidden), lambda *_: (0, 0))) for a in both] + pack_parts(packs, "bias")
    ins += [(a, pl.BlockSpec((hidden, width), lambda *_: (1, 0))) for a in both]
    bias_grads = [whole((1, hidden), F32)] * 2
    if extra is None:
        kernel, name = hidden_first_kernel, "hidden_first"
        results = [whole((n, width), F32)] * 2 + [whole((2 * width, hidden))] * 2 + bias_grads
    else:
        kernel, name = hidden_second_kernel, "hidden_second"
        ins += [(a, full(a)) for a in extra]
        results = [whole((n, width)), whole((n, width), F32), whole((8, width), F32)]
        results += [whole((2 * width, hidden)), whole((4 * width, hidden))] + bias_grads
    return call(partial(kernel, feature_count=grads.shape[0]), name, (1,), t, ins, results, us=7)


def attentions_backward(blocks):
    dps = [mm_nt(v, do) for _, _, v, _, do in blocks]
    pfs = [b[3].astype(F32) for b in blocks]
    dss = [(pf * (dp - jnp.sum(dp * pf, axis=0, keepdims=True))).astype(BF) for dp, pf in zip(dps, pfs)]
    dvs = [mm(p, do) for _, _, _, p, do in blocks]
    dks = [mm(ds, b[0]) * SCALE for ds, b in zip(dss, blocks)]
    dqs = [mm_tn(ds, b[1]) * SCALE for ds, b in zip(dss, blocks)]
    return list(zip(dqs, dks, dvs))


def row_backward_kernel(
    t_ref, d_ref, g2_ref, first_ref, qkv_ref, p_ref, gains_ref, n2_ref, o2_ref, m0, m1, m2, m3, fq0, fq2,
    w0, w1, w2, w3, r0, r1, r2, r3, s0, near_ref, s2, s3, stats_ref, keep_ref, send_ref, g1_scr, dqkv_ref,
):
    width = fq0.shape[1]
    for j, weights in enumerate((fq0, fq2)):
        tall = 3 * width // 4
        for lane in range(4):
            for at, first, count in stretches(lane * tall, tall, width):
                near_ref[j * tall + at : j * tall + at + count, lane * HD : (lane + 1) * HD] = (
                    weights[first // width, first % width : first % width + count, :])
    g2 = g2_ref[...]
    cells, width = g2.shape
    side = p_ref.shape[2]
    gl2 = g2.astype(BF)
    do = mm_nt(gl2, wide((r0, r1, r2, r3))).astype(BF)
    spans = [slice(b, b + side) for b in range(0, cells, side)]
    for first in range(0, 4, 2):
        heads = range(first, first + 2)
        blocks = [
            [qkv_ref[span, (3 * h + c) * HD : (3 * h + c + 1) * HD] for c in range(3)]
            + [p_ref[h, j], do[span, HD * h : HD * (h + 1)]] for h in heads for j, span in enumerate(spans)]
        places = [(h, span) for h in heads for span in spans]
        for (h, span), parts in zip(places, attentions_backward(blocks)):
            for c, part in enumerate(parts):
                dqkv_ref[span, (3 * h + c) * HD : (3 * h + c + 1) * HD] = part.astype(BF)
    dn2 = mm_nt(dqkv_ref[...], jnp.concatenate([stacked(w) for w in (w0, w1, w2, w3)], axis=-1))
    normed, inverse = standardize(first_ref[...])
    g1 = g2 + norm_backward(dn2, normed, inverse, gains_ref[...].astype(F32)[1:2])
    columns, rows, _ = g1_scr.shape
    g1_scr[...] = g1.reshape(columns, rows, width)
    share = rows // 4
    for k, out in enumerate((s0, near_ref.at[pl.ds(6 * width // 4, columns * share)], s2, s3)):
        at = pl.multiple_of(lax.bitwise_xor(t_ref[0], k) * share, share)
        out[...] = g1_scr[:, pl.ds(at, share), :].reshape(columns * share, width).astype(BF)
    stats_ref[...] = rows_of([g1, dn2 * normed, dn2])
    mixed = [in_order(m, columns) for m in (m0, m1, m2, m3)]
    row_grads(n2_ref[...], dqkv_ref[...], gl2, o2_ref[...], g1.astype(BF), mixed, keep_ref, send_ref)


def stretches(first, count, size):
    at = 0
    while at < count:
        rows = min(count - at, size - (first + at) % size)
        yield at, first + at, rows
        at += rows


def row_grads(n2, dqkv, gl2, o2, gl1, mixed, keep_ref, send_ref):
    width = n2.shape[1]
    grad = mm(n2.T, dqkv).astype(BF)
    out_grad = mm(gl2.T, o2).astype(BF)
    feat_grad = mm(gl1.T, jnp.concatenate(mixed, axis=-1)).astype(BF)
    for h in range(4):
        out = (keep_ref, send_ref)[h % 2].at[h // 2]
        blocks = [grad[:, (3 * h + c) * HD : (3 * h + c + 1) * HD] for c in range(3)]
        blocks += [out_grad[:, HD * h : HD * (h + 1)], feat_grad[:, HD * h : HD * (h + 1)]]
        for at, first, count, lane in row_places(width):
            out[at : at + count, lane * HD : (lane + 1) * HD] = blocks[first // width][first % width : first % width + count]


def row_backward(t, g2, first, qkv, p, gains, n2, o2, mixed, fq, fq_far, packs, rows):
    n, width = g2.shape
    ins = [(a, full(a)) for a in (g2, first, qkv, p, gains, n2, o2, *mixed, fq, fq_far)]
    ins += pack_parts(packs, "qkv") + pack_parts(packs, "row_out")
    piece = whole((n // 4, width))
    return call(
        row_backward_kernel, "row_backward", (1,), t, ins,
        [piece, whole((6 * width // 4 + n // 4, width)), piece, piece, whole((8, width), F32)]
        + [whole((2, 5 * width // 4, 4 * HD))] * 2,
        [pltpu.VMEM((n // rows, rows, width), F32), pltpu.VMEM(qkv.shape, BF)], us=11,
    )


def row_places(width):
    tall = 5 * width // 4
    first = 0
    while first < 5 * width:
        count = min(width - first % width, tall - first % tall)
        yield first % tall, first, count, first // tall
        first += count


def own_rows(t_ref, cells_ref, cell_scr, share):
    feature_count, block_rows, width = cells_ref.shape
    cell_scr[0:feature_count] = cells_ref[...].astype(F32)
    cell_scr[feature_count:] = jnp.zeros_like(cell_scr[feature_count:])
    at = pl.multiple_of(lax.rem(t_ref[0], block_rows // share) * share, share)
    return cell_scr[:, pl.ds(at, share), :].reshape(cell_scr.shape[0] * share, width)


def row_block(cells, share):
    feature_count, _, width = cells.shape
    per = RB // share
    return pl.BlockSpec((feature_count, RB, width), lambda i, t, d: (0, lax.div(t[0], per), 0))


def feature_again_kernel(
    t_ref, d_ref, cells_ref, gains_ref, shifts_ref, w0, w1, w2, w3, n1_ref, qkv_ref, p_ref, cell_scr, qkv_scr
):
    feature_count = cells_ref.shape[0]
    share, padded, _ = qkv_ref.shape
    normed, _ = standardize(own_rows(t_ref, cells_ref, cell_scr, share))
    low = (normed * gains_ref[...].astype(F32)[0:1] + shifts_ref[...].astype(F32)[0:1]).astype(BF)
    n1_ref[...] = low
    packed = mm(low, jnp.concatenate([three(w0), unpacked(w1), three(w2), unpacked(w3)], axis=-1))
    for c in range(12):
        qkv_scr[c] = packed[:, c * HD : (c + 1) * HD]
    for h in range(4):
        parts = [[qkv_scr[3 * h + c, pl.ds(r, padded, stride=share), :].astype(BF) for c in range(3)] for r in range(share)]
        scores = [mm_nt(k, q) * SCALE for q, k, _ in parts]
        for r in range(share):
            for c, part in enumerate(parts[r]):
                qkv_ref[r, :, (3 * h + c) * HD : (3 * h + c + 1) * HD] = part
            p_ref[r, h] = masked_softmax(scores[r], feature_count)


def feature_again(t, cells, gains, shifts, fq, fq_far, near, columns, share):
    width = cells.shape[2]
    padded = 4 * columns
    return call(
        feature_again_kernel, "feature_again", (1,), t,
        [(cells, row_block(cells, share))] + [(a, full(a)) for a in (gains, shifts)] + four_weights(fq, fq_far, near),
        [whole((padded * share, width)), whole((share, padded, 12 * HD)), whole((share, 4, padded, padded))],
        [pltpu.VMEM((padded, RB, width), F32), pltpu.VMEM((12, padded * share, HD), F32)], vmem=KNOBS["vs"], us=4
    )


def feature_backward_kernel(
    t_ref, d_ref, r0, r1, r2, r3, f0, f1, f2, f3, qkv_ref, p_ref, n1_ref,
    g1_ref, dqkv_ref, keep0, keep1, send0, send1, low_scr, do_scr, dqkv_scr,
):
    width = g1_ref.shape[1]
    share, padded, _ = qkv_ref.shape
    for k, piece in enumerate((r0, r1, r2, r3)):
        count = piece.shape[0]
        at = pl.multiple_of(lax.bitwise_xor(t_ref[0], k) * count, count)
        low_scr[pl.ds(at, count), :] = piece[...]
        g1_ref[pl.ds(at, count), :] = piece[...].astype(F32)
    do = mm_nt(low_scr[...], wide((f0, f1, f2, f3)))
    for h in range(4):
        do_scr[h] = do[:, h * HD : (h + 1) * HD]
    n1_t = n1_ref[...].T
    for h in range(4):
        rows = [pl.ds(r, padded, stride=share) for r in range(share)]
        heads = range(h, h + HEADS) if h % HEADS == 0 else ()
        blocks = [
            [qkv_ref[r, :, (3 * g + c) * HD : (3 * g + c + 1) * HD] for c in range(3)]
            + [p_ref[r, g], do_scr[g, every, :].astype(BF)] for g in heads for r, every in enumerate(rows)]
        places = [(g, every) for g in heads for every in rows]
        for (g, every), parts in zip(places, attentions_backward(blocks)):
            for c, part in enumerate(parts):
                dqkv_scr[3 * g + c, every, :] = part
        out = ((keep0, keep1), (send0, send1))[h % 2]
        for c in range(3):
            dqkv_ref[:, (3 * h + c) * HD : (3 * h + c + 1) * HD] = dqkv_scr[3 * h + c].astype(BF)
        grad = mm(n1_t, dqkv_ref[:, 3 * HD * h : 3 * HD * (h + 1)]).astype(BF)
        for c in range(3):
            out[h // 2][c * width : (c + 1) * width, :] = grad[:, c * HD : (c + 1) * HD]


def feature_backward(t, pieces, packs, qkv, p, n1):
    share, _, padded, _ = p.shape
    width = pieces[0].shape[1]
    cells = share * padded
    return call(
        feature_backward_kernel, "feature_backward", (1,), t,
        [(a, pl.BlockSpec(pieces[0].shape, partial(lambda j, *_: (j, 0), 0 if k != 1 else a.shape[0] // pieces[0].shape[0] - 1)))
         for k, a in enumerate(pieces)] + pack_parts(packs, "feat_out") + [(a, full(a)) for a in (qkv, p, n1)],
        [whole((cells, width), F32), whole((cells, 12 * HD))] + [whole((3 * width, HD))] * 4,
        [pltpu.VMEM((cells, width), BF), pltpu.VMEM((4, cells, HD), F32), pltpu.VMEM((12, cells, HD), F32)], us=11
    )


def feature_input_kernel(
    t_ref, d_ref, cells_ref, g1_ref, dqkv_ref, gains_ref, w0, w1, w2, w3, stats_a, stats_b, b0, b1, b2, b3,
    out_ref, stats_ref, cell_scr, sums_scr,
):
    cells, width = g1_ref.shape
    share = cells // cell_scr.shape[0]
    normed, inverse = standardize(own_rows(t_ref, cells_ref, cell_scr, share))
    dn1 = mm_nt(dqkv_ref[...], jnp.concatenate([three(w0), unpacked(w1), three(w2), unpacked(w3)], axis=-1))
    g0 = g1_ref[...] + norm_backward(dn1, normed, inverse, gains_ref[...].astype(F32)[0:1])
    out_ref[...] = g0[: out_ref.shape[0]].astype(BF)
    sums_scr[0:8] = stats_a[...]
    sums_scr[8:16] = stats_b[...]
    sums_scr[4:5] = column_sum(dn1 * normed)
    sums_scr[5:6] = column_sum(dn1)
    sums_scr[16:32] = jnp.zeros((16, width), F32)
    for k, row in enumerate((b0, b1, b2, b3)):
        sums_scr[pl.ds(16 + lax.bitwise_xor(t_ref[0], k), 1), :] = row[...]
    for j in range(4):
        stats_ref[32 * j : 32 * (j + 1)] = sums_scr[:, j * HD : (j + 1) * HD]


def feature_input(t, cells, g1, dqkv, gains, fq, fq_far, near, sums, share):
    count, width = g1.shape
    kept = (cells.shape[0] + 1) // 2 * 2 * share
    ins = [(cells, row_block(cells, share))] + [(a, full(a)) for a in (g1, dqkv, gains)]
    ins += four_weights(fq, fq_far, near) + [(a, full(a)) for a in sums]
    return call(
        feature_input_kernel, "feature_input", (1,), t, ins, [whole((kept, width)), whole((128, HD), F32)],
        [pltpu.VMEM((count // share, RB, width), F32), pltpu.VMEM((32, width), F32)], vmem=KNOBS["vs"], us=2,
    )


def pair_kernel(t_ref, d_ref, own, far, out_ref):
    out_ref[: own.shape[0]] = own[...]
    out_ref[own.shape[0] :] = far[...]


def pair(t, own, far):
    return call(pair_kernel, "pair", (), t, [(own, VMEM), (far, VMEM)], [(shaped((2 * own.shape[0], own.shape[1])), VMEM)], vmem=12)[0]


def columns_home_kernel(t_ref, d_ref, p0, p1, p2, p3, out_ref):
    for k, piece in enumerate((p0, p1, p2, p3)):

        @pl.when(pl.program_id(0) == lax.bitwise_xor(t_ref[0], k))
        def _():
            out_ref[...] = piece[...].reshape(out_ref.shape)


def columns_home(t, own, far, near, feature_count, rows):
    count, width = own.shape
    columns = count // rows
    block = lambda i: pl.BlockSpec((count, width), lambda *_: (i, 0))
    return call(
        columns_home_kernel, "columns_home", (4,), t,
        [(own, block(0)), (near, block(0)), (far, block(0)), (near, block(1))],
        [(shaped((feature_count, rows, width)), pl.BlockSpec((columns, rows, width), lambda i, t, d: (i, 0, 0)))], vmem=KNOBS["vh"],
    )[0]


def rows_home_kernel(t_ref, d_ref, p0, p1, p2, p3, out_ref, scr):
    columns, rows, width = scr.shape
    share = rows // 4
    for k, piece in enumerate((p0, p1, p2, p3)):
        at = pl.multiple_of(lax.bitwise_xor(t_ref[0], k) * share, share)
        scr[:, pl.ds(at, share), :] = piece[...].astype(F32).reshape(columns, share, width)
    out_ref[...] = scr[...].astype(BF)


def rows_home(t, own, far, near, feature_count, rows):
    count, width = own.shape
    share = rows // 4
    steps = 5
    columns = count // share // steps
    block = lambda first: pl.BlockSpec((columns * share, width), lambda i, t, d: (first + i, 0))
    return call(
        rows_home_kernel, "rows_home", (steps,), t,
        [(own, block(0)), (near, block(0)), (far, block(0)), (near, block(steps))],
        [(shaped((feature_count, rows, width)), pl.BlockSpec((columns, rows, width), lambda i, t, d: (i, 0, 0)))],
        [pltpu.VMEM((columns, rows, width), F32)], vmem=KNOBS["vh"],
    )[0]


def swap(values, axis, mask):
    count = lax.axis_size(axis)
    return lax.ppermute(values, axis, [(i, i ^ mask) for i in range(count)])


def gather_groups(own):
    far = swap(own, "tensor", 2)
    return own, swap(own, "tensor", 1), far, swap(far, "tensor", 1)


class Box:
    def __init__(self, value):
        self.value = value


def tied(values, *boxes):
    many = isinstance(values, tuple)
    values = values if many else (values,)
    out = lax.optimization_barrier((*values, *[b.value for b in boxes]))
    for box, value in zip(boxes, out[len(values) :]):
        box.value = value
    return out[: len(values)] if many else out[0]


def dp_masks():
    masks, mask = [], 1
    while mask < lax.axis_size("dp"):
        masks.append(mask)
        mask *= 2
    return masks


def digit(d_ref, mask):
    return lax.rem(lax.div(d_ref[0], mask), 2)


def halves(d_ref, mask, rows):
    side = digit(d_ref, mask)
    return [pl.multiple_of(s * rows, rows) for s in (side, 1 - side)]


def added(a, b):
    return a.astype(F32) + b.astype(F32)


def merge(name, kernel, t, ins, outs, scratch=(), vmem=16):
    return call(kernel, name, (), t, [(a, VMEM) for a in ins], [(shaped(o), VMEM) for o in outs], scratch, vmem=vmem)


def first_halves(t, hg0, hg2, row_keep, got, row_got, masks):
    hidden, width = hg0.shape[0] // 2, hg0.shape[1]
    tall, low = hidden // 2, row_keep.shape[1] // 4

    def kernel(t_ref, d_ref, g0, g2, keep, r, row_r, ak, as_, bk, bs):
        for which, (kept, sent, mask) in enumerate(((ak, as_, masks[0]), (bk, bs, masks[1]))):
            for out, first in zip((kept, sent), halves(d_ref, mask, tall)):
                for group, mine in enumerate((g0, g2)):
                    here = pl.multiple_of(which * hidden + first, tall)
                    there = pl.multiple_of((2 * group + which) * hidden + first, tall)
                    out[group, :tall] = added(mine[pl.ds(here, tall), :], r[pl.ds(there, tall), :]).astype(BF)
            for out, first in zip((kept, sent), halves(d_ref, mask, low)):
                span = (slice(None), pl.ds(pl.multiple_of(2 * which * low + first, low), low), slice(None))
                out[:, tall:] = added(keep[span], row_r[span]).astype(BF)

    return merge("ab_first", kernel, t, (hg0, hg2, row_keep, got, row_got), [(2, tall + low, width)] * 4, vmem=20)


def second_halves(t, a, ar, b, br, masks, tall):
    _, rows, width = a.shape

    def kernel(t_ref, d_ref, a, ar, b, br, ak, as_, bk, bs):
        for x, y, kept, sent, mask in ((a, ar, ak, as_, masks[1]), (b, br, bk, bs, masks[0])):
            for base, half in ((0, tall // 2), (tall, (rows - tall) // 2)):
                for out, first in zip((kept, sent), halves(d_ref, mask, half)):
                    span = (slice(None), pl.ds(pl.multiple_of(base + first, 16), half), slice(None))
                    out[:, base // 2 : base // 2 + half] = added(x[span], y[span]).astype(BF)

    return merge("ab_second", kernel, t, (a, ar, b, br), [(2, rows // 2, width)] * 4)


def groups_apart(t, a, ar, b, br):
    _, rows, width = a.shape

    def kernel(t_ref, d_ref, a, ar, b, br, kept, sent):
        for group, out in enumerate((kept, sent)):
            out[:rows] = added(a[group], ar[group]).astype(BF)
            out[rows:] = added(b[group], br[group]).astype(BF)

    return merge("ab_groups", kernel, t, (a, ar, b, br), [(2 * rows, width)] * 2)


def sums(t, k, r):
    def kernel(t_ref, d_ref, k, r, out):
        out[...] = added(k[...], r[...]).astype(BF)

    return merge("sums", kernel, t, (k, r), [k.shape])


def sums_apart(t, k, r):
    rows, width = k.shape[0] // 2, k.shape[1]

    def kernel(t_ref, d_ref, k, r, a, b):
        a[...] = added(k[:rows], r[:rows]).astype(BF)
        b[...] = added(k[rows:], r[rows:]).astype(BF)

    return merge("ab_apart", kernel, t, (k, r), [(rows, width)] * 2)


def joins(t, pairs, masks, first_part=None):
    def kernel(t_ref, d_ref, *refs):
        for j, mask in enumerate(masks):
            own, other, out = refs[2 * j], refs[2 * j + 1], refs[2 * len(masks) + j]
            rows = own.shape[0]
            for base, count in [(0, rows)] if first_part is None else [(0, first_part), (first_part, rows - first_part)]:
                for source, first in zip((own, other), halves(d_ref, mask, count)):
                    out[pl.ds(pl.multiple_of(2 * base + first, 16), count), :] = source[base : base + count]

    return merge("joins", kernel, t, [a for p in pairs for a in p], [(2 * p[0].shape[0], p[0].shape[1]) for p in pairs])


def feature_groups(t, own, got, mine, theirs):
    rows, width = own[0].shape
    more = mine.shape[0]

    def kernel(t_ref, d_ref, a0, a2, b0, b2, sa, sb, kept, sent):
        small = added(sa[...], sb[...]).astype(BF)
        for out, a, b in ((kept, a0, b0), (sent, a2, b2)):
            out[:rows] = added(a[...], b[...]).astype(BF)
            out[rows:] = small

    return merge("f_groups", kernel, t, (*own, *got, mine, theirs), [(rows + more, width)] * 2)


def half_sums(t, k, r, mask):
    rows, width = k.shape[0] // 2, k.shape[1]

    def kernel(t_ref, d_ref, k, r, kept, sent):
        for out, first in zip((kept, sent), halves(d_ref, mask, rows)):
            span = (pl.ds(first, rows), slice(None))
            out[...] = added(k[span], r[span]).astype(BF)

    return merge("f_half", kernel, t, (k, r), [(rows, width)] * 2)


def joined(d_ref, own, other, mask, scr):
    rows = own.shape[0]
    side = digit(d_ref, mask)
    for source, place in ((own, side), (other, 1 - side)):
        scr[pl.ds(pl.multiple_of(place * rows, rows), rows), :] = source[...].astype(F32)


def finish_kernel(t_ref, d_ref, a0, a1, b0, b1, up_ref, down_ref, qkv_ref, row_out_ref, feat_out_ref, scr_a, scr_b, tall, *, masks):
    width = up_ref.shape[0]
    for own, other, mask, scr in ((a0, a1, masks[0], scr_a), (b0, b1, masks[1], scr_b)):
        for base, count in ((0, width // 2), (width // 2, own.shape[0] - width // 2)):
            for source, first in zip((own, other), halves(d_ref, mask, count)):
                scr[pl.ds(pl.multiple_of(2 * base + first, 16), count), :] = source[base : base + count].astype(F32)
    half = scr_a.shape[0] - width
    up_ref[...] = scr_a[0:width]
    down_ref[...] = scr_b[0:width].T
    for at, first, count, lane in row_places(width):
        for scr, low, high in ((scr_a, 0, half), (scr_b, half, 2 * half)):
            begin, end = max(at, low), min(at + count, high)
            if begin < end:
                to = first + begin - at
                tall[to : to + end - begin, :] = scr[width + begin - low : width + end - low, lane * HD : (lane + 1) * HD]
    qkv_ref[...] = tall[0 : 3 * width]
    row_out_ref[...] = tall[3 * width : 4 * width].T
    feat_out_ref[...] = tall[4 * width : 5 * width].T


def finish(t, a, b, masks, width):
    rows, w = a[0].shape
    scr = pltpu.VMEM((2 * rows, w), F32)
    outs = [shaped(s, F32) for s in ((width, w), (w, width), (3 * width, HD), (HD, width), (HD, width))]
    return call(
        partial(finish_kernel, masks=masks), "finish", (), t,
        [(x, VMEM) for x in (*a, *b)], [(o, VMEM) for o in outs],
        [scr, scr, pltpu.VMEM((5 * width, HD), F32)], vmem=KNOBS["vz"])


def finish_feature_kernel(
    t_ref, d_ref, own, other, qkv_ref, feat_bias, row_bias, up_bias, down_bias, gains, shifts, scr, sums, *, mask
):
    joined(d_ref, own, other, mask, scr)
    rows = qkv_ref.shape[0]
    qkv_ref[...] = scr[0:rows]
    tall = sums.shape[0]
    for j in range(4):
        sums[:, j * HD : (j + 1) * HD] = scr[rows + j * tall : rows + (j + 1) * tall]
    down_bias[...] = sums[0:1]
    row_bias[...] = sums[1:2]
    feat_bias[...] = sums[8:9]
    up_bias[...] = sums[pl.ds(16 + t_ref[0], 1), :]
    for out, places in ((gains, (4, 9, 2)), (shifts, (5, 10, 3))):
        for i, place in enumerate(places):
            out[i : i + 1] = sums[place : place + 1]


def finish_feature(t, own, other, mask, width, small):
    rows, w = own.shape
    return call(
        partial(finish_feature_kernel, mask=mask), "finish_feature", (), t, [(own, VMEM), (other, VMEM)],
        [(shaped((3 * width, w), F32), VMEM)] + [(shaped((n, width), F32), VMEM) for n in (1, 1, 1, 1, 3, 3)],
        [pltpu.VMEM((2 * rows, w), F32), pltpu.VMEM((small, width), F32)], vmem=16)


def shards(
    table_cells, splits, feat_qkv, feat_out, feat_out_bias, row_qkv, row_out, row_out_bias,
    up_weight, up_bias, down_weight, down_bias, norm_gains, norm_biases, cotangent,
):
    shape = table_cells.shape
    _, row_count, feature_count, width = shape
    share = row_count // 4
    columns = -(-feature_count // (4 * FB)) * FB
    t = tuple(lax.axis_index(a).astype(jnp.int32).reshape(1) for a in ("tensor", "dp"))
    masks = dp_masks()
    cells = jnp.transpose(table_cells[0], (1, 0, 2))
    grads = jnp.transpose(cotangent[0], (1, 0, 2))
    fob, rob, dnb = (b.reshape(1, width) for b in (feat_out_bias, row_out_bias, down_bias))
    fq = jnp.transpose(feat_qkv, (1, 0, 2))
    rq = jnp.transpose(row_qkv, (1, 0, 2))

    near, far = masks[:2], masks[2:]
    over = lambda v, mask: swap(v, "tensor", 2) if mask == "x" else swap(v, "dp", mask)
    core = lambda v: swap(v, "tensor", 1)

    own = pack(t, rq, feat_out, row_out, up_bias)
    own_far = swap(own, "tensor", 2)
    *mixed, both = feature_forward(t, cells, norm_gains, norm_biases, fq, up_weight, down_weight, columns)
    kept = Box(mixed[0])
    own_far = tied(own_far, kept)
    packs = own, core(own), own_far, core(own_far)
    mixed = [kept.value] + [swap(mixed[k], "tensor", k) for k in (1, 2, 3)]
    a1, a2, a3 = Box(mixed[1]), Box(mixed[2]), Box(mixed[3])
    both_far = swap({"c": lambda: tied(both, a1, a2, a3), "a": lambda: tied(both, a2, a3), "2": lambda: tied(both, a2), "": lambda: both}[KNOBS["ud_tie"]](), "tensor", 2)
    mixed[1:] = a1.value, a2.value, a3.value

    first, n2, row_packed, row_p, o2, second, n3 = row_forward(
        t, splits, mixed, cells, packs, fob, rob, norm_gains, norm_biases, columns)
    out_a, dn3_a, hg0, hg1, bg0, bg1 = hidden_call(t, n3, grads, (both, core(both)), packs[:2], columns)
    kept, fq_kept = Box(out_a), Box(hg0)
    both_far = tied(both_far, kept)
    fq_far = swap(tied(fq, fq_kept), "tensor", 2)
    hg0 = fq_kept.value
    out_f, g2, stats_a, hg2, hidden_send, bg2, bg3 = hidden_call(
        t, n3, grads, (both_far, core(both_far)), packs[2:], columns,
        [kept.value, dn3_a, second, dnb, norm_gains, hg1])
    fq_box = Box(fq_far)
    if KNOBS["hs_tie"] == "fq":
        hidden_got = core(tied(hidden_send, fq_box))
    fq_far = fq_box.value
    s0, near_send, s2, s3, stats_b, row_keep, row_send = row_backward(
        (*t, out_f), g2, first, row_packed, row_p, norm_gains, n2, o2, mixed, fq, fq_far, packs, row_count)
    pieces = [s0, core(near_send), swap(s2, "tensor", 2), swap(s3, "tensor", 3)]
    near_got = pieces[1]
    K = KNOBS
    boxes = {"s0": Box(s0), "rs": Box(row_send), "near": Box(near_got)}
    if K["hs_tie"] != "fq":
        hidden_got = core(tied(hidden_send, boxes[K["hs_tie"]]) if K["hs_tie"] else hidden_send)
    row_got = core(tied(row_send, boxes[K["rs_tie"]]) if K["rs_tie"] else boxes["rs"].value)
    pieces[0] = boxes["s0"].value
    pieces[1] = near_got = boxes["near"].value

    last = [s0]
    boxes.update(out=Box(out_f), w=Box(pieces[3]), w2=Box(pieces[2]))
    out_far = None
    if K["out_tie"] == "s0":
        out_far = swap(tied(out_f, boxes["s0"]), "tensor", 2)
        pieces[0] = boxes["s0"].value
    if K["out_tie"] == "hs":
        out_far = swap(out_f, "tensor", 2)
    for what in K["window"]:
        if what == "A":
            n1, feat_packed, feat_p = feature_again(
                (*t, *last), cells, norm_gains, norm_biases, fq, fq_far, near_got, columns, share)
            last = [feat_p]
        elif what == "M":
            ak, a_sent, bk, b_sent = first_halves((*t, *last), hg0, hg2, row_keep, hidden_got, row_got, near)
            last = [ak]
            ar, br = over(a_sent, near[0]), over(b_sent, near[1])
        else:
            last = [*last, pieces[2], pieces[3]]
    if K["out_tie"] in ("w", "Aw"):
        after = [Box(feat_p)] if K["out_tie"] == "Aw" else []
        out_far = swap(tied(out_f, boxes["w"], boxes["w2"], *after), "tensor", 2)
        if after:
            feat_p = after[0].value
            last = [feat_p]
        pieces[2:] = boxes["w2"].value, boxes["w"].value

    g1, dqkv_f, f0, f2, f1, f3 = feature_backward((*t, *last), pieces, packs, feat_packed, feat_p, n1)
    g0, small = feature_input(
        t, cells, g1, dqkv_f, norm_gains, fq, fq_far, near_got, (stats_a, stats_b, bg0, bg1, bg2, bg3), share)
    f_got = core(f1), core(f3)
    small_got = core(small)
    last = [small]

    state = {"O": 0, "F": 0}
    grads_other = feat_grad = None

    def step_other(last):
        nonlocal ak, ar, bk, br, ab, abr, grads_other
        here = state["O"]
        tt = (*t, *last)
        if here == 0:
            ak, a_sent, bk, b_sent = out = second_halves(tt, ak, ar, bk, br, near, width // 2)
            ar, br = over(a_sent, near[1]), over(b_sent, near[0])
        elif here == 1:
            ab, sent = out = groups_apart(tt, ak, ar, bk, br)
            abr = over(sent, "x")
        elif here < 2 + len(far):
            ab, = out = sums(tt, ab, abr)
            abr = over(ab, far[here - 2])
        elif here == 2 + len(far):
            ak, bk = out = sums_apart(tt, ab, abr)
            ar, br = over(ak, near[1]), over(bk, near[0])
        elif here == 3 + len(far):
            ak, bk = out = joins(tt, ((ak, ar), (bk, br)), (near[1], near[0]), width // 4)
            ar, br = over(ak, near[0]), over(bk, near[1])
        else:
            grads_other = out = finish(tt, (ak, ar), (bk, br), near, width)
        state["O"] += 1
        return out[:1]

    def step_feature(last):
        nonlocal fk, fr, feat_grad, small_sums
        here = state["F"]
        tt = (*t, *last)
        if here == 0:
            fk, sent = out = feature_groups(tt, (f0, f2), f_got, small, small_got)
            fr = over(sent, "x")
        elif here < 3:
            fk, sent = out = half_sums(tt, fk, fr, near[here - 1])
            fr = over(sent, near[here - 1])
        elif here < 3 + len(far):
            fk, = out = sums(tt, fk, fr)
            fr = over(fk, far[here - 3])
        elif here == 3 + len(far):
            fk, = out = sums(tt, fk, fr)
            fr = over(fk, near[1])
        elif here == 4 + len(far):
            fk, = out = joins(tt, ((fk, fr),), (near[1],))
            fr = over(fk, near[0])
        else:
            feat_grad, *small_sums = out = finish_feature(tt, fk, fr, near[0], width, small.shape[0] // 4)
        state["F"] += 1
        return out[:1]

    ab = abr = fk = fr = small_sums = g0_far = None
    steps = list(K["tail"])
    while steps or grads_other is None or feat_grad is None:
        what = steps.pop(0) if steps else ("O" if grads_other is None else "F")
        if what == "O" and grads_other is None:
            last = step_other(last)
        elif what == "F" and feat_grad is None:
            last = step_feature(last)
        elif what == "p":
            out_pair = pair((*t, *last), out_f, out_far)
            out_near = core(out_pair)
            last = [out_pair]
        elif what == "c":
            output = columns_home((*t, *last), out_f, out_far, out_near, feature_count, row_count)
            last = [output]
        elif what == "g":
            g0_pair = pair((*t, *last), g0, g0_far)
            g0_near = core(g0_pair)
            last = [g0_pair]
        elif what == "r":
            input_grad = rows_home((*t, *last), g0, g0_far, g0_near, feature_count, row_count)
            last = [input_grad]
        key = what + str(state.get(what, ""))
        if g0_far is None and key == K["g_tie"]:
            box = Box(last[0])
            g0_far = swap(tied(g0, box), "tensor", 2)
            last = [box.value]
    feat_bias, row_bias, up_bias_grad, down_bias_grad, gain_grad, shift_grad = small_sums

    def qkv_shape(grad):
        return jnp.transpose(grad.reshape(3, width, HD), (1, 0, 2))

    home = lambda a: jnp.transpose(a, (1, 0, 2)).reshape(shape)
    return (
        home(output),
        home(input_grad),
        qkv_shape(feat_grad),
        grads_other[4],
        feat_bias.reshape(width),
        qkv_shape(grads_other[2]),
        grads_other[3],
        row_bias.reshape(width),
        grads_other[0],
        up_bias_grad.reshape(up_bias.shape),
        grads_other[1],
        down_bias_grad.reshape(width),
        gain_grad,
        shift_grad,
    )


def solution(mesh):
    return jax.shard_map(
        shards,
        mesh=mesh,
        in_specs=(
            P("dp", None, None, None), P("dp"), P(None, None, "tensor"), P("tensor", None), P(),
            P(None, None, "tensor"), P("tensor", None), P(), P(None, "tensor"), P("tensor"),
            P("tensor", None), P(), P(), P(), P("dp", None, None, None),
        ),
        out_specs=(
            P("dp", None, None, None), P("dp", None, None, None), P(None, None, "tensor"),
            P("tensor", None), P(), P(None, None, "tensor"), P("tensor", None), P(),
            P(None, "tensor"), P("tensor"), P("tensor", None), P(), P(), P(),
        ),
        check_vma=False,
    )
```
